128 devices in a mesh: gx: 8 (over z, core), gy: 16 (over y, x).
Axes of the slice: x: 4, y: 4, z: 4, core: 2. Of those that a mesh axis runs over, the one named last changes fastest.
Arguments:
- depth: float32 [2048, 16384], P('gx', 'gy'), may hold values from 2 to 4
- momentum_x: float32 [2048, 16384], P('gx', 'gy'), may hold values from -3 to 3
- momentum_y: float32 [2048, 16384], P('gx', 'gy'), may hold values from -3 to 3
- bed: float32 [2048, 16384], P('gx', 'gy'), may hold values from 0 to 1
- open_cell: int32 [2048, 16384], P('gx', 'gy'), may hold values 0 or 1
- send_strip: int32 [128, 128, 16], P(('gx', 'gy')), may hold values from -1 to 2047, as said below
- inlet_slot: int32 [2048, 128], P(('gx', 'gy')), may hold values from -1 to 2047, as said below
- inlet_section: int32 [2048, 128], P(('gx', 'gy')), may hold values from 0 to 511
- inlet_coef: float32 [2048, 128], P(('gx', 'gy')), may hold values from 0.1 to 1
- sewer_head: float32 [2048, 512], P(('gx', 'gy')), may hold values from -4 to 4
- conveyance: float32 [2048, 512], P(('gx', 'gy')), may hold values from 0.1 to 1
Outputs:
- depth_out: float32 [2048, 16384], P('gx', 'gy')
- momentum_x_out: float32 [2048, 16384], P('gx', 'gy')
- momentum_y_out: float32 [2048, 16384], P('gx', 'gy')
- sewer_out: float32 [2048, 512], P(('gx', 'gy'))
The draws below stay inside these ranges and needn't reach their ends.
Inputs may be any that keep to these rules, and one draw needn't show every extreme that they name: Entry [s, d, k] is a strip of tile s, or -1 for an empty slot; used slots come first. No strip of a tile appears twice in send_strip[s]. Each tile sends at most 16 strips to one device, exactly 16 to some device in every column d, and one device receives 16 strips from every tile. `inlet_slot`: over the 16 lines of one device, each used slot s * 16 + k of what that device receives appears exactly once; every other entry is -1.
All inputs are finite; a program needn't handle non-finite values. No bound on the sum of `open_cell` on one device may be relied on, other than what follows from the above.
Results may differ from the reference program's by a relative error of at most 0.00012.
Values sent between devices are 32-bit elements; how exact they have to be, the bound alone decides.
A program may use at most 128 MiB of HBM per device.

```python
import math
import jax
import jax.numpy as jnp
from jax import lax

CX = 256
CY = 1024
L_DEV = 16
INLETS = 128
SECTIONS = 512
SUBSTEPS = 8
TILES = 128
CAP = 16
LINES = 2048
STRIPS_DEV = 2048
NX = 2048
NY = 16384


def route_counts(key):
    shortened = jax.random.randint(jax.random.fold_in(key, 11), (TILES, TILES), 0, 8) == 0
    extra = jax.random.randint(jax.random.fold_in(key, 16), (TILES, TILES), 0, max(1, CAP // 4))
    counts = jnp.maximum(1, CAP - jnp.where(shortened, 1 + extra, 0))
    columns = jnp.arange(TILES)
    full_source = jax.random.permutation(jax.random.fold_in(key, 12), TILES)
    counts = counts.at[full_source, columns].set(CAP)
    busiest = jax.random.randint(jax.random.fold_in(key, 13), (), 0, TILES)
    counts = jnp.where(columns[None, :] == busiest, CAP, counts)
    return counts.astype(jnp.int32)


def draw_send_strip(key, part):
    counts = route_counts(key)
    keys = jax.random.split(jax.random.fold_in(key, 14), TILES)
    orders = jax.vmap(lambda each: jax.random.permutation(each, STRIPS_DEV)[:TILES * CAP])(keys)
    strips = orders.reshape(TILES, TILES, CAP)
    position = jnp.arange(CAP)
    return jnp.where(position[None, None, :] < counts[:, :, None], strips, -1).astype(jnp.int32)


def draw_inlet_slot(key, part):
    counts = route_counts(key)
    keys = jax.random.split(jax.random.fold_in(key, 15), TILES)
    orders = jax.vmap(lambda each: jax.random.permutation(each, TILES * CAP))(keys)
    source_tile = orders // CAP
    position = orders % CAP
    limit = counts[source_tile, jnp.arange(TILES)[:, None]]
    slots = jnp.where(position < limit, orders, -1)
    return slots.reshape(LINES, INLETS).astype(jnp.int32)


def place_ends(values, key, least, top_value):
    dims = values.shape
    spot = [jax.random.randint(jax.random.fold_in(key, axis), (), 0, dims[axis]) for axis in range(len(dims))]
    values = values.at[tuple(spot)].set(least)
    longest = dims.index(max(dims))
    spot[longest] = (spot[longest] + 1) % dims[longest]
    return values.at[tuple(spot)].set(top_value)


def level_of(rng, extent, shards, low, top_value):
    factor_of, own = 1.0, jax.random.fold_in(rng, 6)
    for dim, shards_of in shards:
        draws = jnp.exp(jax.random.uniform(jax.random.fold_in(own, dim), (shards_of,), jnp.float32, low / len(shards), top_value / len(shards)))
        factor_of = factor_of * jnp.repeat(draws, extent[dim] // shards_of).reshape([-1 if axis == dim else 1 for axis in range(len(extent))])
    return factor_of


def normal_values(rng, dims, scale, reach, shards=(), kind=jnp.bfloat16):
    entries = jax.random.normal(rng, dims, jnp.float32) * scale
    if len(shards) > 0:
        entries = level_of(rng, dims, shards, -0.22, 0.18) * entries
    return jnp.clip(entries, min=-reach, max=reach).astype(kind)


def setup_inputs(seed: int = 0) -> dict:
    splits = jax.random.split(jax.random.key(seed), 12)
    depth = jnp.clip(2.0 + 2.0 * jax.random.uniform(splits[0], (NX, NY), jnp.float32) ** level_of(splits[0], (NX, NY), ((0, 8), (1, 16)), -0.2, 0.2), 2.0, 4.0)
    momentum_x = normal_values(splits[1], (NX, NY), 1.0, 3.0, ((0, 8), (1, 16)), jnp.float32)
    momentum_y = normal_values(splits[2], (NX, NY), 1.0, 3.0, ((0, 8), (1, 16)), jnp.float32)
    bed = jnp.clip(1.0 * jax.random.uniform(splits[3], (NX, NY), jnp.float32) ** level_of(splits[3], (NX, NY), ((0, 8), (1, 16)), -0.2, 0.2), 0.0, 1.0)
    open_cell = place_ends((jax.random.randint(splits[4], (NX, NY), 0, 8) < 7).astype(jnp.int32), jax.random.fold_in(splits[4], 1), 0, 1)
    send_strip = draw_send_strip(jax.random.fold_in(splits[11], 71), 0)
    inlet_slot = draw_inlet_slot(jax.random.fold_in(splits[11], 71), 0)
    inlet_section = place_ends(jax.random.randint(splits[7], (LINES, INLETS), 0, SECTIONS), jax.random.fold_in(splits[7], 1), 0, SECTIONS - 1).astype(jnp.int32)
    inlet_coef = jnp.clip(jnp.exp(math.log(1.0) - 2.3025851 * jax.random.uniform(splits[8], (LINES, INLETS), jnp.float32) ** level_of(splits[8], (LINES, INLETS), ((0, 128),), -0.2, 0.2)), 0.1, 1.0)
    sewer_head = normal_values(splits[9], (LINES, SECTIONS), 1.0, 4.0, ((0, 128),), jnp.float32)
    conveyance = jnp.clip(jnp.exp(math.log(1.0) - 2.3025851 * jax.random.uniform(splits[10], (LINES, SECTIONS), jnp.float32) ** level_of(splits[10], (LINES, SECTIONS), ((0, 128),), -0.2, 0.2)), 0.1, 1.0)
    return {"depth": depth, "momentum_x": momentum_x, "momentum_y": momentum_y, "bed": bed, "open_cell": open_cell, "send_strip": send_strip, "inlet_slot": inlet_slot, "inlet_section": inlet_section, "inlet_coef": inlet_coef, "sewer_head": sewer_head, "conveyance": conveyance}


gravity = 9.81
surface_dt = 0.02
sewer_dt = 0.5
section_area = 256.0

def surface_step(h, hu, hv, z, m, drain):
    hs = h + (1.0 - m)
    u = hu / hs
    v = hv / hs
    speed = jnp.sqrt(gravity * hs)
    press = 0.5 * gravity * h * h
    xl = (slice(None, -1), slice(1, -1))
    xr = (slice(1, None), slice(1, -1))
    yl = (slice(1, -1), slice(None, -1))
    yr = (slice(1, -1), slice(1, None))
    core = (slice(1, -1), slice(1, -1))
    ax = jnp.maximum(jnp.abs(u[xl]) + speed[xl], jnp.abs(u[xr]) + speed[xr])
    wall_x = m[xl] * m[xr]
    fh = wall_x * (0.5 * (hu[xl] + hu[xr]) - 0.5 * ax * (h[xr] - h[xl]))
    fu = wall_x * (0.5 * (hu[xl] * u[xl] + press[xl] + hu[xr] * u[xr] + press[xr]) - 0.5 * ax * (hu[xr] - hu[xl]))
    fv = wall_x * (0.5 * (hu[xl] * v[xl] + hu[xr] * v[xr]) - 0.5 * ax * (hv[xr] - hv[xl]))
    ay = jnp.maximum(jnp.abs(v[yl]) + speed[yl], jnp.abs(v[yr]) + speed[yr])
    wall_y = m[yl] * m[yr]
    gh = wall_y * (0.5 * (hv[yl] + hv[yr]) - 0.5 * ay * (h[yr] - h[yl]))
    gu = wall_y * (0.5 * (hv[yl] * u[yl] + hv[yr] * u[yr]) - 0.5 * ay * (hu[yr] - hu[yl]))
    gv = wall_y * (0.5 * (hv[yl] * v[yl] + press[yl] + hv[yr] * v[yr] + press[yr]) - 0.5 * ay * (hv[yr] - hv[yl]))
    h_core = h[core]
    m_core = m[core]
    slope_x = 0.5 * (z[2:, 1:-1] - z[:-2, 1:-1])
    slope_y = 0.5 * (z[1:-1, 2:] - z[1:-1, :-2])
    h_new = h_core - surface_dt * (m_core * (fh[1:] - fh[:-1] + gh[:, 1:] - gh[:, :-1]) + drain)
    hu_new = hu[core] - surface_dt * m_core * (fu[1:] - fu[:-1] + gu[:, 1:] - gu[:, :-1] + gravity * h_core * slope_x)
    hv_new = hv[core] - surface_dt * m_core * (fv[1:] - fv[:-1] + gv[:, 1:] - gv[:, :-1] + gravity * h_core * slope_y)
    return (h_new, hu_new, hv_new)

def sewer_steps(head, conveyance, inflow):
    face_k = 0.5 * (conveyance[:, :-1] + conveyance[:, 1:])
    first = jnp.zeros((head.shape[0], 1), jnp.float32)
    for turn in range(SUBSTEPS):
        inner = face_k * (head[:, :-1] - head[:, 1:])
        outlet = conveyance[:, -1:] * head[:, -1:]
        leaving = jnp.concatenate([inner, outlet], axis=1)
        entering = jnp.concatenate([first, inner], axis=1)
        head = head + sewer_dt * (entering - leaving + inflow / section_area)
    return head

def reference(depth, momentum_x, momentum_y, bed, open_cell, send_strip, inlet_slot, inlet_section, inlet_coef, sewer_head, conveyance):
    n_gx = NX // CX
    n_gy = NY // CY
    level = depth + bed
    strips_all = level.reshape(n_gx, CX, n_gy, CY).transpose(0, 2, 1, 3).reshape(TILES, STRIPS_DEV, 128)
    owner = (jnp.arange(LINES) // L_DEV).astype(jnp.int32)
    valid = inlet_slot >= 0
    slot = jnp.maximum(inlet_slot, 0)
    source_tile = (slot // CAP).astype(jnp.int32)
    position = (slot % CAP).astype(jnp.int32)
    strip = jnp.maximum(send_strip[source_tile, owner[:, None], position], 0)
    inlet_level = strips_all[source_tile, strip]
    pipe_level = jnp.take_along_axis(sewer_head, inlet_section, axis=1)
    rate = jnp.where(valid, inlet_coef, 0.0)[:, :, None] * (inlet_level - pipe_level[:, :, None])
    drained = jnp.zeros((TILES, STRIPS_DEV, 128), jnp.float32).at[source_tile, strip].add(rate)
    drain = drained.reshape(n_gx, n_gy, CX, CY).transpose(0, 2, 1, 3).reshape(NX, NY)
    inflow = jnp.zeros((LINES, SECTIONS), jnp.float32).at[jnp.arange(LINES)[:, None], inlet_section].add(lax.optimization_barrier(jnp.sum(rate, axis=2)))
    sewer_out = sewer_steps(sewer_head, conveyance, inflow)
    mask = open_cell.astype(jnp.float32)
    z_pad = jnp.pad(bed, 1)
    m_pad = jnp.pad(mask, 1)
    h1, hu1, hv1 = surface_step(jnp.pad(depth, 1), jnp.pad(momentum_x, 1), jnp.pad(momentum_y, 1), z_pad, m_pad, drain)
    h2, hu2, hv2 = surface_step(jnp.pad(h1, 1), jnp.pad(hu1, 1), jnp.pad(hv1, 1), z_pad, m_pad, drain)
    return (h2, hu2, hv2, sewer_out)
```

```python
import functools
import math

import jax
import jax.numpy as jnp
from jax import lax
from jax.experimental import pallas as pl
from jax.experimental.pallas import tpu as pltpu
from jax.sharding import PartitionSpec as P

SUBSTEPS = 8
GRAVITY = 9.81
DT = 0.02
SEWER_DT = 0.5
AREA = 256.0
HALF_DT = 0.5 * DT
ROOT_G = math.sqrt(GRAVITY)
HALF_G = 0.5 * GRAVITY
SLOPE = 0.5 * GRAVITY * DT
NGX = 8
NGY = 16
ROWS = 256
UNROLL = 8
F32 = jnp.float32
BF16 = jnp.bfloat16
I32 = jnp.int32
NT = (((1,), (1,)), ((), ()))


def thirds(x):
    a = x.astype(BF16)
    rest = x - a.astype(F32)
    b = rest.astype(BF16)
    c = (rest - b.astype(F32)).astype(BF16)
    return a, b, c


def lanes_at(row, idx):
    return jnp.take_along_axis(row, idx, axis=1, mode="promise_in_bounds")


def prim(h, hu, hv, om):
    hs = h + om
    y = lax.rsqrt(hs)
    inv = y * y
    u = hu * inv
    v = hv * inv
    c = (ROOT_G * hs) * y
    p = HALF_G * h * h
    return dict(
        h=h,
        hu=hu,
        hv=hv,
        uu=hu * u + p,
        uv=hu * v,
        vv=hv * v + p,
        sx=jnp.abs(u) + c,
        sy=jnp.abs(v) + c,
    )


def face_x(wall, l, r):
    a = jnp.maximum(l["sx"], r["sx"])
    return (
        wall * ((l["hu"] + r["hu"]) - a * (r["h"] - l["h"])),
        wall * ((l["uu"] + r["uu"]) - a * (r["hu"] - l["hu"])),
        wall * ((l["uv"] + r["uv"]) - a * (r["hv"] - l["hv"])),
    )


def face_y(wall, l, r):
    a = jnp.maximum(l["sy"], r["sy"])
    return (
        wall * ((l["hv"] + r["hv"]) - a * (r["h"] - l["h"])),
        wall * ((l["uv"] + r["uv"]) - a * (r["hu"] - l["hu"])),
        wall * ((l["vv"] + r["vv"]) - a * (r["hv"] - l["hv"])),
    )


def kernel(
    depth, mom_x, mom_y, bed, cells, strips, slots, sections, coefs, heads, conv,
    out_h, out_hu, out_hv, out_sewer,
    h0, hu0, hv0, z0, m0, level, h1, hu1, hv1, h2, hu2, hv2,
    om_s, wx_s, wy_s, sx_s, sy_s,
    onehot, msg, mid, mid_t, got, cpt,
    row_snd1, row_rcv1, row_snd2, row_rcv2, col_snd1, col_rcv1, col_snd2, col_rcv2,
    inflow_s,
    in_sem, out_sem, p1_send, p1_recv, p2_send, p2_recv, halo_send, halo_recv,
):
    gx = lax.axis_index("gx")
    gy = lax.axis_index("gy")

    def gx_peer(i):
        return {"gx": lax.rem(gx + i, NGX)}

    def gy_peer(i):
        return {"gy": lax.rem(gy + i, NGY)}

    pairs = ((depth, h0), (bed, z0), (cells, m0), (mom_x, hu0), (mom_y, hv0))

    def load(f, j):
        src, dst = pairs[f]
        return pltpu.make_async_copy(
            src.at[:, pl.ds(128 * j, 128)], dst.at[pl.ds(0, ROWS), j, :], in_sem.at[f, j]
        )

    for f in range(5):
        for j in range(8):
            load(f, j).start()

    barrier = pltpu.get_barrier_semaphore()
    for i in range(1, NGX):
        pl.semaphore_signal(barrier, inc=1, device_id=gx_peer(i), device_id_type=pl.DeviceIdType.MESH)
    for i in range(1, NGY):
        pl.semaphore_signal(barrier, inc=1, device_id=gy_peer(i), device_id_type=pl.DeviceIdType.MESH)

    lane = lax.broadcasted_iota(I32, (8, 128), 1)
    sub = lax.broadcasted_iota(I32, (8, 128), 0)
    zero_row = jnp.zeros((8, 128), F32)
    for ref in (h0, hu0, hv0, z0):
        ref[ROWS] = zero_row
    m0[ROWS] = jnp.zeros((8, 128), I32)
    for ref in (h1, hu1, hv1):
        ref[ROWS + 1] = zero_row
    cpt[2] = jnp.zeros((16, 128), F32)

    slot = slots[...]
    sec = sections[...]
    coef = coefs[...]
    tile_of = slot >> 4
    k_of = slot & 15
    pipe = jnp.zeros((16, 128), F32)
    for b in range(4):
        part = lanes_at(heads[:, pl.ds(128 * b, 128)], sec & 127)
        pipe = jnp.where((sec >> 7) == b, part, pipe)
    tile_iota = lax.broadcasted_iota(I32, (128, 128), 0)
    k_iota = lax.broadcasted_iota(I32, (16, 128), 0)
    left = []
    right = []
    for l in range(16):
        left.append((jnp.broadcast_to(tile_of[l : l + 1], (128, 128)) == tile_iota).astype(F32).astype(BF16))
        hit = jnp.broadcast_to(k_of[l : l + 1], (16, 128)) == k_iota
        both = jnp.concatenate(
            [
                jnp.where(hit, jnp.broadcast_to(coef[l : l + 1], (16, 128)), 0.0),
                jnp.where(hit, jnp.broadcast_to(pipe[l : l + 1], (16, 128)), 0.0),
            ],
            axis=0,
        )
        right.append(jnp.concatenate(thirds(both), axis=0))
    by_slot = lax.dot_general(
        jnp.concatenate(right, axis=1), jnp.concatenate(left, axis=1), NT, preferred_element_type=F32
    )
    by_slot = by_slot[0:32] + by_slot[32:64] + by_slot[64:96]

    strip = strips[0].T
    strip_row = strip >> 3
    strip_j = strip & 7
    for f in (0, 1):
        for j in range(8):
            load(f, j).wait()
    lane2 = lax.broadcasted_iota(I32, (8, 256), 1)

    def level_rows(t, sums):
        for i in range(UNROLL):
            r = t * UNROLL + i
            lev = h0[r] + z0[r]
            level[r] = lev
            sums = jnp.where(lane2 == r, jnp.sum(lev, axis=1, keepdims=True), sums)
        return sums

    sums = lax.fori_loop(0, ROWS // UNROLL, level_rows, jnp.zeros((8, 256), F32))
    level[ROWS] = zero_row
    by_strip = jnp.zeros((16, 128), F32)
    for half in range(2):
        for j in range(8):
            row = jnp.broadcast_to(sums[j : j + 1, 128 * half : 128 * half + 128], (16, 128))
            part = lanes_at(row, strip_row & 127)
            by_strip = jnp.where((strip_j == j) & ((strip_row >> 7) == half), part, by_strip)
    packed = jnp.concatenate([by_slot, by_strip, jnp.zeros((80, 128), F32)], axis=0).T
    msg[...] = packed.reshape(NGX, NGY, 128)

    pl.semaphore_wait(barrier, NGX + NGY - 2)

    def phase1(i):
        return pltpu.make_async_remote_copy(
            src_ref=msg.at[lax.rem(gx + i, NGX)],
            dst_ref=mid.at[gx],
            send_sem=p1_send.at[i - 1],
            recv_sem=p1_recv.at[i - 1],
            device_id=gx_peer(i),
            device_id_type=pl.DeviceIdType.MESH,
        )

    for i in range(1, NGX):
        phase1(i).start()
    mid[gx] = msg[gx]

    for f in (2, 3, 4):
        for j in range(8):
            load(f, j).wait()

    def rows_of(r):
        return (h0[r], hu0[r], hv0[r], m0[r].astype(F32), z0[r])

    for side, r in ((0, 0), (1, ROWS - 1)):
        for f, value in enumerate(rows_of(r)):
            row_snd1[side, f] = value

    def halo_rows(snd, rcv, side, base):
        return pltpu.make_async_remote_copy(
            src_ref=snd.at[side],
            dst_ref=rcv.at[1 - side],
            send_sem=halo_send.at[base + side],
            recv_sem=halo_recv.at[base + side],
            device_id=gx_peer(NGX - 1 if side == 0 else 1),
            device_id_type=pl.DeviceIdType.MESH,
        )

    def halo_cols(snd, rcv, side, base):
        return pltpu.make_async_remote_copy(
            src_ref=snd.at[side],
            dst_ref=rcv.at[1 - side],
            send_sem=halo_send.at[base + 2 + side],
            recv_sem=halo_recv.at[base + 2 + side],
            device_id=gy_peer(NGY - 1 if side == 0 else 1),
            device_id_type=pl.DeviceIdType.MESH,
        )

    for side in (0, 1):
        halo_rows(row_snd1, row_rcv1, side, 0).start()

    lane_col = lax.broadcasted_iota(I32, (ROWS, 128), 1)

    def slab(ref, first, j):
        return ref.reshape(ref.shape[0] * 8, 128)[pl.ds(first * 8 + j, ROWS, stride=8), :]

    def pack_columns(refs, first):
        total = jnp.zeros((ROWS, 128), F32)
        for f, ref in enumerate(refs):
            low = slab(ref, first, 0).astype(F32)
            high = slab(ref, first, 7).astype(F32)
            total = jnp.where(lane_col == f, pltpu.roll(low, f, 1) if f else low, total)
            total = jnp.where(lane_col == 8 + f, pltpu.roll(high, 9 + f, 1), total)
        return total.T[0:16]

    cols1 = pack_columns((h0, hu0, hv0, m0, z0), 0)
    for side in (0, 1):
        col_snd1[side] = cols1[8 * side : 8 * side + 8]
    for side in (0, 1):
        halo_cols(col_snd1, col_rcv1, side, 0).start()

    for i in range(1, NGX):
        phase1(i).wait_recv()
    mid_flat = mid.reshape(NGX * NGY, 128)
    for b in range(NGY):
        mid_t[b] = mid_flat[pl.ds(b, NGX, stride=NGY), :]

    def phase2(i):
        return pltpu.make_async_remote_copy(
            src_ref=mid_t.at[lax.rem(gy + i, NGY)],
            dst_ref=got.at[gy],
            send_sem=p2_send.at[i - 1],
            recv_sem=p2_recv.at[i - 1],
            device_id=gy_peer(i),
            device_id_type=pl.DeviceIdType.MESH,
        )

    for i in range(1, NGY):
        phase2(i).start()
    got[gy] = mid_t[gy]

    row_iota = lax.broadcasted_iota(I32, (ROWS, 128), 0)
    for k in range(16):
        hit = jnp.broadcast_to(strip_row[k : k + 1], (ROWS, 128)) == row_iota
        onehot[:, pl.ds(128 * k, 128)] = hit.astype(F32).astype(BF16)

    last_lane = lane == 127
    first_lane = lane == 0
    corner_r = (lane == 127) & (sub == 7)
    corner_l = (lane == 0) & (sub == 0)

    def from_right(x):
        a = pltpu.roll(x, 127, 1)
        return jnp.where(last_lane, pltpu.roll(a, 7, 0), a)

    def from_left(x):
        a = pltpu.roll(x, 1, 1)
        return jnp.where(first_lane, pltpu.roll(a, 1, 0), a)

    def inner_y(q, wall):
        r = {name: from_right(q[name]) for name in ("h", "hu", "hv", "uv", "vv", "sy")}
        flux = face_y(wall, q, r)
        return tuple(f - from_left(f) for f in flux)

    NAMES = ("h", "hu", "hv", "uu", "uv", "sx")

    def step_rows(r, carry, fields, om, wx, wy, sx, sy, outs, drain):
        prev, part = carry
        q = prim(*fields, om)
        fx = face_x(wx, prev, q)
        out_h_ref, out_hu_ref, out_hv_ref = outs
        out_h_ref[r] = part[0] - fx[0]
        out_hu_ref[r] = part[1] - fx[1] - prev["h"] * sx
        out_hv_ref[r] = part[2] - fx[2]
        dy = inner_y(q, wy)
        part_h = q["h"] - dy[0] + fx[0]
        if drain is not None:
            part_h = part_h - drain
        part = (part_h, q["hu"] - dy[1] + fx[1], q["hv"] - dy[2] - q["h"] * sy + fx[2])
        return {name: q[name] for name in NAMES}, part

    no_row = ({name: zero_row for name in NAMES}, (zero_row,) * 3)

    def first_row(r, carry):
        state, m_prev, z_prev, z_prev2 = carry
        m = m0[r].astype(F32)
        z = z0[r]
        om = 1.0 - m
        wx = (HALF_DT * m_prev) * m
        wy = jnp.where(corner_r, 0.0, (HALF_DT * m) * from_right(m))
        sx = (SLOPE * m_prev) * (z - z_prev2)
        zr = jnp.where(corner_r, 0.0, from_right(z))
        zl = jnp.where(corner_l, 0.0, from_left(z))
        sy = (SLOPE * m) * (zr - zl)
        om_s[r] = om
        wx_s[r] = wx
        wy_s[r] = wy
        sx_s[r] = sx
        sy_s[r] = sy
        state = step_rows(
            r, state, (h0[r], hu0[r], hv0[r]), om, wx, wy, sx, sy, (h1, hu1, hv1), None
        )
        return state, m, z, z_prev

    def first_rows(t, carry):
        for i in range(UNROLL):
            carry = first_row(t * UNROLL + i, carry)
        return carry

    carry = lax.fori_loop(0, ROWS // UNROLL, first_rows, (no_row, zero_row, zero_row, zero_row))
    first_row(ROWS, carry)

    def edge_faces_x(rows, halo, halo_m, halo_z, mine_m):
        out = []
        for side in (0, 1):
            mine = prim(*rows[side], 1.0 - mine_m[side])
            other = prim(*halo[side], 1.0 - halo_m[side])
            wall = (HALF_DT * halo_m[side]) * mine_m[side]
            slope = (SLOPE * mine_m[side]) * (halo_z[side] * mine["h"])
            if side == 0:
                f = face_x(wall, other, mine)
                out.append((f[0], f[1] + slope, f[2]))
            else:
                f = face_x(wall, mine, other)
                out.append((-f[0], -f[1] - slope, -f[2]))
        return out

    def edge_faces_y(cols, halo, halo_m, halo_z, mine_m):
        out = []
        for side in (0, 1):
            mine = prim(*cols[side], 1.0 - mine_m[side])
            other = prim(*halo[side], 1.0 - halo_m[side])
            wall = (HALF_DT * halo_m[side]) * mine_m[side]
            slope = (SLOPE * mine_m[side]) * (halo_z[side] * mine["h"])
            if side == 0:
                f = face_y(wall, other, mine)
                out.append((f[0], f[1], f[2] + slope))
            else:
                f = face_y(wall, mine, other)
                out.append((-f[0], -f[1], -f[2] - slope))
        return out

    def add_columns(refs, first, faces):
        rows = []
        for side in (0, 1):
            rows += list(faces[side]) + [jnp.zeros((5, ROWS), F32)]
        by_row = jnp.concatenate(rows + [jnp.zeros((112, ROWS), F32)], axis=0).T
        for f, ref in enumerate(refs):
            flat = ref.reshape(ref.shape[0] * 8, 128)
            low = pl.ds(first * 8, ROWS, stride=8)
            high = pl.ds(first * 8 + 7, ROWS, stride=8)
            more = pltpu.roll(by_row, 128 - f, 1) if f else by_row
            flat[low, :] = flat[low, :] + jnp.where(lane_col == 0, more, 0.0)
            more = pltpu.roll(by_row, 127 - 8 - f, 1)
            flat[high, :] = flat[high, :] + jnp.where(lane_col == 127, more, 0.0)

    for side in (0, 1):
        halo_rows(row_snd1, row_rcv1, side, 0).wait()
        halo_cols(col_snd1, col_rcv1, side, 0).wait()
    exists_x = (gx > 0, gx < NGX - 1)
    exists_y = (gy > 0, gy < NGY - 1)

    def keep(yes, x):
        return jnp.where(yes, x, 0.0)

    halo_x = [[keep(exists_x[side], row_rcv1[side, f]) for f in range(5)] for side in (0, 1)]
    mine_x = [[row_snd1[side, f] for f in range(5)] for side in (0, 1)]
    halo_y = [[keep(exists_y[side], col_rcv1[side, f : f + 1]) for f in range(5)] for side in (0, 1)]
    mine_y = [[col_snd1[side, f : f + 1] for f in range(5)] for side in (0, 1)]
    hmx = [halo_x[s][3] for s in (0, 1)]
    hzx = [halo_x[s][4] for s in (0, 1)]
    mmx = [mine_x[s][3] for s in (0, 1)]
    hmy = [halo_y[s][3] for s in (0, 1)]
    hzy = [halo_y[s][4] for s in (0, 1)]
    mmy = [mine_y[s][3] for s in (0, 1)]
    faces = edge_faces_x([mine_x[s][:3] for s in (0, 1)], [halo_x[s][:3] for s in (0, 1)], hmx, hzx, mmx)
    for side, r in ((0, 1), (1, ROWS)):
        for f, ref in enumerate((h1, hu1, hv1)):
            ref[r] = ref[r] + faces[side][f]
    faces = edge_faces_y([mine_y[s][:3] for s in (0, 1)], [halo_y[s][:3] for s in (0, 1)], hmy, hzy, mmy)
    add_columns((h1, hu1, hv1), 1, faces)
    cols2 = pack_columns((h1, hu1, hv1), 1)

    for i in range(1, NGY):
        phase2(i).wait_recv()
    got_flat = got.reshape(NGX * NGY, 128)
    arrived = jnp.concatenate([got_flat[pl.ds(a, NGY, stride=NGX), :] for a in range(NGX)], axis=0).T
    right = []
    j_iota = lax.broadcasted_iota(I32, (8, 128), 0)
    for k in range(16):
        hit = jnp.broadcast_to(strip_j[k : k + 1], (8, 128)) == j_iota
        both = jnp.concatenate(
            [
                jnp.where(hit, jnp.broadcast_to(arrived[k : k + 1], (8, 128)), 0.0),
                jnp.where(hit, jnp.broadcast_to(arrived[16 + k : 17 + k], (8, 128)), 0.0),
            ],
            axis=0,
        )
        right.append(jnp.concatenate(thirds(both), axis=0))
    by_row = lax.dot_general(jnp.concatenate(right, axis=1), onehot[...], NT, preferred_element_type=F32)
    by_row = by_row[0:16] + by_row[16:32] + by_row[32:48]
    for half in range(2):
        cpt[half] = by_row[:, 128 * half : 128 * half + 128]

    def drain_of(r):
        half = r // 128
        at = jnp.full((8, 128), r - half * 128, I32)
        c = lanes_at(cpt[half, 0:8], at)
        p = lanes_at(cpt[half, 8:16], at)
        return (DT * c) * (level[r] - p)

    own_x = []
    for side, r in ((0, 0), (1, ROWS - 1)):
        own_x.append((h1[r + 1] - drain_of(r), hu1[r + 1], hv1[r + 1]))
        for f in range(3):
            row_snd2[side, f] = own_x[side][f]
    own_y = []
    for side, j in ((0, 0), (1, 7)):
        lev = mine_y[side][0] + mine_y[side][4]
        less = (DT * by_row[j : j + 1]) * (lev - by_row[8 + j : 9 + j])
        c = cols2[8 * side : 8 * side + 8]
        own_y.append((c[0:1] - less, c[1:2], c[2:3]))
        col_snd2[side] = jnp.concatenate(list(own_y[side]) + [jnp.zeros((5, ROWS), F32)], axis=0)
    for side in (0, 1):
        halo_rows(row_snd2, row_rcv2, side, 4).start()
        halo_cols(col_snd2, col_rcv2, side, 4).start()

    def second_row(r, state):
        less = drain_of(r)
        fields = (h1[r + 1] - less, hu1[r + 1], hv1[r + 1])
        return step_rows(
            r, state, fields, om_s[r], wx_s[r], wy_s[r], sx_s[r], sy_s[r], (h2, hu2, hv2), less
        )

    def second_rows(t, state):
        for i in range(UNROLL):
            state = second_row(t * UNROLL + i, state)
        return state

    state = lax.fori_loop(0, ROWS // UNROLL, second_rows, no_row)
    second_row(ROWS, state)

    for side in (0, 1):
        halo_rows(row_snd2, row_rcv2, side, 4).wait()
        halo_cols(col_snd2, col_rcv2, side, 4).wait()
    halo_x = [[keep(exists_x[side], row_rcv2[side, f]) for f in range(3)] for side in (0, 1)]
    halo_y = [[keep(exists_y[side], col_rcv2[side, f : f + 1]) for f in range(3)] for side in (0, 1)]
    faces = edge_faces_x(own_x, halo_x, hmx, hzx, mmx)
    for side, r in ((0, 1), (1, ROWS)):
        for f, ref in enumerate((h2, hu2, hv2)):
            ref[r] = ref[r] + faces[side][f]

    outs = ((h2, out_h), (hu2, out_hu), (hv2, out_hv))

    def store(f, j):
        src, dst = outs[f]
        return pltpu.make_async_copy(
            src.at[pl.ds(1, ROWS), j, :], dst.at[:, pl.ds(128 * j, 128)], out_sem.at[f, j]
        )

    for f in range(3):
        for j in range(1, 7):
            store(f, j).start()
    faces = edge_faces_y(own_y, halo_y, hmy, hzy, mmy)
    add_columns((h2, hu2, hv2), 1, faces)
    for f in range(3):
        for j in (0, 7):
            store(f, j).start()

    level_sum = jnp.zeros((16, 128), F32)
    for k in range(16):
        row = jnp.broadcast_to(arrived[32 + k : 33 + k], (16, 128))
        level_sum = jnp.where(k_of == k, lanes_at(row, tile_of & 127), level_sum)
    rate = jnp.where(slot >= 0, coef * (level_sum - 128.0 * pipe), 0.0)
    block = lax.broadcasted_iota(I32, (8, 128), 0)
    for l in range(16):
        s_row = sec[l : l + 1]
        hit = (jnp.broadcast_to(s_row & 127, (128, 128)) == tile_iota).astype(F32).astype(BF16)
        value = jnp.where(
            jnp.broadcast_to(s_row >> 7, (8, 128)) == block, jnp.broadcast_to(rate[l : l + 1], (8, 128)), 0.0
        )
        got_l = lax.dot_general(jnp.concatenate(thirds(value), axis=0), hit, NT, preferred_element_type=F32)
        got_l = got_l[0:8] + got_l[8:16] + got_l[16:24]
        for b in range(4):
            inflow_s[l : l + 1, pl.ds(128 * b, 128)] = got_l[b : b + 1]
    share = inflow_s[...] / AREA
    head = heads[...]
    cv = conv[...]
    sec_lane = lax.broadcasted_iota(I32, (16, 512), 1)
    face_k = jnp.where(sec_lane == 511, cv, 0.5 * (cv + pltpu.roll(cv, 511, 1)))
    for turn in range(SUBSTEPS):
        below = jnp.where(sec_lane == 511, 0.0, pltpu.roll(head, 511, 1))
        leaving = face_k * (head - below)
        entering = jnp.where(sec_lane == 0, 0.0, pltpu.roll(leaving, 1, 1))
        head = head + SEWER_DT * (entering - leaving + share)
    out_sewer[...] = head

    for i in range(1, NGX):
        phase1(i).wait_send()
    for i in range(1, NGY):
        phase2(i).wait_send()
    for f in range(3):
        for j in range(8):
            store(f, j).wait()


def body(*args):
    rows, cols = args[0].shape
    field = functools.partial(pltpu.VMEM, dtype=F32)
    any_space = pl.BlockSpec(memory_space=pl.ANY)
    vmem = pl.BlockSpec(memory_space=pltpu.VMEM)
    grid = jax.ShapeDtypeStruct((rows, cols), F32)
    sewer = jax.ShapeDtypeStruct(args[9].shape, F32)
    dma = pltpu.SemaphoreType.DMA
    return pl.pallas_call(
        kernel,
        out_shape=(grid, grid, grid, sewer),
        in_specs=[any_space] * 5 + [vmem] * 6,
        out_specs=(any_space, any_space, any_space, vmem),
        scratch_shapes=[
            pltpu.VMEM((ROWS + 1, 8, 128), F32),
            pltpu.VMEM((ROWS + 1, 8, 128), F32),
            pltpu.VMEM((ROWS + 1, 8, 128), F32),
            pltpu.VMEM((ROWS + 1, 8, 128), F32),
            pltpu.VMEM((ROWS + 1, 8, 128), I32),
            pltpu.VMEM((ROWS + 1, 8, 128), F32),
        ]
        + [pltpu.VMEM((ROWS + 2, 8, 128), F32)] * 3
        + [pltpu.VMEM((ROWS + 1, 8, 128), F32)] * 8
        + [
            pltpu.VMEM((ROWS, 2048), BF16),
            pltpu.VMEM((NGX, NGY, 128), F32),
            pltpu.VMEM((NGX, NGY, 128), F32),
            pltpu.VMEM((NGY, NGX, 128), F32),
            pltpu.VMEM((NGY, NGX, 128), F32),
            pltpu.VMEM((3, 16, 128), F32),
            pltpu.VMEM((2, 5, 8, 128), F32),
            pltpu.VMEM((2, 5, 8, 128), F32),
            pltpu.VMEM((2, 3, 8, 128), F32),
            pltpu.VMEM((2, 3, 8, 128), F32),
            pltpu.VMEM((2, 8, ROWS), F32),
            pltpu.VMEM((2, 8, ROWS), F32),
            pltpu.VMEM((2, 8, ROWS), F32),
            pltpu.VMEM((2, 8, ROWS), F32),
            pltpu.VMEM((16, 512), F32),
            dma((5, 8)),
            dma((3, 8)),
            dma((NGX - 1,)),
            dma((NGX - 1,)),
            dma((NGY - 1,)),
            dma((NGY - 1,)),
            dma((8,)),
            dma((8,)),
        ],
        compiler_params=pltpu.CompilerParams(
            collective_id=0, has_side_effects=True, vmem_limit_bytes=48 * 1024 * 1024
        ),
        name="street_flood",
    )(*args)


def solution(mesh):
    tiles = P("gx", "gy")
    lines = P(("gx", "gy"), None)
    return jax.shard_map(
        body,
        mesh=mesh,
        in_specs=(tiles,) * 5 + (P(("gx", "gy"), None, None),) + (lines,) * 5,
        out_specs=(tiles, tiles, tiles, lines),
        check_vma=False,
    )
```

```python
import math

import jax
import jax.numpy as jnp
from jax import lax
from jax.experimental import pallas as pl
from jax.experimental.pallas import tpu as pltpu
from jax.sharding import PartitionSpec as P

SUBSTEPS = 8
GRAVITY = 9.81
DT = 0.02
SEWER_DT = 0.5
AREA = 256.0
HALF_DT = 0.5 * DT
ROOT_G = math.sqrt(GRAVITY)
HALF_G = 0.5 * GRAVITY
SLOPE = 0.5 * GRAVITY * DT
NGX = 8
NGY = 16
ROWS = 256
UNROLL = 16
F32 = jnp.float32
BF16 = jnp.bfloat16
I32 = jnp.int32
NT = (((1,), (1,)), ((), ()))


def thirds(x):
    a = x.astype(BF16)
    rest = x - a.astype(F32)
    b = rest.astype(BF16)
    c = (rest - b.astype(F32)).astype(BF16)
    return a, b, c


def lanes_at(row, idx):
    return jnp.take_along_axis(row, idx, axis=1, mode="promise_in_bounds")


def prim(h, hu, hv, om):
    hs = h + om
    y = lax.rsqrt(hs)
    inv = y * y
    u = hu * inv
    v = hv * inv
    c = (ROOT_G * hs) * y
    p = HALF_G * h * h
    return dict(
        h=h,
        hu=hu,
        hv=hv,
        uu=hu * u + p,
        uv=hu * v,
        vv=hv * v + p,
        sx=jnp.abs(u) + c,
        sy=jnp.abs(v) + c,
    )


def face_x(wall, l, r):
    a = jnp.maximum(l["sx"], r["sx"])
    return (
        wall * ((l["hu"] + r["hu"]) - a * (r["h"] - l["h"])),
        wall * ((l["uu"] + r["uu"]) - a * (r["hu"] - l["hu"])),
        wall * ((l["uv"] + r["uv"]) - a * (r["hv"] - l["hv"])),
    )


def face_y(wall, l, r):
    a = jnp.maximum(l["sy"], r["sy"])
    return (
        wall * ((l["hv"] + r["hv"]) - a * (r["h"] - l["h"])),
        wall * ((l["uv"] + r["uv"]) - a * (r["hu"] - l["hu"])),
        wall * ((l["vv"] + r["vv"]) - a * (r["hv"] - l["hv"])),
    )


def faces_x(rows, halo, halo_m, halo_z, mine_m):
    out = []
    for side in (0, 1):
        mine = prim(*rows[side], 1.0 - mine_m[side])
        other = prim(*halo[side], 1.0 - halo_m[side])
        wall = (HALF_DT * halo_m[side]) * mine_m[side]
        slope = (SLOPE * mine_m[side]) * (halo_z[side] * mine["h"])
        if side == 0:
            f = face_x(wall, other, mine)
            out.append((f[0], f[1] + slope, f[2]))
        else:
            f = face_x(wall, mine, other)
            out.append((-f[0], -f[1] - slope, -f[2]))
    return out


def faces_y(cols, halo, halo_m, halo_z, mine_m):
    out = []
    for side in (0, 1):
        mine = prim(*cols[side], 1.0 - mine_m[side])
        other = prim(*halo[side], 1.0 - halo_m[side])
        wall = (HALF_DT * halo_m[side]) * mine_m[side]
        slope = (SLOPE * mine_m[side]) * (halo_z[side] * mine["h"])
        if side == 0:
            f = face_y(wall, other, mine)
            out.append((f[0], f[1], f[2] + slope))
        else:
            f = face_y(wall, mine, other)
            out.append((-f[0], -f[1], -f[2] - slope))
    return out


def slab_of(ref, first, j):
    return ref.reshape(ref.shape[0] * 8, 128), pl.ds(first * 8 + j, ROWS, stride=8)


def faces_by_row(faces):
    rows = []
    for side in (0, 1):
        rows += list(faces[side]) + [jnp.zeros((5, ROWS), F32)]
    return jnp.concatenate(rows + [jnp.zeros((112, ROWS), F32)], axis=0).T


def column_sum(by_row, f, side, flat, rows):
    at = 0 if side == 0 else 127
    lane = lax.broadcasted_iota(I32, (ROWS, 128), 1)
    move = (at - 8 * side - f) % 128
    more = pltpu.roll(by_row, move, 1) if move else by_row
    return flat[rows, :] + jnp.where(lane == at, more, 0.0)


def kernel(
    depth, mom_x, mom_y, bed, cells, strips_in, slots_in, sections_in, coefs_in, heads_in,
    h2, hu2, hv2, edge_out, rate_out,
    h0, hu0, hv0, z0, m0, level, h1, hu1, hv1,
    om_s, omr_s, wx_s, wy_s, sx_s, sy_s,
    strips, slots, sections, coefs, heads,
    onehot, msg, mid, mid_t, got, cpt,
    row_snd1, row_rcv1, row_snd2, row_rcv2, col_snd1, col_rcv1, col_snd2, col_rcv2,
    in_sem, small_sem, p1_send, p1_recv, p2_send, p2_recv, halo_send, halo_recv,
):
    gx = lax.axis_index("gx")
    gy = lax.axis_index("gy")

    def gx_peer(i):
        return {"gx": lax.rem(gx + i, NGX)}

    def gy_peer(i):
        return {"gy": lax.rem(gy + i, NGY)}

    pairs = ((depth, h0), (bed, z0), (cells, m0), (mom_x, hu0), (mom_y, hv0))

    def load(f, j):
        src, dst = pairs[f]
        return pltpu.make_async_copy(
            src.at[:, pl.ds(128 * j, 128)], dst.at[pl.ds(0, ROWS), j, :], in_sem.at[f, j]
        )

    small = ((slots_in, slots), (sections_in, sections), (coefs_in, coefs), (heads_in, heads), (strips_in, strips))

    def load_small(i):
        return pltpu.make_async_copy(small[i][0], small[i][1], small_sem.at[i])

    for i in range(5):
        load_small(i).start()
    for f in range(5):
        for j in range(8):
            load(f, j).start()

    barrier = pltpu.get_barrier_semaphore()
    for i in range(1, NGX):
        pl.semaphore_signal(barrier, inc=1, device_id=gx_peer(i), device_id_type=pl.DeviceIdType.MESH)
    for i in range(1, NGY):
        pl.semaphore_signal(barrier, inc=1, device_id=gy_peer(i), device_id_type=pl.DeviceIdType.MESH)

    lane = lax.broadcasted_iota(I32, (8, 128), 1)
    sub = lax.broadcasted_iota(I32, (8, 128), 0)
    zero_row = jnp.zeros((8, 128), F32)

    for i in range(4):
        load_small(i).wait()
    slot = slots[...]
    sec = sections[...]
    coef = coefs[...]
    tile_of = slot >> 4
    k_of = slot & 15
    pipe = jnp.zeros((16, 128), F32)
    for b in range(4):
        part = lanes_at(heads[:, pl.ds(128 * b, 128)], sec & 127)
        pipe = jnp.where((sec >> 7) == b, part, pipe)
    tile_iota = lax.broadcasted_iota(I32, (128, 128), 0)
    k_iota = lax.broadcasted_iota(I32, (16, 128), 0)
    left = []
    right = []
    for l in range(16):
        left.append((jnp.broadcast_to(tile_of[l : l + 1], (128, 128)) == tile_iota).astype(F32).astype(BF16))
        hit = jnp.broadcast_to(k_of[l : l + 1], (16, 128)) == k_iota
        both = jnp.concatenate(
            [
                jnp.where(hit, jnp.broadcast_to(coef[l : l + 1], (16, 128)), 0.0),
                jnp.where(hit, jnp.broadcast_to(pipe[l : l + 1], (16, 128)), 0.0),
            ],
            axis=0,
        )
        right.append(jnp.concatenate(thirds(both), axis=0))
    by_slot = lax.dot_general(
        jnp.concatenate(right, axis=1), jnp.concatenate(left, axis=1), NT, preferred_element_type=F32
    )
    by_slot = by_slot[0:32] + by_slot[32:64] + by_slot[64:96]

    load_small(4).wait()
    strip = strips[0]
    strip_row = strip >> 3
    strip_j = strip & 7
    for f in (0, 1):
        for j in range(8):
            load(f, j).wait()
    lane2 = lax.broadcasted_iota(I32, (8, 256), 1)

    def level_rows(t, sums):
        for i in range(32):
            r = t * 32 + i
            lev = h0[r] + z0[r]
            level[r] = lev
            sums = jnp.where(lane2 == r, jnp.sum(lev, axis=1, keepdims=True), sums)
        return sums

    sums = lax.fori_loop(0, ROWS // 32, level_rows, jnp.zeros((8, 256), F32))
    by_strip = jnp.zeros((16, 128), F32)
    for half in range(2):
        for j in range(8):
            row = jnp.broadcast_to(sums[j : j + 1, 128 * half : 128 * half + 128], (16, 128))
            part = lanes_at(row, strip_row & 127)
            by_strip = jnp.where((strip_j == j) & ((strip_row >> 7) == half), part, by_strip)
    packed = jnp.concatenate([by_slot, by_strip, jnp.zeros((80, 128), F32)], axis=0).T
    msg[...] = packed.reshape(NGX, NGY, 128)

    pl.semaphore_wait(barrier, NGX + NGY - 2)

    def phase1(i):
        return pltpu.make_async_remote_copy(
            src_ref=msg.at[lax.rem(gx + i, NGX)],
            dst_ref=mid.at[gx],
            send_sem=p1_send.at[i - 1],
            recv_sem=p1_recv.at[i - 1],
            device_id=gx_peer(i),
            device_id_type=pl.DeviceIdType.MESH,
        )

    for i in range(1, NGX):
        phase1(i).start()
    mid[gx] = msg[gx]

    for f in (2, 3, 4):
        for j in range(8):
            load(f, j).wait()

    def rows_of(r):
        return (h0[r], hu0[r], hv0[r], m0[r].astype(F32), z0[r])

    for side, r in ((0, 0), (1, ROWS - 1)):
        for f, value in enumerate(rows_of(r)):
            row_snd1[side, f] = value

    def halo_rows(snd, rcv, side, base):
        return pltpu.make_async_remote_copy(
            src_ref=snd.at[side],
            dst_ref=rcv.at[1 - side],
            send_sem=halo_send.at[base + side],
            recv_sem=halo_recv.at[base + side],
            device_id=gx_peer(NGX - 1 if side == 0 else 1),
            device_id_type=pl.DeviceIdType.MESH,
        )

    def halo_cols(snd, rcv, side, base):
        return pltpu.make_async_remote_copy(
            src_ref=snd.at[side],
            dst_ref=rcv.at[1 - side],
            send_sem=halo_send.at[base + 2 + side],
            recv_sem=halo_recv.at[base + 2 + side],
            device_id=gy_peer(NGY - 1 if side == 0 else 1),
            device_id_type=pl.DeviceIdType.MESH,
        )

    for side in (0, 1):
        halo_rows(row_snd1, row_rcv1, side, 0).start()

    lane_col = lax.broadcasted_iota(I32, (ROWS, 128), 1)

    def slab(ref, first, j):
        flat, rows = slab_of(ref, first, j)
        return flat[rows, :]

    def pack_columns(refs, first):
        total = jnp.zeros((ROWS, 128), F32)
        for f, ref in enumerate(refs):
            low = slab(ref, first, 0).astype(F32)
            high = slab(ref, first, 7).astype(F32)
            total = jnp.where(lane_col == f, pltpu.roll(low, f, 1) if f else low, total)
            total = jnp.where(lane_col == 8 + f, pltpu.roll(high, 9 + f, 1), total)
        return total.T[0:16]

    cols1 = pack_columns((h0, hu0, hv0, m0, z0), 0)
    for side in (0, 1):
        col_snd1[side] = cols1[8 * side : 8 * side + 8]
    for side in (0, 1):
        halo_cols(col_snd1, col_rcv1, side, 0).start()

    last_lane = lane == 127
    first_lane = lane == 0
    corner_r = (lane == 127) & (sub == 7)
    corner_l = (lane == 0) & (sub == 0)

    def from_right(x):
        a = pltpu.roll(x, 127, 1)
        return jnp.where(last_lane, pltpu.roll(a, 7, 0), a)

    def from_left(x):
        a = pltpu.roll(x, 1, 1)
        return jnp.where(first_lane, pltpu.roll(a, 1, 0), a)

    def static_rows(t, carry):
        for i in range(UNROLL):
            r = t * UNROLL + i
            m_prev, z_prev, z_prev2 = carry
            m = m0[r].astype(F32)
            z = z0[r]
            mr = from_right(m)
            om_s[r] = 1.0 - m
            omr_s[r] = 1.0 - mr
            wx_s[r] = (HALF_DT * m_prev) * m
            wy_s[r] = jnp.where(corner_r, 0.0, (HALF_DT * m) * mr)
            sx_s[r] = (SLOPE * m_prev) * (z - z_prev2)
            zr = jnp.where(corner_r, 0.0, from_right(z))
            zl = jnp.where(corner_l, 0.0, from_left(z))
            sy_s[r] = (SLOPE * m) * (zr - zl)
            carry = (m, z, z_prev)
        return carry

    m_end, _, z_end = lax.fori_loop(0, ROWS // UNROLL, static_rows, (zero_row,) * 3)
    sx_s[ROWS] = (SLOPE * m_end) * (-z_end)

    for i in range(1, NGX):
        phase1(i).wait_recv()
    mid_flat = mid.reshape(NGX * NGY, 128)
    for b in range(NGY):
        mid_t[b] = mid_flat[pl.ds(b, NGX, stride=NGY), :]

    def phase2(i):
        return pltpu.make_async_remote_copy(
            src_ref=mid_t.at[lax.rem(gy + i, NGY)],
            dst_ref=got.at[gy],
            send_sem=p2_send.at[i - 1],
            recv_sem=p2_recv.at[i - 1],
            device_id=gy_peer(i),
            device_id_type=pl.DeviceIdType.MESH,
        )

    for i in range(1, NGY):
        phase2(i).start()
    got[gy] = mid_t[gy]

    row_iota = lax.broadcasted_iota(I32, (ROWS, 128), 0)
    for k in range(16):
        hit = jnp.broadcast_to(strip_row[k : k + 1], (ROWS, 128)) == row_iota
        onehot[:, pl.ds(128 * k, 128)] = hit.astype(F32).astype(BF16)

    NAMES = ("h", "hu", "hv", "uu", "uv", "sx")

    def sweep(src, off, outs, drain):
        def one(r, carry):
            prev, part = carry
            raw = [ref[r + off] for ref in src]
            q = prim(*raw, om_s[r])
            right = prim(*[from_right(x) for x in raw], omr_s[r])
            fx = face_x(wx_s[r], prev, q)
            outs[0][r] = part[0] - fx[0]
            outs[1][r] = part[1] - fx[1] - prev["h"] * sx_s[r]
            outs[2][r] = part[2] - fx[2]
            dy = [f - from_left(f) for f in face_y(wy_s[r], q, right)]
            part_h = q["h"] - dy[0] + fx[0]
            if drain is not None:
                part_h = part_h - drain[r]
            part = (part_h, q["hu"] - dy[1] + fx[1], q["hv"] - dy[2] - q["h"] * sy_s[r] + fx[2])
            return {name: q[name] for name in NAMES}, part

        def some(t, carry):
            for i in range(UNROLL):
                carry = one(t * UNROLL + i, carry)
            return carry

        start = ({name: zero_row for name in NAMES}, (zero_row,) * 3)
        prev, part = lax.fori_loop(0, ROWS // UNROLL, some, start)
        outs[0][ROWS] = part[0]
        outs[1][ROWS] = part[1] - prev["h"] * sx_s[ROWS]
        outs[2][ROWS] = part[2]

    sweep((h0, hu0, hv0), 0, (h1, hu1, hv1), None)

    for side in (0, 1):
        halo_rows(row_snd1, row_rcv1, side, 0).wait()
        halo_cols(col_snd1, col_rcv1, side, 0).wait()
    exists_x = (gx > 0, gx < NGX - 1)
    exists_y = (gy > 0, gy < NGY - 1)

    def keep(yes, x):
        return jnp.where(yes, x, 0.0)

    halo_x = [[keep(exists_x[side], row_rcv1[side, f]) for f in range(5)] for side in (0, 1)]
    mine_x = [[row_snd1[side, f] for f in range(5)] for side in (0, 1)]
    halo_y = [[keep(exists_y[side], col_rcv1[side, f : f + 1]) for f in range(5)] for side in (0, 1)]
    mine_y = [[col_snd1[side, f : f + 1] for f in range(5)] for side in (0, 1)]
    hmx = [halo_x[s][3] for s in (0, 1)]
    hzx = [halo_x[s][4] for s in (0, 1)]
    mmx = [mine_x[s][3] for s in (0, 1)]
    hmy = [halo_y[s][3] for s in (0, 1)]
    hzy = [halo_y[s][4] for s in (0, 1)]
    mmy = [mine_y[s][3] for s in (0, 1)]
    faces = faces_x([mine_x[s][:3] for s in (0, 1)], [halo_x[s][:3] for s in (0, 1)], hmx, hzx, mmx)
    for side, r in ((0, 1), (1, ROWS)):
        for f, ref in enumerate((h1, hu1, hv1)):
            ref[r] = ref[r] + faces[side][f]
    faces = faces_y([mine_y[s][:3] for s in (0, 1)], [halo_y[s][:3] for s in (0, 1)], hmy, hzy, mmy)
    by_row = faces_by_row(faces)
    for f, ref in enumerate((h1, hu1, hv1)):
        for side in (0, 1):
            flat, rows = slab_of(ref, 1, 7 * side)
            flat[rows, :] = column_sum(by_row, f, side, flat, rows)
    cols2 = pack_columns((h1, hu1, hv1), 1)

    for i in range(1, NGY):
        phase2(i).wait_recv()
    got_flat = got.reshape(NGX * NGY, 128)
    arrived = jnp.concatenate([got_flat[pl.ds(a, NGY, stride=NGX), :] for a in range(NGX)], axis=0).T
    right = []
    j_iota = lax.broadcasted_iota(I32, (8, 128), 0)
    for k in range(16):
        hit = jnp.broadcast_to(strip_j[k : k + 1], (8, 128)) == j_iota
        both = jnp.concatenate(
            [
                jnp.where(hit, jnp.broadcast_to(arrived[k : k + 1], (8, 128)), 0.0),
                jnp.where(hit, jnp.broadcast_to(arrived[16 + k : 17 + k], (8, 128)), 0.0),
            ],
            axis=0,
        )
        right.append(jnp.concatenate(thirds(both), axis=0))
    by_row = lax.dot_general(jnp.concatenate(right, axis=1), onehot[...], NT, preferred_element_type=F32)
    by_row = by_row[0:16] + by_row[16:32] + by_row[32:48]
    for half in range(2):
        cpt[half] = by_row[:, 128 * half : 128 * half + 128]

    def drain_of(r):
        half = r // 128
        at = jnp.full((8, 128), r - half * 128, I32)
        c = lanes_at(cpt[half, 0:8], at)
        p = lanes_at(cpt[half, 8:16], at)
        return (DT * c) * (level[r] - p)

    own_x = []
    for side, r in ((0, 0), (1, ROWS - 1)):
        own_x.append((h1[r + 1] - drain_of(r), hu1[r + 1], hv1[r + 1]))
        for f in range(3):
            row_snd2[side, f] = own_x[side][f]
    own_y = []
    for side, j in ((0, 0), (1, 7)):
        lev = mine_y[side][0] + mine_y[side][4]
        less = (DT * by_row[j : j + 1]) * (lev - by_row[8 + j : 9 + j])
        c = cols2[8 * side : 8 * side + 8]
        own_y.append((c[0:1] - less, c[1:2], c[2:3]))
        col_snd2[side] = jnp.concatenate(list(own_y[side]) + [jnp.zeros((5, ROWS), F32)], axis=0)
    for side in (0, 1):
        halo_rows(row_snd2, row_rcv2, side, 4).start()
        halo_cols(col_snd2, col_rcv2, side, 4).start()

    def drain_rows(t, carry):
        for i in range(32):
            r = t * 32 + i
            less = drain_of(r)
            level[r] = less
            h1[r + 1] = h1[r + 1] - less
        return carry

    lax.fori_loop(0, ROWS // 32, drain_rows, 0)
    sweep((h1, hu1, hv1), 1, (h2, hu2, hv2), level)

    for side in (0, 1):
        halo_rows(row_snd2, row_rcv2, side, 4).wait()
        halo_cols(col_snd2, col_rcv2, side, 4).wait()
    halo_x = [[keep(exists_x[side], row_rcv2[side, f]) for f in range(3)] for side in (0, 1)]
    halo_y = [[keep(exists_y[side], col_rcv2[side, f : f + 1]) for f in range(3)] for side in (0, 1)]
    faces = faces_x(own_x, halo_x, hmx, hzx, mmx)
    for side, r in ((0, 1), (1, ROWS)):
        for f, ref in enumerate((h2, hu2, hv2)):
            ref[r] = ref[r] + faces[side][f]

    for side in (0, 1):
        rows = list(own_y[side]) + [mmy[side], hzy[side], hmy[side]] + halo_y[side]
        edge_out[side] = jnp.concatenate(rows + [jnp.zeros((7, ROWS), F32)], axis=0)

    level_sum = jnp.zeros((16, 128), F32)
    for k in range(16):
        row = jnp.broadcast_to(arrived[32 + k : 33 + k], (16, 128))
        level_sum = jnp.where(k_of == k, lanes_at(row, tile_of & 127), level_sum)
    rate = jnp.where(slot >= 0, coef * (level_sum - 128.0 * pipe), 0.0)
    rate_out[...] = rate

    for i in range(1, NGX):
        phase1(i).wait_send()
    for i in range(1, NGY):
        phase2(i).wait_send()


def finish(
    h2, hu2, hv2, edge, rate_in, sections_in, heads_in, conv_in,
    out_h, out_hu, out_hv, out_sewer,
    slabs, sections, heads, conv, inflow_s, sewer_s,
    out_sem, small_sem, sewer_sem,
):
    small = ((sections_in, sections), (heads_in, heads), (conv_in, conv))

    def load_small(i):
        return pltpu.make_async_copy(small[i][0], small[i][1], small_sem.at[i])

    for i in range(3):
        load_small(i).start()
    outs = ((h2, out_h), (hu2, out_hu), (hv2, out_hv))

    def store(f, j):
        src, dst = outs[f]
        if j in (0, 7):
            part = slabs.at[f, j // 7]
        else:
            part = src.at[pl.ds(1, ROWS), j, :]
        return pltpu.make_async_copy(part, dst.at[:, pl.ds(128 * j, 128)], out_sem.at[f, j])

    for f in range(3):
        for j in range(1, 7):
            store(f, j).start()

    def row(side, i):
        return edge[side, i : i + 1]

    own = [[row(s, i) for i in range(3)] for s in (0, 1)]
    halo = [[row(s, 6 + i) for i in range(3)] for s in (0, 1)]
    faces = faces_y(
        own, halo, [row(s, 5) for s in (0, 1)], [row(s, 4) for s in (0, 1)], [row(s, 3) for s in (0, 1)]
    )
    by_row = faces_by_row(faces)
    for f, (ref, _) in enumerate(outs):
        for side in (0, 1):
            flat, rows = slab_of(ref, 1, 7 * side)
            slabs[f, side] = column_sum(by_row, f, side, flat, rows)
            store(f, 7 * side).start()

    for i in range(3):
        load_small(i).wait()
    rate = rate_in[...]
    sec = sections[...]
    tile_iota = lax.broadcasted_iota(I32, (128, 128), 0)
    block = lax.broadcasted_iota(I32, (8, 128), 0)
    for l in range(16):
        s_row = sec[l : l + 1]
        hit = (jnp.broadcast_to(s_row & 127, (128, 128)) == tile_iota).astype(F32).astype(BF16)
        value = jnp.where(
            jnp.broadcast_to(s_row >> 7, (8, 128)) == block, jnp.broadcast_to(rate[l : l + 1], (8, 128)), 0.0
        )
        got_l = lax.dot_general(jnp.concatenate(thirds(value), axis=0), hit, NT, preferred_element_type=F32)
        got_l = got_l[0:8] + got_l[8:16] + got_l[16:24]
        for b in range(4):
            inflow_s[l : l + 1, pl.ds(128 * b, 128)] = got_l[b : b + 1]
    share = inflow_s[...] / AREA
    head = heads[...]
    cv = conv[...]
    sec_lane = lax.broadcasted_iota(I32, (16, 512), 1)
    face_k = jnp.where(sec_lane == 511, cv, 0.5 * (cv + pltpu.roll(cv, 511, 1)))
    for turn in range(SUBSTEPS):
        below = jnp.where(sec_lane == 511, 0.0, pltpu.roll(head, 511, 1))
        leaving = face_k * (head - below)
        entering = jnp.where(sec_lane == 0, 0.0, pltpu.roll(leaving, 1, 1))
        head = head + SEWER_DT * (entering - leaving + share)
    sewer_s[...] = head
    last = pltpu.make_async_copy(sewer_s, out_sewer, sewer_sem)
    last.start()
    for f in range(3):
        for j in range(8):
            store(f, j).wait()
    last.wait()

def body(*args):
    args = [jnp.swapaxes(a, 1, 2) if a.ndim == 3 else a for a in args]
    rows, cols = args[0].shape
    grid = jax.ShapeDtypeStruct((rows, cols), F32)
    sewer = jax.ShapeDtypeStruct(args[9].shape, F32)
    args = [pltpu.with_memory_space_constraint(a, pltpu.HBM) for a in args]
    depth, mom_x, mom_y, bed, cells, strips, slots, sections, coefs, heads, conv = args
    hbm = pl.BlockSpec(memory_space=pltpu.HBM)
    vmem = pl.BlockSpec(memory_space=pltpu.VMEM)
    dma = pltpu.SemaphoreType.DMA
    padded = pltpu.VMEM((ROWS + 1, 8, 128), F32)
    h2, hu2, hv2, edge, rate = pl.pallas_call(
        kernel,
        out_shape=(padded,) * 3
        + (pltpu.VMEM((2, 16, ROWS), F32), pltpu.VMEM(slots.shape, F32)),
        in_specs=[hbm] * 10,
        out_specs=(vmem,) * 5,
        scratch_shapes=[pltpu.VMEM((ROWS, 8, 128), F32)] * 4
        + [pltpu.VMEM((ROWS, 8, 128), I32), pltpu.VMEM((ROWS, 8, 128), F32)]
        + [pltpu.VMEM((ROWS + 1, 8, 128), F32)] * 9
        + [
            pltpu.VMEM((1, 16, 128), I32),
            pltpu.VMEM((16, 128), I32),
            pltpu.VMEM((16, 128), I32),
            pltpu.VMEM((16, 128), F32),
            pltpu.VMEM((16, 512), F32),
            pltpu.VMEM((ROWS, 2048), BF16),
            pltpu.VMEM((NGX, NGY, 128), F32),
            pltpu.VMEM((NGX, NGY, 128), F32),
            pltpu.VMEM((NGY, NGX, 128), F32),
            pltpu.VMEM((NGY, NGX, 128), F32),
            pltpu.VMEM((2, 16, 128), F32),
            pltpu.VMEM((2, 5, 8, 128), F32),
            pltpu.VMEM((2, 5, 8, 128), F32),
            pltpu.VMEM((2, 3, 8, 128), F32),
            pltpu.VMEM((2, 3, 8, 128), F32),
            pltpu.VMEM((2, 8, ROWS), F32),
            pltpu.VMEM((2, 8, ROWS), F32),
            pltpu.VMEM((2, 8, ROWS), F32),
            pltpu.VMEM((2, 8, ROWS), F32),
            dma((5, 8)),
            dma((5,)),
            dma((NGX - 1,)),
            dma((NGX - 1,)),
            dma((NGY - 1,)),
            dma((NGY - 1,)),
            dma((8,)),
            dma((8,)),
        ],
        compiler_params=pltpu.CompilerParams(
            collective_id=0, has_side_effects=True, vmem_limit_bytes=40 * 1024 * 1024
        ),
        name="street_flood",
    )(depth, mom_x, mom_y, bed, cells, strips, slots, sections, coefs, heads)
    return pl.pallas_call(
        finish,
        out_shape=(grid, grid, grid, sewer),
        in_specs=[vmem] * 5 + [hbm] * 3,
        out_specs=(hbm,) * 4,
        scratch_shapes=[
            pltpu.VMEM((3, 2, ROWS, 128), F32),
            pltpu.VMEM((16, 128), I32),
            pltpu.VMEM((16, 512), F32),
            pltpu.VMEM((16, 512), F32),
            pltpu.VMEM((16, 512), F32),
            pltpu.VMEM((16, 512), F32),
            dma((3, 8)),
            dma((3,)),
            dma,
        ],
        compiler_params=pltpu.CompilerParams(vmem_limit_bytes=16 * 1024 * 1024),
        name="flood_finish",
    )(h2, hu2, hv2, edge, rate, sections, heads, conv)


def solution(mesh):
    tiles = P("gx", "gy")
    lines = P(("gx", "gy"), None)
    return jax.shard_map(
        body,
        mesh=mesh,
        in_specs=(tiles,) * 5 + (P(("gx", "gy"), None, None),) + (lines,) * 5,
        out_specs=(tiles, tiles, tiles, lines),
        check_vma=False,
    )
```

```python
import math

import jax
import jax.numpy as jnp
from jax import lax
from jax.experimental import pallas as pl
from jax.experimental.pallas import tpu as pltpu
from jax.sharding import PartitionSpec as P

SUBSTEPS = 8
GRAVITY = 9.81
DT = 0.02
SEWER_DT = 0.5
AREA = 256.0
HALF_DT = 0.5 * DT
ROOT_G = math.sqrt(GRAVITY)
HALF_G = 0.5 * GRAVITY
SLOPE = 0.5 * GRAVITY * DT
NGX = 8
NGY = 16
ROWS = 256
UNROLL = 16
F32 = jnp.float32
BF16 = jnp.bfloat16
I32 = jnp.int32
NT = (((1,), (1,)), ((), ()))


def thirds(x):
    a = x.astype(BF16)
    rest = x - a.astype(F32)
    b = rest.astype(BF16)
    c = (rest - b.astype(F32)).astype(BF16)
    return a, b, c


def lanes_at(row, idx):
    return jnp.take_along_axis(row, idx, axis=1, mode="promise_in_bounds")


def prim(h, hu, hv, om):
    hs = h + om
    y = lax.rsqrt(hs)
    inv = y * y
    u = hu * inv
    v = hv * inv
    c = (ROOT_G * hs) * y
    p = HALF_G * h * h
    return dict(
        h=h,
        hu=hu,
        hv=hv,
        uu=hu * u + p,
        uv=hu * v,
        vv=hv * v + p,
        sx=jnp.abs(u) + c,
        sy=jnp.abs(v) + c,
    )


def face_x(wall, l, r):
    a = jnp.maximum(l["sx"], r["sx"])
    return (
        wall * ((l["hu"] + r["hu"]) - a * (r["h"] - l["h"])),
        wall * ((l["uu"] + r["uu"]) - a * (r["hu"] - l["hu"])),
        wall * ((l["uv"] + r["uv"]) - a * (r["hv"] - l["hv"])),
    )


def face_y(wall, l, r):
    a = jnp.maximum(l["sy"], r["sy"])
    return (
        wall * ((l["hv"] + r["hv"]) - a * (r["h"] - l["h"])),
        wall * ((l["uv"] + r["uv"]) - a * (r["hu"] - l["hu"])),
        wall * ((l["vv"] + r["vv"]) - a * (r["hv"] - l["hv"])),
    )


def faces_x(rows, halo, halo_m, halo_z, mine_m):
    out = []
    for side in (0, 1):
        mine = prim(*rows[side], 1.0 - mine_m[side])
        other = prim(*halo[side], 1.0 - halo_m[side])
        wall = (HALF_DT * halo_m[side]) * mine_m[side]
        slope = (SLOPE * mine_m[side]) * (halo_z[side] * mine["h"])
        if side == 0:
            f = face_x(wall, other, mine)
            out.append((f[0], f[1] + slope, f[2]))
        else:
            f = face_x(wall, mine, other)
            out.append((-f[0], -f[1] - slope, -f[2]))
    return out


def faces_y(cols, halo, halo_m, halo_z, mine_m):
    out = []
    for side in (0, 1):
        mine = prim(*cols[side], 1.0 - mine_m[side])
        other = prim(*halo[side], 1.0 - halo_m[side])
        wall = (HALF_DT * halo_m[side]) * mine_m[side]
        slope = (SLOPE * mine_m[side]) * (halo_z[side] * mine["h"])
        if side == 0:
            f = face_y(wall, other, mine)
            out.append((f[0], f[1], f[2] + slope))
        else:
            f = face_y(wall, mine, other)
            out.append((-f[0], -f[1], -f[2] - slope))
    return out


def slab_of(ref, first, j):
    return ref.reshape(ref.shape[0] * 8, 128), pl.ds(first * 8 + j, ROWS, stride=8)


def edge_matrix(left, right):
    sub = lax.broadcasted_iota(I32, (8, ROWS), 0)
    top = jnp.where(sub == 0, jnp.broadcast_to(left, (8, ROWS)), 0.0)
    bottom = jnp.where(sub == 7, jnp.broadcast_to(right, (8, ROWS)), 0.0)
    return jnp.concatenate([top, jnp.zeros((112, ROWS), F32), bottom], axis=0).T


def edge_slabs(ref, first, terms):
    lane = lax.broadcasted_iota(I32, (ROWS, 128), 1)
    flat, low = slab_of(ref, first, 0)
    _, high = slab_of(ref, first, 7)
    return (
        flat[low, :] + jnp.where(lane == 0, terms, 0.0),
        flat[high, :] + jnp.where(lane == 127, terms, 0.0),
    )


def edge_columns(low, high):
    lane = lax.broadcasted_iota(I32, (ROWS, 128), 1)
    both = jnp.where(lane < 64, low, high).T
    return both[0:1], both[127:128]


def kernel(
    depth, mom_x, mom_y, bed, cells, strips_in, slots_in, sections_in, coefs_in, heads_in,
    h2, hu2, hv2, edge_out, rate_out,
    h0, hu0, hv0, z0, m0, level, h1, hu1, hv1,
    om_s, omr_s, wx_s, wy_s, sx_s, sy_s,
    strips, slots, sections, coefs, heads,
    onehot, msg, mid, mid_t, got, slot_coef, slot_pipe, ring,
    row_snd1, row_rcv1, row_snd2, row_rcv2, col_snd1, col_rcv1, col_snd2, col_rcv2,
    in_sem, small_sem, p1_send, p1_recv, p2_send, p2_recv, halo_send, halo_recv,
):
    gx = lax.axis_index("gx")
    gy = lax.axis_index("gy")

    def gx_peer(i):
        return {"gx": lax.rem(gx + i, NGX)}

    def gy_peer(i):
        return {"gy": lax.rem(gy + i, NGY)}

    pairs = ((depth, h0), (bed, z0), (cells, m0), (mom_x, hu0), (mom_y, hv0))

    def load(f, j):
        src, dst = pairs[f]
        return pltpu.make_async_copy(
            src.at[:, pl.ds(128 * j, 128)], dst.at[pl.ds(0, ROWS), j, :], in_sem.at[f, j]
        )

    small = ((slots_in, slots), (sections_in, sections), (coefs_in, coefs), (heads_in, heads), (strips_in, strips))

    def load_small(i):
        return pltpu.make_async_copy(small[i][0], small[i][1], small_sem.at[i])

    for i in range(5):
        load_small(i).start()
    for f in range(5):
        for j in range(8):
            load(f, j).start()

    barrier = pltpu.get_barrier_semaphore()
    for i in range(1, NGX):
        pl.semaphore_signal(barrier, inc=1, device_id=gx_peer(i), device_id_type=pl.DeviceIdType.MESH)
    for i in range(1, NGY):
        pl.semaphore_signal(barrier, inc=1, device_id=gy_peer(i), device_id_type=pl.DeviceIdType.MESH)

    lane = lax.broadcasted_iota(I32, (8, 128), 1)
    sub = lax.broadcasted_iota(I32, (8, 128), 0)
    zero_row = jnp.zeros((8, 128), F32)

    for i in range(4):
        load_small(i).wait()
    slot = slots[...]
    sec = sections[...]
    coef = coefs[...]
    tile_of = slot >> 4
    k_of = slot & 15
    pipe = jnp.zeros((16, 128), F32)
    for b in range(4):
        part = lanes_at(heads[:, pl.ds(128 * b, 128)], sec & 127)
        pipe = jnp.where((sec >> 7) == b, part, pipe)
    tile_iota = lax.broadcasted_iota(I32, (128, 128), 0)
    k_iota = lax.broadcasted_iota(I32, (16, 128), 0)
    left = []
    right = []
    for l in range(16):
        left.append((jnp.broadcast_to(tile_of[l : l + 1], (128, 128)) == tile_iota).astype(F32).astype(BF16))
        hit = jnp.broadcast_to(k_of[l : l + 1], (16, 128)) == k_iota
        both = jnp.concatenate(
            [
                jnp.where(hit, jnp.broadcast_to(coef[l : l + 1], (16, 128)), 0.0),
                jnp.where(hit, jnp.broadcast_to(pipe[l : l + 1], (16, 128)), 0.0),
            ],
            axis=0,
        )
        right.append(jnp.concatenate(thirds(both), axis=0))
    by_slot = lax.dot_general(
        jnp.concatenate(right, axis=1), jnp.concatenate(left, axis=1), NT, preferred_element_type=F32
    )
    by_slot = by_slot[0:32] + by_slot[32:64] + by_slot[64:96]

    load_small(4).wait()
    strip = strips[0]
    strip_row = strip >> 3
    strip_j = strip & 7
    for f in (0, 1):
        for j in range(8):
            load(f, j).wait()
    lane2 = lax.broadcasted_iota(I32, (8, 256), 1)

    def level_rows(t, sums):
        for i in range(32):
            r = t * 32 + i
            lev = h0[r] + z0[r]
            level[r] = lev
            sums = jnp.where(lane2 == r, jnp.sum(lev, axis=1, keepdims=True), sums)
        return sums

    sums = lax.fori_loop(0, ROWS // 32, level_rows, jnp.zeros((8, 256), F32))
    by_strip = jnp.zeros((16, 128), F32)
    for half in range(2):
        for j in range(8):
            row = jnp.broadcast_to(sums[j : j + 1, 128 * half : 128 * half + 128], (16, 128))
            part = lanes_at(row, strip_row & 127)
            by_strip = jnp.where((strip_j == j) & ((strip_row >> 7) == half), part, by_strip)
    packed = jnp.concatenate([by_slot, by_strip, jnp.zeros((80, 128), F32)], axis=0).T
    msg[...] = packed.reshape(NGX, NGY, 128)

    pl.semaphore_wait(barrier, NGX + NGY - 2)

    def phase1(i):
        return pltpu.make_async_remote_copy(
            src_ref=msg.at[lax.rem(gx + i, NGX)],
            dst_ref=mid.at[gx],
            send_sem=p1_send.at[i - 1],
            recv_sem=p1_recv.at[i - 1],
            device_id=gx_peer(i),
            device_id_type=pl.DeviceIdType.MESH,
        )

    for i in range(1, NGX):
        phase1(i).start()
    mid[gx] = msg[gx]

    for f in (2, 3, 4):
        for j in range(8):
            load(f, j).wait()

    def rows_of(r):
        return (h0[r], hu0[r], hv0[r], m0[r].astype(F32), z0[r])

    for side, r in ((0, 0), (1, ROWS - 1)):
        for f, value in enumerate(rows_of(r)):
            row_snd1[side, f] = value

    def halo_rows(snd, rcv, side, base):
        return pltpu.make_async_remote_copy(
            src_ref=snd.at[side],
            dst_ref=rcv.at[1 - side],
            send_sem=halo_send.at[base + side],
            recv_sem=halo_recv.at[base + side],
            device_id=gx_peer(NGX - 1 if side == 0 else 1),
            device_id_type=pl.DeviceIdType.MESH,
        )

    def halo_cols(snd, rcv, side, base):
        return pltpu.make_async_remote_copy(
            src_ref=snd.at[side],
            dst_ref=rcv.at[1 - side],
            send_sem=halo_send.at[base + 2 + side],
            recv_sem=halo_recv.at[base + 2 + side],
            device_id=gy_peer(NGY - 1 if side == 0 else 1),
            device_id_type=pl.DeviceIdType.MESH,
        )

    for side in (0, 1):
        halo_rows(row_snd1, row_rcv1, side, 0).start()

    cols1 = ([], [])
    for ref in (h0, hu0, hv0, m0, z0):
        flat, low = slab_of(ref, 0, 0)
        _, high = slab_of(ref, 0, 7)
        ends = edge_columns(flat[low, :].astype(F32), flat[high, :].astype(F32))
        for side in (0, 1):
            cols1[side].append(ends[side])
    for side in (0, 1):
        col_snd1[side] = jnp.concatenate(cols1[side] + [jnp.zeros((3, ROWS), F32)], axis=0)
        halo_cols(col_snd1, col_rcv1, side, 0).start()

    last_lane = lane == 127
    first_lane = lane == 0
    corner_r = (lane == 127) & (sub == 7)
    corner_l = (lane == 0) & (sub == 0)

    def from_right(x):
        a = pltpu.roll(x, 127, 1)
        return jnp.where(last_lane, pltpu.roll(a, 7, 0), a)

    def from_left(x):
        a = pltpu.roll(x, 1, 1)
        return jnp.where(first_lane, pltpu.roll(a, 1, 0), a)

    def static_rows(t, carry):
        for i in range(32):
            r = t * 32 + i
            m_prev, z_prev, z_prev2 = carry
            m = m0[r].astype(F32)
            z = z0[r]
            mr = from_right(m)
            om_s[r] = 1.0 - m
            omr_s[r] = 1.0 - mr
            wx_s[r] = (HALF_DT * m_prev) * m
            wy_s[r] = jnp.where(corner_r, 0.0, (HALF_DT * m) * mr)
            sx_s[r] = (SLOPE * m_prev) * (z - z_prev2)
            zr = jnp.where(corner_r, 0.0, from_right(z))
            zl = jnp.where(corner_l, 0.0, from_left(z))
            sy_s[r] = (SLOPE * m) * (zr - zl)
            carry = (m, z, z_prev)
        return carry

    m_end, _, z_end = lax.fori_loop(0, ROWS // 32, static_rows, (zero_row,) * 3)
    sx_s[ROWS] = (SLOPE * m_end) * (-z_end)

    for i in range(1, NGX):
        phase1(i).wait_recv()
    mid_flat = mid.reshape(NGX * NGY, 128)
    for b in range(NGY):
        mid_t[b] = mid_flat[pl.ds(b, NGX, stride=NGY), :]

    def phase2(i):
        return pltpu.make_async_remote_copy(
            src_ref=mid_t.at[lax.rem(gy + i, NGY)],
            dst_ref=got.at[gy],
            send_sem=p2_send.at[i - 1],
            recv_sem=p2_recv.at[i - 1],
            device_id=gy_peer(i),
            device_id_type=pl.DeviceIdType.MESH,
        )

    for i in range(1, NGY):
        phase2(i).start()
    got[gy] = mid_t[gy]

    row_iota = lax.broadcasted_iota(I32, (ROWS, 128), 0)
    for k in range(16):
        hit = jnp.broadcast_to(strip_row[k : k + 1], (ROWS, 128)) == row_iota
        onehot[:, pl.ds(128 * k, 128)] = hit.astype(F32).astype(BF16)

    NAMES = ("h", "hu", "hv", "uu", "uv", "sx")

    def sweep(src, off, outs, drained):
        def ahead(r, i):
            h = src[0][r + off]
            if drained:
                less = slot_coef[r] * (level[r] - slot_pipe[r])
                h = h - less
                ring[3, i] = less
                ring[4, i] = h
            ring[0, i] = from_right(h)
            ring[1, i] = from_right(src[1][r + off])
            ring[2, i] = from_right(src[2][r + off])

        def one(r, i, carry):
            prev, part = carry
            h = ring[4, i] if drained else src[0][r + off]
            q = prim(h, src[1][r + off], src[2][r + off], om_s[r])
            right = prim(ring[0, i], ring[1, i], ring[2, i], omr_s[r])
            fx = face_x(wx_s[r], prev, q)
            outs[0][r] = part[0] - fx[0]
            outs[1][r] = part[1] - fx[1] - prev["h"] * sx_s[r]
            outs[2][r] = part[2] - fx[2]
            dy = [f - from_left(f) for f in face_y(wy_s[r], q, right)]
            part_h = q["h"] - dy[0] + fx[0]
            if drained:
                part_h = part_h - ring[3, i]
            part = (part_h, q["hu"] - dy[1] + fx[1], q["hv"] - dy[2] - q["h"] * sy_s[r] + fx[2])
            return {name: q[name] for name in NAMES}, part

        turns = ROWS // UNROLL
        for i in range(UNROLL):
            ahead(i, i)

        def some(t, carry):
            following = jnp.minimum(t + 1, turns - 1) * UNROLL
            for i in range(UNROLL):
                carry = one(t * UNROLL + i, i, carry)
                ahead(following + i, i)
            return carry

        start = ({name: zero_row for name in NAMES}, (zero_row,) * 3)
        prev, part = lax.fori_loop(0, turns, some, start)
        outs[0][ROWS] = part[0]
        outs[1][ROWS] = part[1] - prev["h"] * sx_s[ROWS]
        outs[2][ROWS] = part[2]

    sweep((h0, hu0, hv0), 0, (h1, hu1, hv1), False)

    for side in (0, 1):
        halo_rows(row_snd1, row_rcv1, side, 0).wait()
        halo_cols(col_snd1, col_rcv1, side, 0).wait()
    exists_x = (gx > 0, gx < NGX - 1)
    exists_y = (gy > 0, gy < NGY - 1)

    def keep(yes, x):
        return jnp.where(yes, x, 0.0)

    halo_x = [[keep(exists_x[side], row_rcv1[side, f]) for f in range(5)] for side in (0, 1)]
    mine_x = [[row_snd1[side, f] for f in range(5)] for side in (0, 1)]
    halo_y = [[keep(exists_y[side], col_rcv1[side, f : f + 1]) for f in range(5)] for side in (0, 1)]
    mine_y = [[col_snd1[side, f : f + 1] for f in range(5)] for side in (0, 1)]
    hmx = [halo_x[s][3] for s in (0, 1)]
    hzx = [halo_x[s][4] for s in (0, 1)]
    mmx = [mine_x[s][3] for s in (0, 1)]
    hmy = [halo_y[s][3] for s in (0, 1)]
    hzy = [halo_y[s][4] for s in (0, 1)]
    mmy = [mine_y[s][3] for s in (0, 1)]
    faces = faces_x([mine_x[s][:3] for s in (0, 1)], [halo_x[s][:3] for s in (0, 1)], hmx, hzx, mmx)
    for side, r in ((0, 1), (1, ROWS)):
        for f, ref in enumerate((h1, hu1, hv1)):
            ref[r] = ref[r] + faces[side][f]
    faces = faces_y([mine_y[s][:3] for s in (0, 1)], [halo_y[s][:3] for s in (0, 1)], hmy, hzy, mmy)
    cols2 = []
    for f, ref in enumerate((h1, hu1, hv1)):
        low, high = edge_slabs(ref, 1, edge_matrix(faces[0][f], faces[1][f]))
        flat, rows = slab_of(ref, 1, 0)
        flat[rows, :] = low
        flat, rows = slab_of(ref, 1, 7)
        flat[rows, :] = high
        cols2.append(edge_columns(low, high))

    for i in range(1, NGY):
        phase2(i).wait_recv()
    got_flat = got.reshape(NGX * NGY, 128)
    arrived = jnp.concatenate([got_flat[pl.ds(a, NGY, stride=NGX), :] for a in range(NGX)], axis=0).T
    right = []
    j_iota = lax.broadcasted_iota(I32, (8, 128), 0)
    for k in range(16):
        hit = jnp.broadcast_to(strip_j[k : k + 1], (8, 128)) == j_iota
        both = jnp.concatenate(
            [
                jnp.where(hit, jnp.broadcast_to(arrived[k : k + 1], (8, 128)), 0.0),
                jnp.where(hit, jnp.broadcast_to(arrived[16 + k : 17 + k], (8, 128)), 0.0),
            ],
            axis=0,
        )
        right.append(jnp.concatenate(thirds(both), axis=0))
    by_row = lax.dot_general(jnp.concatenate(right, axis=1), onehot[...], NT, preferred_element_type=F32)
    by_row = by_row[0:16] + by_row[16:32] + by_row[32:48]
    by_row = jnp.concatenate([DT * by_row[0:8], by_row[8:16]], axis=0)

    def drain_of(r):
        lanes = by_row[:, 0:128] if r < 128 else by_row[:, 128:256]
        at = r % 128
        c = jnp.broadcast_to(lanes[0:8, at : at + 1], (8, 128))
        p = jnp.broadcast_to(lanes[8:16, at : at + 1], (8, 128))
        return c * (level[r] - p)

    own_x = []
    for side, r in ((0, 0), (1, ROWS - 1)):
        own_x.append((h1[r + 1] - drain_of(r), hu1[r + 1], hv1[r + 1]))
        for f in range(3):
            row_snd2[side, f] = own_x[side][f]
    own_y = []
    for side, j in ((0, 0), (1, 7)):
        lev = mine_y[side][0] + mine_y[side][4]
        less = by_row[j : j + 1] * (lev - by_row[8 + j : 9 + j])
        own_y.append((cols2[0][side] - less, cols2[1][side], cols2[2][side]))
        col_snd2[side] = jnp.concatenate(list(own_y[side]) + [jnp.zeros((5, ROWS), F32)], axis=0)
    for side in (0, 1):
        halo_rows(row_snd2, row_rcv2, side, 4).start()
        halo_cols(col_snd2, col_rcv2, side, 4).start()

    for ref, first in ((slot_coef, 0), (slot_pipe, 8)):
        for half in range(2):
            for j in range(8):
                value = by_row[first + j : first + j + 1, 128 * half : 128 * half + 128]
                flat = ref.reshape(ROWS * 8, 128)
                flat[pl.ds(1024 * half + j, 128, stride=8), :] = jnp.broadcast_to(value, (128, 128)).T
    sweep((h1, hu1, hv1), 1, (h2, hu2, hv2), True)

    for side in (0, 1):
        halo_rows(row_snd2, row_rcv2, side, 4).wait()
        halo_cols(col_snd2, col_rcv2, side, 4).wait()
    halo_x = [[keep(exists_x[side], row_rcv2[side, f]) for f in range(3)] for side in (0, 1)]
    halo_y = [[keep(exists_y[side], col_rcv2[side, f : f + 1]) for f in range(3)] for side in (0, 1)]
    faces = faces_x(own_x, halo_x, hmx, hzx, mmx)
    for side, r in ((0, 1), (1, ROWS)):
        for f, ref in enumerate((h2, hu2, hv2)):
            ref[r] = ref[r] + faces[side][f]

    for side in (0, 1):
        rows = list(own_y[side]) + [mmy[side], hzy[side], hmy[side]] + halo_y[side]
        edge_out[side] = jnp.concatenate(rows + [jnp.zeros((7, ROWS), F32)], axis=0)

    level_sum = jnp.zeros((16, 128), F32)
    for k in range(16):
        row = jnp.broadcast_to(arrived[32 + k : 33 + k], (16, 128))
        level_sum = jnp.where(k_of == k, lanes_at(row, tile_of & 127), level_sum)
    rate = jnp.where(slot >= 0, coef * (level_sum - 128.0 * pipe), 0.0)
    rate_out[...] = rate

    for i in range(1, NGX):
        phase1(i).wait_send()
    for i in range(1, NGY):
        phase2(i).wait_send()


def finish(
    h2, hu2, hv2, edge, rate_in, sections_in, heads_in, conv_in,
    out_h, out_hu, out_hv, out_sewer,
    slabs, sections, heads, conv, inflow_s, sewer_s,
    out_sem, small_sem, sewer_sem,
):
    small = ((sections_in, sections), (heads_in, heads), (conv_in, conv))

    def load_small(i):
        return pltpu.make_async_copy(small[i][0], small[i][1], small_sem.at[i])

    for i in range(3):
        load_small(i).start()
    outs = ((h2, out_h), (hu2, out_hu), (hv2, out_hv))

    def store(f, j):
        src, dst = outs[f]
        if j in (0, 7):
            part = slabs.at[f, j // 7]
        else:
            part = src.at[pl.ds(1, ROWS), j, :]
        return pltpu.make_async_copy(part, dst.at[:, pl.ds(128 * j, 128)], out_sem.at[f, j])

    for f in range(3):
        for j in range(1, 7):
            store(f, j).start()

    def row(side, i):
        return edge[side, i : i + 1]

    own = [[row(s, i) for i in range(3)] for s in (0, 1)]
    halo = [[row(s, 6 + i) for i in range(3)] for s in (0, 1)]
    faces = faces_y(
        own, halo, [row(s, 5) for s in (0, 1)], [row(s, 4) for s in (0, 1)], [row(s, 3) for s in (0, 1)]
    )
    for f, (ref, _) in enumerate(outs):
        both = edge_slabs(ref, 1, edge_matrix(faces[0][f], faces[1][f]))
        for side in (0, 1):
            slabs[f, side] = both[side]
            store(f, 7 * side).start()

    for i in range(3):
        load_small(i).wait()
    rate = rate_in[...]
    sec = sections[...]
    tile_iota = lax.broadcasted_iota(I32, (128, 128), 0)
    block = lax.broadcasted_iota(I32, (8, 128), 0)
    for l in range(16):
        s_row = sec[l : l + 1]
        hit = (jnp.broadcast_to(s_row & 127, (128, 128)) == tile_iota).astype(F32).astype(BF16)
        value = jnp.where(
            jnp.broadcast_to(s_row >> 7, (8, 128)) == block, jnp.broadcast_to(rate[l : l + 1], (8, 128)), 0.0
        )
        got_l = lax.dot_general(jnp.concatenate(thirds(value), axis=0), hit, NT, preferred_element_type=F32)
        got_l = got_l[0:8] + got_l[8:16] + got_l[16:24]
        for b in range(4):
            inflow_s[l : l + 1, pl.ds(128 * b, 128)] = got_l[b : b + 1]
    share = inflow_s[...] / AREA
    head = heads[...]
    cv = conv[...]
    sec_lane = lax.broadcasted_iota(I32, (16, 512), 1)
    face_k = jnp.where(sec_lane == 511, cv, 0.5 * (cv + pltpu.roll(cv, 511, 1)))
    above_k = jnp.where(sec_lane == 0, 0.0, pltpu.roll(face_k, 1, 1))
    for turn in range(SUBSTEPS):
        below = jnp.where(sec_lane == 511, 0.0, pltpu.roll(head, 511, 1))
        leaving = face_k * (head - below)
        entering = above_k * (pltpu.roll(head, 1, 1) - head)
        head = head + SEWER_DT * (entering - leaving + share)
    sewer_s[...] = head
    last = pltpu.make_async_copy(sewer_s, out_sewer, sewer_sem)
    last.start()
    for f in range(3):
        for j in range(8):
            store(f, j).wait()
    last.wait()

def body(*args):
    args = [jnp.swapaxes(a, 1, 2) if a.ndim == 3 else a for a in args]
    rows, cols = args[0].shape
    grid = jax.ShapeDtypeStruct((rows, cols), F32)
    sewer = jax.ShapeDtypeStruct(args[9].shape, F32)
    args = [pltpu.with_memory_space_constraint(a, pltpu.HBM) for a in args]
    depth, mom_x, mom_y, bed, cells, strips, slots, sections, coefs, heads, conv = args
    hbm = pl.BlockSpec(memory_space=pltpu.HBM)
    vmem = pl.BlockSpec(memory_space=pltpu.VMEM)
    dma = pltpu.SemaphoreType.DMA
    padded = pltpu.VMEM((ROWS + 1, 8, 128), F32)
    h2, hu2, hv2, edge, rate = pl.pallas_call(
        kernel,
        out_shape=(padded,) * 3
        + (pltpu.VMEM((2, 16, ROWS), F32), pltpu.VMEM(slots.shape, F32)),
        in_specs=[hbm] * 10,
        out_specs=(vmem,) * 5,
        scratch_shapes=[pltpu.VMEM((ROWS, 8, 128), F32)] * 4
        + [pltpu.VMEM((ROWS, 8, 128), I32), pltpu.VMEM((ROWS, 8, 128), F32)]
        + [pltpu.VMEM((ROWS + 1, 8, 128), F32)] * 9
        + [
            pltpu.VMEM((1, 16, 128), I32),
            pltpu.VMEM((16, 128), I32),
            pltpu.VMEM((16, 128), I32),
            pltpu.VMEM((16, 128), F32),
            pltpu.VMEM((16, 512), F32),
            pltpu.VMEM((ROWS, 2048), BF16),
            pltpu.VMEM((NGX, NGY, 128), F32),
            pltpu.VMEM((NGX, NGY, 128), F32),
            pltpu.VMEM((NGY, NGX, 128), F32),
            pltpu.VMEM((NGY, NGX, 128), F32),
            pltpu.VMEM((ROWS, 8, 128), F32),
            pltpu.VMEM((ROWS, 8, 128), F32),
            pltpu.VMEM((5, UNROLL, 8, 128), F32),
            pltpu.VMEM((2, 5, 8, 128), F32),
            pltpu.VMEM((2, 5, 8, 128), F32),
            pltpu.VMEM((2, 3, 8, 128), F32),
            pltpu.VMEM((2, 3, 8, 128), F32),
            pltpu.VMEM((2, 8, ROWS), F32),
            pltpu.VMEM((2, 8, ROWS), F32),
            pltpu.VMEM((2, 8, ROWS), F32),
            pltpu.VMEM((2, 8, ROWS), F32),
            dma((5, 8)),
            dma((5,)),
            dma((NGX - 1,)),
            dma((NGX - 1,)),
            dma((NGY - 1,)),
            dma((NGY - 1,)),
            dma((8,)),
            dma((8,)),
        ],
        compiler_params=pltpu.CompilerParams(
            collective_id=0, has_side_effects=True, vmem_limit_bytes=40 * 1024 * 1024
        ),
        name="street_flood",
    )(depth, mom_x, mom_y, bed, cells, strips, slots, sections, coefs, heads)
    return pl.pallas_call(
        finish,
        out_shape=(grid, grid, grid, sewer),
        in_specs=[vmem] * 5 + [hbm] * 3,
        out_specs=(hbm,) * 4,
        scratch_shapes=[
            pltpu.VMEM((3, 2, ROWS, 128), F32),
            pltpu.VMEM((16, 128), I32),
            pltpu.VMEM((16, 512), F32),
            pltpu.VMEM((16, 512), F32),
            pltpu.VMEM((16, 512), F32),
            pltpu.VMEM((16, 512), F32),
            dma((3, 8)),
            dma((3,)),
            dma,
        ],
        compiler_params=pltpu.CompilerParams(vmem_limit_bytes=16 * 1024 * 1024),
        name="flood_finish",
    )(h2, hu2, hv2, edge, rate, sections, heads, conv)


def solution(mesh):
    tiles = P("gx", "gy")
    lines = P(("gx", "gy"), None)
    return jax.shard_map(
        body,
        mesh=mesh,
        in_specs=(tiles,) * 5 + (P(("gx", "gy"), None, None),) + (lines,) * 5,
        out_specs=(tiles, tiles, tiles, lines),
        check_vma=False,
    )
```

```python
import math

import jax
import jax.numpy as jnp
from jax import lax
from jax.experimental import pallas as pl
from jax.experimental.pallas import tpu as pltpu
from jax.sharding import PartitionSpec as P

SUBSTEPS = 8
GRAVITY = 9.81
DT = 0.02
SEWER_DT = 0.5
AREA = 256.0
HALF_DT = 0.5 * DT
ROOT_G = math.sqrt(GRAVITY)
HALF_G = 0.5 * GRAVITY
SLOPE = 0.5 * GRAVITY * DT
NGX = 8
NGY = 16
ROWS = 256
UNROLL = 16
F32 = jnp.float32
BF16 = jnp.bfloat16
I32 = jnp.int32
NT = (((1,), (1,)), ((), ()))


def thirds(x):
    a = x.astype(BF16)
    rest = x - a.astype(F32)
    b = rest.astype(BF16)
    c = (rest - b.astype(F32)).astype(BF16)
    return a, b, c


def lanes_at(row, idx):
    return jnp.take_along_axis(row, idx, axis=1, mode="promise_in_bounds")


def prim(h, hu, hv, om):
    hs = h + om
    y = lax.rsqrt(hs)
    inv = y * y
    u = hu * inv
    v = hv * inv
    c = (ROOT_G * hs) * y
    p = HALF_G * h * h
    return dict(
        h=h,
        hu=hu,
        hv=hv,
        uu=hu * u + p,
        uv=hu * v,
        vv=hv * v + p,
        sx=jnp.abs(u) + c,
        sy=jnp.abs(v) + c,
    )


def face_x(wall, l, r):
    a = jnp.maximum(l["sx"], r["sx"])
    return (
        wall * ((l["hu"] + r["hu"]) - a * (r["h"] - l["h"])),
        wall * ((l["uu"] + r["uu"]) - a * (r["hu"] - l["hu"])),
        wall * ((l["uv"] + r["uv"]) - a * (r["hv"] - l["hv"])),
    )


def face_y(wall, l, r):
    a = jnp.maximum(l["sy"], r["sy"])
    return (
        wall * ((l["hv"] + r["hv"]) - a * (r["h"] - l["h"])),
        wall * ((l["uv"] + r["uv"]) - a * (r["hu"] - l["hu"])),
        wall * ((l["vv"] + r["vv"]) - a * (r["hv"] - l["hv"])),
    )


def faces_x(rows, halo, halo_m, halo_z, mine_m):
    out = []
    for side in (0, 1):
        mine = prim(*rows[side], 1.0 - mine_m[side])
        other = prim(*halo[side], 1.0 - halo_m[side])
        wall = (HALF_DT * halo_m[side]) * mine_m[side]
        slope = (SLOPE * mine_m[side]) * (halo_z[side] * mine["h"])
        if side == 0:
            f = face_x(wall, other, mine)
            out.append((f[0], f[1] + slope, f[2]))
        else:
            f = face_x(wall, mine, other)
            out.append((-f[0], -f[1] - slope, -f[2]))
    return out


def faces_y(cols, halo, halo_m, halo_z, mine_m):
    out = []
    for side in (0, 1):
        mine = prim(*cols[side], 1.0 - mine_m[side])
        other = prim(*halo[side], 1.0 - halo_m[side])
        wall = (HALF_DT * halo_m[side]) * mine_m[side]
        slope = (SLOPE * mine_m[side]) * (halo_z[side] * mine["h"])
        if side == 0:
            f = face_y(wall, other, mine)
            out.append((f[0], f[1], f[2] + slope))
        else:
            f = face_y(wall, mine, other)
            out.append((-f[0], -f[1], -f[2] - slope))
    return out


def slab_of(ref, first, j):
    return ref.reshape(ref.shape[0] * 8, 128), pl.ds(first * 8 + j, ROWS, stride=8)


def edge_matrix(left, right):
    sub = lax.broadcasted_iota(I32, (8, ROWS), 0)
    top = jnp.where(sub == 0, jnp.broadcast_to(left, (8, ROWS)), 0.0)
    bottom = jnp.where(sub == 7, jnp.broadcast_to(right, (8, ROWS)), 0.0)
    return jnp.concatenate([top, jnp.zeros((112, ROWS), F32), bottom], axis=0).T


def edge_slabs(ref, first, terms):
    lane = lax.broadcasted_iota(I32, (ROWS, 128), 1)
    flat, low = slab_of(ref, first, 0)
    _, high = slab_of(ref, first, 7)
    return (
        flat[low, :] + jnp.where(lane == 0, terms, 0.0),
        flat[high, :] + jnp.where(lane == 127, terms, 0.0),
    )


def edge_columns(low, high):
    lane = lax.broadcasted_iota(I32, (ROWS, 128), 1)
    both = jnp.where(lane < 64, low, high).T
    return both[0:1], both[127:128]


def kernel(
    depth, mom_x, mom_y, bed, cells, strips_in, slots_in, sections_in, coefs_in, heads_in, conv_in,
    h2, hu2, hv2, edge_out, inflow_out, sewer_in,
    h0, hu0, hv0, z0, m0, level, h1, hu1, hv1,
    om_s, omr_s, wx_s, wy_s, sx_s, sy_s,
    strips, slots, sections, coefs, heads, conv,
    onehot, msg, mid, mid_t, got, slot_coef, slot_pipe, ring,
    row_snd1, row_rcv1, row_snd2, row_rcv2, col_snd1, col_rcv1, col_snd2, col_rcv2,
    in_sem, small_sem, p1_send, p1_recv, p2_send, p2_recv, halo_send, halo_recv,
):
    gx = lax.axis_index("gx")
    gy = lax.axis_index("gy")

    def gx_peer(i):
        return {"gx": lax.rem(gx + i, NGX)}

    def gy_peer(i):
        return {"gy": lax.rem(gy + i, NGY)}

    pairs = ((depth, h0), (bed, z0), (cells, m0), (mom_x, hu0), (mom_y, hv0))

    def load(f, j, part=None):
        src, dst = pairs[f]
        rows = pl.ds(0, ROWS) if part is None else pl.ds(part * (ROWS // 2), ROWS // 2)
        return pltpu.make_async_copy(
            src.at[rows, pl.ds(128 * j, 128)], dst.at[rows, j, :], in_sem.at[f, part or 0]
        )

    def loaded(f, part=None):
        rows = pl.ds(0, ROWS) if part is None else pl.ds(part * (ROWS // 2), ROWS // 2)
        whole = pairs[f][1].at[rows]
        return pltpu.make_async_copy(whole, whole, in_sem.at[f, part or 0])

    small = ((slots_in, slots), (sections_in, sections), (coefs_in, coefs), (heads_in, heads), (strips_in, strips), (conv_in, conv))

    def load_small(i):
        return pltpu.make_async_copy(small[i][0], small[i][1], small_sem.at[i])

    for i in range(6):
        load_small(i).start()
    for part in (0, 1):
        for f in (0, 1):
            for j in range(8):
                load(f, j, part).start()
    for f in (2, 3, 4):
        for j in range(8):
            load(f, j).start()

    barrier = pltpu.get_barrier_semaphore()
    for i in range(1, NGX):
        pl.semaphore_signal(barrier, inc=1, device_id=gx_peer(i), device_id_type=pl.DeviceIdType.MESH)
    for i in range(1, NGY):
        pl.semaphore_signal(barrier, inc=1, device_id=gy_peer(i), device_id_type=pl.DeviceIdType.MESH)

    lane = lax.broadcasted_iota(I32, (8, 128), 1)
    sub = lax.broadcasted_iota(I32, (8, 128), 0)
    zero_row = jnp.zeros((8, 128), F32)

    for i in range(4):
        load_small(i).wait()
    slot = slots[...]
    sec = sections[...]
    coef = coefs[...]
    tile_of = slot >> 4
    k_of = slot & 15
    pipe = jnp.zeros((16, 128), F32)
    for b in range(4):
        part = lanes_at(heads[:, pl.ds(128 * b, 128)], sec & 127)
        pipe = jnp.where((sec >> 7) == b, part, pipe)
    tile_iota = lax.broadcasted_iota(I32, (128, 128), 0)
    k_iota = lax.broadcasted_iota(I32, (16, 128), 0)
    left = []
    right = []
    for l in range(16):
        left.append((jnp.broadcast_to(tile_of[l : l + 1], (128, 128)) == tile_iota).astype(F32).astype(BF16))
        hit = jnp.broadcast_to(k_of[l : l + 1], (16, 128)) == k_iota
        both = jnp.concatenate(
            [
                jnp.where(hit, jnp.broadcast_to(coef[l : l + 1], (16, 128)), 0.0),
                jnp.where(hit, jnp.broadcast_to(pipe[l : l + 1], (16, 128)), 0.0),
            ],
            axis=0,
        )
        right.append(jnp.concatenate(thirds(both), axis=0))
    by_slot = lax.dot_general(
        jnp.concatenate(right, axis=1), jnp.concatenate(left, axis=1), NT, preferred_element_type=F32
    )
    by_slot = by_slot[0:32] + by_slot[32:64] + by_slot[64:96]

    load_small(4).wait()
    strip = strips[0]
    strip_row = strip >> 3
    strip_j = strip & 7
    lane2 = lax.broadcasted_iota(I32, (8, 256), 1)

    def level_rows(t, sums):
        for i in range(32):
            r = t * 32 + i
            lev = h0[r] + z0[r]
            level[r] = lev
            sums = jnp.where(lane2 == r, jnp.sum(lev, axis=1, keepdims=True), sums)
        return sums

    sums = jnp.zeros((8, 256), F32)
    for part in (0, 1):
        for f in (0, 1):
            loaded(f, part).wait()
        sums = lax.fori_loop(4 * part, 4 * part + 4, level_rows, sums)
    by_strip = jnp.zeros((16, 128), F32)
    for half in range(2):
        for j in range(8):
            row = jnp.broadcast_to(sums[j : j + 1, 128 * half : 128 * half + 128], (16, 128))
            part = lanes_at(row, strip_row & 127)
            by_strip = jnp.where((strip_j == j) & ((strip_row >> 7) == half), part, by_strip)
    packed = jnp.concatenate([by_slot, by_strip, jnp.zeros((80, 128), F32)], axis=0).T
    msg[...] = packed.reshape(NGX, NGY, 128)

    pl.semaphore_wait(barrier, NGX + NGY - 2)

    def phase1(i):
        return pltpu.make_async_remote_copy(
            src_ref=msg.at[lax.rem(gx + i, NGX)],
            dst_ref=mid.at[gx],
            send_sem=p1_send,
            recv_sem=p1_recv,
            device_id=gx_peer(i),
            device_id_type=pl.DeviceIdType.MESH,
        )

    for i in range(1, NGX):
        phase1(i).start()
    mid[gx] = msg[gx]

    loaded(2).wait()
    last_lane = lane == 127
    first_lane = lane == 0
    corner_r = (lane == 127) & (sub == 7)
    corner_l = (lane == 0) & (sub == 0)

    def from_right(x):
        a = pltpu.roll(x, 127, 1)
        return jnp.where(last_lane, pltpu.roll(a, 7, 0), a)

    def from_left(x):
        a = pltpu.roll(x, 1, 1)
        return jnp.where(first_lane, pltpu.roll(a, 1, 0), a)

    def static_rows(t, carry):
        for i in range(32):
            r = t * 32 + i
            m_prev, z_prev, z_prev2 = carry
            m = m0[r].astype(F32)
            z = z0[r]
            mr = from_right(m)
            om_s[r] = 1.0 - m
            omr_s[r] = 1.0 - mr
            wx_s[r] = (HALF_DT * m_prev) * m
            wy_s[r] = jnp.where(corner_r, 0.0, (HALF_DT * m) * mr)
            sx_s[r] = (SLOPE * m_prev) * (z - z_prev2)
            zr = jnp.where(corner_r, 0.0, from_right(z))
            zl = jnp.where(corner_l, 0.0, from_left(z))
            sy_s[r] = (SLOPE * m) * (zr - zl)
            carry = (m, z, z_prev)
        return carry

    m_end, _, z_end = lax.fori_loop(0, ROWS // 32, static_rows, (zero_row,) * 3)
    sx_s[ROWS] = (SLOPE * m_end) * (-z_end)

    for f in (3, 4):
        loaded(f).wait()

    def rows_of(r):
        return (h0[r], hu0[r], hv0[r], m0[r].astype(F32), z0[r])

    for side, r in ((0, 0), (1, ROWS - 1)):
        for f, value in enumerate(rows_of(r)):
            row_snd1[side, f] = value

    def halo_rows(snd, rcv, side, base):
        return pltpu.make_async_remote_copy(
            src_ref=snd.at[side],
            dst_ref=rcv.at[1 - side],
            send_sem=halo_send.at[base + side],
            recv_sem=halo_recv.at[base + side],
            device_id=gx_peer(NGX - 1 if side == 0 else 1),
            device_id_type=pl.DeviceIdType.MESH,
        )

    def halo_cols(snd, rcv, side, base):
        return pltpu.make_async_remote_copy(
            src_ref=snd.at[side],
            dst_ref=rcv.at[1 - side],
            send_sem=halo_send.at[base + 2 + side],
            recv_sem=halo_recv.at[base + 2 + side],
            device_id=gy_peer(NGY - 1 if side == 0 else 1),
            device_id_type=pl.DeviceIdType.MESH,
        )

    for side in (0, 1):
        halo_rows(row_snd1, row_rcv1, side, 0).start()

    cols1 = ([], [])
    for ref in (h0, hu0, hv0, m0, z0):
        flat, low = slab_of(ref, 0, 0)
        _, high = slab_of(ref, 0, 7)
        ends = edge_columns(flat[low, :].astype(F32), flat[high, :].astype(F32))
        for side in (0, 1):
            cols1[side].append(ends[side])
    for side in (0, 1):
        col_snd1[side] = jnp.concatenate(cols1[side] + [jnp.zeros((3, ROWS), F32)], axis=0)
        halo_cols(col_snd1, col_rcv1, side, 0).start()

    pltpu.make_async_copy(mid.at[pl.ds(0, NGX - 1)], mid.at[pl.ds(0, NGX - 1)], p1_recv).wait()
    mid_flat = mid.reshape(NGX * NGY, 128)
    for b in range(NGY):
        mid_t[b] = mid_flat[pl.ds(b, NGX, stride=NGY), :]

    def phase2(i):
        return pltpu.make_async_remote_copy(
            src_ref=mid_t.at[lax.rem(gy + i, NGY)],
            dst_ref=got.at[gy],
            send_sem=p2_send,
            recv_sem=p2_recv,
            device_id=gy_peer(i),
            device_id_type=pl.DeviceIdType.MESH,
        )

    for i in range(1, NGY):
        phase2(i).start()
    got[gy] = mid_t[gy]

    row_iota = lax.broadcasted_iota(I32, (ROWS, 128), 0)
    for k in range(16):
        hit = jnp.broadcast_to(strip_row[k : k + 1], (ROWS, 128)) == row_iota
        onehot[:, pl.ds(128 * k, 128)] = hit.astype(F32).astype(BF16)

    NAMES = ("h", "hu", "hv", "uu", "uv", "sx")

    def sweep(src, off, outs, drained):
        def ahead(r, i):
            h = src[0][r + off]
            if drained:
                less = slot_coef[r] * (level[r] - slot_pipe[r])
                h = h - less
                ring[3, i] = less
                ring[4, i] = h
            ring[0, i] = from_right(h)
            ring[1, i] = from_right(src[1][r + off])
            ring[2, i] = from_right(src[2][r + off])

        def one(r, i, carry):
            prev, part = carry
            h = ring[4, i] if drained else src[0][r + off]
            q = prim(h, src[1][r + off], src[2][r + off], om_s[r])
            right = prim(ring[0, i], ring[1, i], ring[2, i], omr_s[r])
            fx = face_x(wx_s[r], prev, q)
            outs[0][r] = part[0] - fx[0]
            outs[1][r] = part[1] - fx[1] - prev["h"] * sx_s[r]
            outs[2][r] = part[2] - fx[2]
            dy = [f - from_left(f) for f in face_y(wy_s[r], q, right)]
            part_h = q["h"] - dy[0] + fx[0]
            if drained:
                part_h = part_h - ring[3, i]
            part = (part_h, q["hu"] - dy[1] + fx[1], q["hv"] - dy[2] - q["h"] * sy_s[r] + fx[2])
            return {name: q[name] for name in NAMES}, part

        turns = ROWS // UNROLL
        for i in range(UNROLL):
            ahead(i, i)

        def some(t, carry):
            following = jnp.minimum(t + 1, turns - 1) * UNROLL
            for i in range(UNROLL):
                carry = one(t * UNROLL + i, i, carry)
                ahead(following + i, i)
            return carry

        start = ({name: zero_row for name in NAMES}, (zero_row,) * 3)
        prev, part = lax.fori_loop(0, turns, some, start)
        outs[0][ROWS] = part[0]
        outs[1][ROWS] = part[1] - prev["h"] * sx_s[ROWS]
        outs[2][ROWS] = part[2]

    sweep((h0, hu0, hv0), 0, (h1, hu1, hv1), False)

    for side in (0, 1):
        halo_rows(row_snd1, row_rcv1, side, 0).wait()
        halo_cols(col_snd1, col_rcv1, side, 0).wait()
    exists_x = (gx > 0, gx < NGX - 1)
    exists_y = (gy > 0, gy < NGY - 1)

    def keep(yes, x):
        return jnp.where(yes, x, 0.0)

    halo_x = [[keep(exists_x[side], row_rcv1[side, f]) for f in range(5)] for side in (0, 1)]
    mine_x = [[row_snd1[side, f] for f in range(5)] for side in (0, 1)]
    halo_y = [[keep(exists_y[side], col_rcv1[side, f : f + 1]) for f in range(5)] for side in (0, 1)]
    mine_y = [[col_snd1[side, f : f + 1] for f in range(5)] for side in (0, 1)]
    hmx = [halo_x[s][3] for s in (0, 1)]
    hzx = [halo_x[s][4] for s in (0, 1)]
    mmx = [mine_x[s][3] for s in (0, 1)]
    hmy = [halo_y[s][3] for s in (0, 1)]
    hzy = [halo_y[s][4] for s in (0, 1)]
    mmy = [mine_y[s][3] for s in (0, 1)]
    faces = faces_x([mine_x[s][:3] for s in (0, 1)], [halo_x[s][:3] for s in (0, 1)], hmx, hzx, mmx)
    for side, r in ((0, 1), (1, ROWS)):
        for f, ref in enumerate((h1, hu1, hv1)):
            ref[r] = ref[r] + faces[side][f]
    faces = faces_y([mine_y[s][:3] for s in (0, 1)], [halo_y[s][:3] for s in (0, 1)], hmy, hzy, mmy)
    cols2 = []
    for f, ref in enumerate((h1, hu1, hv1)):
        low, high = edge_slabs(ref, 1, edge_matrix(faces[0][f], faces[1][f]))
        flat, rows = slab_of(ref, 1, 0)
        flat[rows, :] = low
        flat, rows = slab_of(ref, 1, 7)
        flat[rows, :] = high
        cols2.append(edge_columns(low, high))

    pltpu.make_async_copy(got.at[pl.ds(0, NGY - 1)], got.at[pl.ds(0, NGY - 1)], p2_recv).wait()
    got_flat = got.reshape(NGX * NGY, 128)
    arrived = jnp.concatenate([got_flat[pl.ds(a, NGY, stride=NGX), :] for a in range(NGX)], axis=0).T
    level_sum = jnp.zeros((16, 128), F32)
    for k in range(16):
        row = jnp.broadcast_to(arrived[32 + k : 33 + k], (16, 128))
        level_sum = jnp.where(k_of == k, lanes_at(row, tile_of & 127), level_sum)
    rate = jnp.where(slot >= 0, coef * (level_sum - 128.0 * pipe), 0.0)
    block = lax.broadcasted_iota(I32, (8, 128), 0)
    for l in range(16):
        s_row = sec[l : l + 1]
        hit = (jnp.broadcast_to(s_row & 127, (128, 128)) == tile_iota).astype(F32).astype(BF16)
        value = jnp.where(
            jnp.broadcast_to(s_row >> 7, (8, 128)) == block, jnp.broadcast_to(rate[l : l + 1], (8, 128)), 0.0
        )
        got_l = lax.dot_general(jnp.concatenate(thirds(value), axis=0), hit, NT, preferred_element_type=F32)
        got_l = got_l[0:8] + got_l[8:16] + got_l[16:24]
        for b in range(4):
            inflow_out[l : l + 1, pl.ds(128 * b, 128)] = got_l[b : b + 1]

    load_small(5).wait()
    cv = conv[...]
    sec_lane = lax.broadcasted_iota(I32, (16, 512), 1)
    face_k = jnp.where(sec_lane == 511, cv, 0.5 * (cv + pltpu.roll(cv, 511, 1)))
    sewer_in[0] = heads[...]
    sewer_in[1] = face_k
    sewer_in[2] = jnp.where(sec_lane == 0, 0.0, pltpu.roll(face_k, 1, 1))
    right = []
    j_iota = lax.broadcasted_iota(I32, (8, 128), 0)
    for k in range(16):
        hit = jnp.broadcast_to(strip_j[k : k + 1], (8, 128)) == j_iota
        both = jnp.concatenate(
            [
                jnp.where(hit, jnp.broadcast_to(arrived[k : k + 1], (8, 128)), 0.0),
                jnp.where(hit, jnp.broadcast_to(arrived[16 + k : 17 + k], (8, 128)), 0.0),
            ],
            axis=0,
        )
        right.append(jnp.concatenate(thirds(both), axis=0))
    by_row = lax.dot_general(jnp.concatenate(right, axis=1), onehot[...], NT, preferred_element_type=F32)
    by_row = by_row[0:16] + by_row[16:32] + by_row[32:48]
    by_row = jnp.concatenate([DT * by_row[0:8], by_row[8:16]], axis=0)

    def drain_of(r):
        lanes = by_row[:, 0:128] if r < 128 else by_row[:, 128:256]
        at = r % 128
        c = jnp.broadcast_to(lanes[0:8, at : at + 1], (8, 128))
        p = jnp.broadcast_to(lanes[8:16, at : at + 1], (8, 128))
        return c * (level[r] - p)

    own_x = []
    for side, r in ((0, 0), (1, ROWS - 1)):
        own_x.append((h1[r + 1] - drain_of(r), hu1[r + 1], hv1[r + 1]))
        for f in range(3):
            row_snd2[side, f] = own_x[side][f]
    own_y = []
    for side, j in ((0, 0), (1, 7)):
        lev = mine_y[side][0] + mine_y[side][4]
        less = by_row[j : j + 1] * (lev - by_row[8 + j : 9 + j])
        own_y.append((cols2[0][side] - less, cols2[1][side], cols2[2][side]))
        col_snd2[side] = jnp.concatenate(list(own_y[side]) + [jnp.zeros((5, ROWS), F32)], axis=0)
    for side in (0, 1):
        halo_rows(row_snd2, row_rcv2, side, 4).start()
        halo_cols(col_snd2, col_rcv2, side, 4).start()

    for ref, first in ((slot_coef, 0), (slot_pipe, 8)):
        for half in range(2):
            for j in range(8):
                value = by_row[first + j : first + j + 1, 128 * half : 128 * half + 128]
                flat = ref.reshape(ROWS * 8, 128)
                flat[pl.ds(1024 * half + j, 128, stride=8), :] = jnp.broadcast_to(value, (128, 128)).T
    sweep((h1, hu1, hv1), 1, (h2, hu2, hv2), True)

    for side in (0, 1):
        halo_rows(row_snd2, row_rcv2, side, 4).wait()
        halo_cols(col_snd2, col_rcv2, side, 4).wait()
    halo_x = [[keep(exists_x[side], row_rcv2[side, f]) for f in range(3)] for side in (0, 1)]
    halo_y = [[keep(exists_y[side], col_rcv2[side, f : f + 1]) for f in range(3)] for side in (0, 1)]
    faces = faces_x(own_x, halo_x, hmx, hzx, mmx)
    for side, r in ((0, 1), (1, ROWS)):
        for f, ref in enumerate((h2, hu2, hv2)):
            ref[r] = ref[r] + faces[side][f]

    for side in (0, 1):
        rows = list(own_y[side]) + [mmy[side], hzy[side], hmy[side]] + halo_y[side]
        edge_out[side] = jnp.concatenate(rows + [jnp.zeros((7, ROWS), F32)], axis=0)

    pltpu.make_async_copy(msg.at[pl.ds(0, NGX - 1)], msg.at[pl.ds(0, NGX - 1)], p1_send).wait()
    pltpu.make_async_copy(mid_t.at[pl.ds(0, NGY - 1)], mid_t.at[pl.ds(0, NGY - 1)], p2_send).wait()


def finish(
    h2, hu2, hv2, edge, inflow, sewer_in,
    out_h, out_hu, out_hv, out_sewer,
    slabs, sewer,
    out_sem, sewer_sem,
):
    outs = ((h2, out_h), (hu2, out_hu), (hv2, out_hv))

    def store(f, j):
        src, dst = outs[f]
        if j in (0, 7):
            part = slabs.at[f, j // 7]
        else:
            part = src.at[pl.ds(1, ROWS), j, :]
        return pltpu.make_async_copy(part, dst.at[:, pl.ds(128 * j, 128)], out_sem.at[f])

    for f in range(3):
        for j in range(1, 7):
            store(f, j).start()

    def row(side, i):
        return edge[side, i : i + 1]

    own = [[row(s, i) for i in range(3)] for s in (0, 1)]
    halo = [[row(s, 6 + i) for i in range(3)] for s in (0, 1)]
    faces = faces_y(
        own, halo, [row(s, 5) for s in (0, 1)], [row(s, 4) for s in (0, 1)], [row(s, 3) for s in (0, 1)]
    )
    for f, (ref, _) in enumerate(outs):
        both = edge_slabs(ref, 1, edge_matrix(faces[0][f], faces[1][f]))
        for side in (0, 1):
            slabs[f, side] = both[side]

    share = inflow[...] / AREA
    head, face_k, above_k = sewer_in[0], sewer_in[1], sewer_in[2]
    sec_lane = lax.broadcasted_iota(I32, (16, 512), 1)
    for turn in range(SUBSTEPS):
        below = jnp.where(sec_lane == 511, 0.0, pltpu.roll(head, 511, 1))
        leaving = face_k * (head - below)
        entering = above_k * (pltpu.roll(head, 1, 1) - head)
        head = head + SEWER_DT * (entering - leaving + share)
    sewer[...] = head
    for f in range(3):
        for side in (0, 1):
            store(f, 7 * side).start()
    sewer_copy = pltpu.make_async_copy(sewer, out_sewer, sewer_sem)
    sewer_copy.start()
    for f, (src, _) in enumerate(outs):
        whole = src.at[pl.ds(1, ROWS)]
        pltpu.make_async_copy(whole, whole, out_sem.at[f]).wait()
    sewer_copy.wait()

def body(*args):
    args = [jnp.swapaxes(a, 1, 2) if a.ndim == 3 else a for a in args]
    rows, cols = args[0].shape
    grid = jax.ShapeDtypeStruct((rows, cols), F32)
    sewer = jax.ShapeDtypeStruct(args[9].shape, F32)
    args = [pltpu.with_memory_space_constraint(a, pltpu.HBM) for a in args]
    depth, mom_x, mom_y, bed, cells, strips, slots, sections, coefs, heads, conv = args
    hbm = pl.BlockSpec(memory_space=pltpu.HBM)
    vmem = pl.BlockSpec(memory_space=pltpu.VMEM)
    dma = pltpu.SemaphoreType.DMA
    padded = pltpu.VMEM((ROWS + 1, 8, 128), F32)
    h2, hu2, hv2, edge, inflow, sewer_in = pl.pallas_call(
        kernel,
        out_shape=(padded,) * 3
        + (pltpu.VMEM((2, 16, ROWS), F32), pltpu.VMEM((16, 512), F32), pltpu.VMEM((3, 16, 512), F32)),
        in_specs=[hbm] * 11,
        out_specs=(vmem,) * 6,
        scratch_shapes=[pltpu.VMEM((ROWS, 8, 128), F32)] * 4
        + [pltpu.VMEM((ROWS, 8, 128), I32), pltpu.VMEM((ROWS, 8, 128), F32)]
        + [pltpu.VMEM((ROWS + 1, 8, 128), F32)] * 9
        + [
            pltpu.VMEM((1, 16, 128), I32),
            pltpu.VMEM((16, 128), I32),
            pltpu.VMEM((16, 128), I32),
            pltpu.VMEM((16, 128), F32),
            pltpu.VMEM((16, 512), F32),
            pltpu.VMEM((16, 512), F32),
            pltpu.VMEM((ROWS, 2048), BF16),
            pltpu.VMEM((NGX, NGY, 128), F32),
            pltpu.VMEM((NGX, NGY, 128), F32),
            pltpu.VMEM((NGY, NGX, 128), F32),
            pltpu.VMEM((NGY, NGX, 128), F32),
            pltpu.VMEM((ROWS, 8, 128), F32),
            pltpu.VMEM((ROWS, 8, 128), F32),
            pltpu.VMEM((5, UNROLL, 8, 128), F32),
            pltpu.VMEM((2, 5, 8, 128), F32),
            pltpu.VMEM((2, 5, 8, 128), F32),
            pltpu.VMEM((2, 3, 8, 128), F32),
            pltpu.VMEM((2, 3, 8, 128), F32),
            pltpu.VMEM((2, 8, ROWS), F32),
            pltpu.VMEM((2, 8, ROWS), F32),
            pltpu.VMEM((2, 8, ROWS), F32),
            pltpu.VMEM((2, 8, ROWS), F32),
            dma((5, 2)),
            dma((6,)),
            dma,
            dma,
            dma,
            dma,
            dma((8,)),
            dma((8,)),
        ],
        compiler_params=pltpu.CompilerParams(
            collective_id=0, has_side_effects=True, vmem_limit_bytes=40 * 1024 * 1024
        ),
        name="street_flood",
    )(depth, mom_x, mom_y, bed, cells, strips, slots, sections, coefs, heads, conv)
    return pl.pallas_call(
        finish,
        out_shape=(grid, grid, grid, sewer),
        in_specs=[vmem] * 6,
        out_specs=(hbm,) * 4,
        scratch_shapes=[
            pltpu.VMEM((3, 2, ROWS, 128), F32),
            pltpu.VMEM((16, 512), F32),
            dma((3,)),
            dma,
        ],
        compiler_params=pltpu.CompilerParams(vmem_limit_bytes=16 * 1024 * 1024),
        name="flood_finish",
    )(h2, hu2, hv2, edge, inflow, sewer_in)


def solution(mesh):
    tiles = P("gx", "gy")
    lines = P(("gx", "gy"), None)
    return jax.shard_map(
        body,
        mesh=mesh,
        in_specs=(tiles,) * 5 + (P(("gx", "gy"), None, None),) + (lines,) * 5,
        out_specs=(tiles, tiles, tiles, lines),
        check_vma=False,
    )
```

```python
import math

import jax
import jax.numpy as jnp
from jax import lax
from jax.experimental import pallas as pl
from jax.experimental.pallas import tpu as pltpu
from jax.sharding import PartitionSpec as P

SUBSTEPS = 8
GRAVITY = 9.81
DT = 0.02
SEWER_DT = 0.5
AREA = 256.0
HALF_DT = 0.5 * DT
ROOT_G = math.sqrt(GRAVITY)
HALF_G = 0.5 * GRAVITY
SLOPE = 0.5 * GRAVITY * DT
NGX = 8
FAR_GY = (10, 9, 11, 6, 14, 8, 2, 5, 7, 13, 15, 1, 3, 4, 12)
FAR_GX = (4, 3, 5, 2, 6, 1, 7)
NGY = 16
ROWS = 256
UNROLL = 16
F32 = jnp.float32
BF16 = jnp.bfloat16
I32 = jnp.int32
NT = (((1,), (1,)), ((), ()))


def thirds(x):
    a = x.astype(BF16)
    rest = x - a.astype(F32)
    b = rest.astype(BF16)
    c = (rest - b.astype(F32)).astype(BF16)
    return a, b, c


def lanes_at(row, idx):
    return jnp.take_along_axis(row, idx, axis=1, mode="promise_in_bounds")


def prim(h, hu, hv, om):
    hs = h + om
    y = lax.rsqrt(hs)
    inv = y * y
    u = hu * inv
    v = hv * inv
    c = (ROOT_G * hs) * y
    p = HALF_G * h * h
    return dict(
        h=h,
        hu=hu,
        hv=hv,
        uu=hu * u + p,
        uv=hu * v,
        vv=hv * v + p,
        sx=jnp.abs(u) + c,
        sy=jnp.abs(v) + c,
    )


def face_x(wall, l, r):
    a = jnp.maximum(l["sx"], r["sx"])
    return (
        wall * ((l["hu"] + r["hu"]) - a * (r["h"] - l["h"])),
        wall * ((l["uu"] + r["uu"]) - a * (r["hu"] - l["hu"])),
        wall * ((l["uv"] + r["uv"]) - a * (r["hv"] - l["hv"])),
    )


def face_y(wall, l, r):
    a = jnp.maximum(l["sy"], r["sy"])
    return (
        wall * ((l["hv"] + r["hv"]) - a * (r["h"] - l["h"])),
        wall * ((l["uv"] + r["uv"]) - a * (r["hu"] - l["hu"])),
        wall * ((l["vv"] + r["vv"]) - a * (r["hv"] - l["hv"])),
    )


def faces_x(rows, halo, halo_m, halo_z, mine_m):
    out = []
    for side in (0, 1):
        mine = prim(*rows[side], 1.0 - mine_m[side])
        other = prim(*halo[side], 1.0 - halo_m[side])
        wall = (HALF_DT * halo_m[side]) * mine_m[side]
        slope = (SLOPE * mine_m[side]) * (halo_z[side] * mine["h"])
        if side == 0:
            f = face_x(wall, other, mine)
            out.append((f[0], f[1] + slope, f[2]))
        else:
            f = face_x(wall, mine, other)
            out.append((-f[0], -f[1] - slope, -f[2]))
    return out


def faces_y(cols, halo, halo_m, halo_z, mine_m):
    out = []
    for side in (0, 1):
        mine = prim(*cols[side], 1.0 - mine_m[side])
        other = prim(*halo[side], 1.0 - halo_m[side])
        wall = (HALF_DT * halo_m[side]) * mine_m[side]
        slope = (SLOPE * mine_m[side]) * (halo_z[side] * mine["h"])
        if side == 0:
            f = face_y(wall, other, mine)
            out.append((f[0], f[1], f[2] + slope))
        else:
            f = face_y(wall, mine, other)
            out.append((-f[0], -f[1], -f[2] - slope))
    return out


def slab_of(ref, first, j):
    return ref.reshape(ref.shape[0] * 8, 128), pl.ds(first * 8 + j, ROWS, stride=8)


def edge_matrix(left, right):
    sub = lax.broadcasted_iota(I32, (8, ROWS), 0)
    top = jnp.where(sub == 0, jnp.broadcast_to(left, (8, ROWS)), 0.0)
    bottom = jnp.where(sub == 7, jnp.broadcast_to(right, (8, ROWS)), 0.0)
    return jnp.concatenate([top, jnp.zeros((112, ROWS), F32), bottom], axis=0).T


def edge_slabs(ref, first, terms):
    lane = lax.broadcasted_iota(I32, (ROWS, 128), 1)
    flat, low = slab_of(ref, first, 0)
    _, high = slab_of(ref, first, 7)
    return (
        flat[low, :] + jnp.where(lane == 0, terms, 0.0),
        flat[high, :] + jnp.where(lane == 127, terms, 0.0),
    )


def edge_columns(low, high):
    lane = lax.broadcasted_iota(I32, (ROWS, 128), 1)
    both = jnp.where(lane < 64, low, high).T
    return both[0:1], both[127:128]


def kernel(
    depth, mom_x, mom_y, bed, cells, strips_in, slots_in, sections_in, coefs_in, heads_in, conv_in,
    h2, hu2, hv2, edge_out, inflow_out, sewer_in,
    h0, hu0, hv0, z0, m0, level, h1, hu1, hv1,
    om_s, omr_s, wx_s, wy_s, sx_s, sy_s,
    strips, slots, sections, coefs, heads, conv,
    onehot, msg, mid, mid_t, got, slot_coef, slot_pipe, ring,
    row_snd1, row_rcv1, row_snd2, row_rcv2, col_snd1, col_rcv1, col_snd2, col_rcv2,
    in_sem, small_sem, p1_send, p1_recv, p2_send, p2_recv, halo_send, halo_recv,
):
    gx = lax.axis_index("gx")
    gy = lax.axis_index("gy")

    def gx_peer(i):
        return {"gx": lax.rem(gx + i, NGX)}

    def gy_peer(i):
        return {"gy": lax.rem(gy + i, NGY)}

    barrier = pltpu.get_barrier_semaphore()
    for i in FAR_GX:
        pl.semaphore_signal(barrier, inc=1, device_id=gx_peer(i), device_id_type=pl.DeviceIdType.MESH)
    for i in FAR_GY:
        pl.semaphore_signal(barrier, inc=1, device_id=gy_peer(i), device_id_type=pl.DeviceIdType.MESH)

    pairs = ((depth, h0), (bed, z0), (cells, m0), (mom_x, hu0), (mom_y, hv0))

    def load(f, j, part=None):
        src, dst = pairs[f]
        rows = pl.ds(0, ROWS) if part is None else pl.ds(part * (ROWS // 2), ROWS // 2)
        return pltpu.make_async_copy(
            src.at[rows, pl.ds(128 * j, 128)], dst.at[rows, j, :], in_sem.at[f, part or 0]
        )

    def loaded(f, part=None):
        rows = pl.ds(0, ROWS) if part is None else pl.ds(part * (ROWS // 2), ROWS // 2)
        whole = pairs[f][1].at[rows]
        return pltpu.make_async_copy(whole, whole, in_sem.at[f, part or 0])

    small = ((slots_in, slots), (sections_in, sections), (coefs_in, coefs), (heads_in, heads), (strips_in, strips), (conv_in, conv))

    def load_small(i):
        return pltpu.make_async_copy(small[i][0], small[i][1], small_sem.at[i])

    for i in range(6):
        load_small(i).start()
    for part in (0, 1):
        for f in (0, 1):
            for j in range(8):
                load(f, j, part).start()
    for f in (2, 3, 4):
        for j in range(8):
            load(f, j).start()

    lane = lax.broadcasted_iota(I32, (8, 128), 1)
    sub = lax.broadcasted_iota(I32, (8, 128), 0)
    zero_row = jnp.zeros((8, 128), F32)

    for i in range(4):
        load_small(i).wait()
    slot = slots[...]
    sec = sections[...]
    coef = coefs[...]
    tile_of = slot >> 4
    k_of = slot & 15
    pipe = jnp.zeros((16, 128), F32)
    for b in range(4):
        part = lanes_at(heads[:, pl.ds(128 * b, 128)], sec & 127)
        pipe = jnp.where((sec >> 7) == b, part, pipe)
    tile_iota = lax.broadcasted_iota(I32, (128, 128), 0)
    k_iota = lax.broadcasted_iota(I32, (16, 128), 0)
    left = []
    right = []
    for l in range(16):
        left.append((jnp.broadcast_to(tile_of[l : l + 1], (128, 128)) == tile_iota).astype(F32).astype(BF16))
        hit = jnp.broadcast_to(k_of[l : l + 1], (16, 128)) == k_iota
        both = jnp.concatenate(
            [
                jnp.where(hit, jnp.broadcast_to(coef[l : l + 1], (16, 128)), 0.0),
                jnp.where(hit, jnp.broadcast_to(pipe[l : l + 1], (16, 128)), 0.0),
            ],
            axis=0,
        )
        right.append(jnp.concatenate(thirds(both), axis=0))
    by_slot = lax.dot_general(
        jnp.concatenate(right, axis=1), jnp.concatenate(left, axis=1), NT, preferred_element_type=F32
    )
    by_slot = by_slot[0:32] + by_slot[32:64] + by_slot[64:96]

    load_small(4).wait()
    strip = strips[0]
    strip_row = strip >> 3
    strip_j = strip & 7
    lane2 = lax.broadcasted_iota(I32, (8, 256), 1)

    def level_rows(t, sums):
        for i in range(32):
            r = t * 32 + i
            lev = h0[r] + z0[r]
            level[r] = lev
            sums = jnp.where(lane2 == r, jnp.sum(lev, axis=1, keepdims=True), sums)
        return sums

    sums = jnp.zeros((8, 256), F32)
    for part in (0, 1):
        for f in (0, 1):
            loaded(f, part).wait()
        sums = lax.fori_loop(4 * part, 4 * part + 4, level_rows, sums)
    by_strip = jnp.zeros((16, 128), F32)
    for half in range(2):
        for j in range(8):
            row = jnp.broadcast_to(sums[j : j + 1, 128 * half : 128 * half + 128], (16, 128))
            part = lanes_at(row, strip_row & 127)
            by_strip = jnp.where((strip_j == j) & ((strip_row >> 7) == half), part, by_strip)
    packed = jnp.concatenate([by_slot, by_strip, jnp.zeros((80, 128), F32)], axis=0).T
    msg[...] = packed.reshape(NGX, NGY, 128)

    pl.semaphore_wait(barrier, NGX + NGY - 2)

    def phase1(i):
        return pltpu.make_async_remote_copy(
            src_ref=msg.at[lax.rem(gx + i, NGX)],
            dst_ref=mid.at[gx],
            send_sem=p1_send,
            recv_sem=p1_recv,
            device_id=gx_peer(i),
            device_id_type=pl.DeviceIdType.MESH,
        )

    for i in FAR_GX:
        phase1(i).start()
    mid[gx] = msg[gx]

    loaded(2).wait()
    last_lane = lane == 127
    first_lane = lane == 0
    corner_r = (lane == 127) & (sub == 7)
    corner_l = (lane == 0) & (sub == 0)

    def from_right(x):
        a = pltpu.roll(x, 127, 1)
        return jnp.where(last_lane, pltpu.roll(a, 7, 0), a)

    def from_left(x):
        a = pltpu.roll(x, 1, 1)
        return jnp.where(first_lane, pltpu.roll(a, 1, 0), a)

    def static_rows(t, carry):
        for i in range(32):
            r = t * 32 + i
            m_prev, z_prev, z_prev2 = carry
            m = m0[r].astype(F32)
            z = z0[r]
            mr = from_right(m)
            om_s[r] = 1.0 - m
            omr_s[r] = 1.0 - mr
            wx_s[r] = (HALF_DT * m_prev) * m
            wy_s[r] = jnp.where(corner_r, 0.0, (HALF_DT * m) * mr)
            sx_s[r] = (SLOPE * m_prev) * (z - z_prev2)
            zr = jnp.where(corner_r, 0.0, from_right(z))
            zl = jnp.where(corner_l, 0.0, from_left(z))
            sy_s[r] = (SLOPE * m) * (zr - zl)
            carry = (m, z, z_prev)
        return carry

    m_end, _, z_end = lax.fori_loop(0, ROWS // 32, static_rows, (zero_row,) * 3)
    sx_s[ROWS] = (SLOPE * m_end) * (-z_end)

    for f in (3, 4):
        loaded(f).wait()

    def rows_of(r):
        return (h0[r], hu0[r], hv0[r], m0[r].astype(F32), z0[r])

    for side, r in ((0, 0), (1, ROWS - 1)):
        for f, value in enumerate(rows_of(r)):
            row_snd1[side, f] = value

    def halo_rows(snd, rcv, side, base):
        return pltpu.make_async_remote_copy(
            src_ref=snd.at[side],
            dst_ref=rcv.at[1 - side],
            send_sem=halo_send.at[base + side],
            recv_sem=halo_recv.at[base + side],
            device_id=gx_peer(NGX - 1 if side == 0 else 1),
            device_id_type=pl.DeviceIdType.MESH,
        )

    def halo_cols(snd, rcv, side, base):
        return pltpu.make_async_remote_copy(
            src_ref=snd.at[side],
            dst_ref=rcv.at[1 - side],
            send_sem=halo_send.at[base + 2 + side],
            recv_sem=halo_recv.at[base + 2 + side],
            device_id=gy_peer(NGY - 1 if side == 0 else 1),
            device_id_type=pl.DeviceIdType.MESH,
        )

    for side in (0, 1):
        halo_rows(row_snd1, row_rcv1, side, 0).start()

    cols1 = ([], [])
    for ref in (h0, hu0, hv0, m0, z0):
        flat, low = slab_of(ref, 0, 0)
        _, high = slab_of(ref, 0, 7)
        ends = edge_columns(flat[low, :].astype(F32), flat[high, :].astype(F32))
        for side in (0, 1):
            cols1[side].append(ends[side])
    for side in (0, 1):
        col_snd1[side] = jnp.concatenate(cols1[side] + [jnp.zeros((3, ROWS), F32)], axis=0)
        halo_cols(col_snd1, col_rcv1, side, 0).start()

    row_iota = lax.broadcasted_iota(I32, (ROWS, 128), 0)
    for k in range(16):
        hit = jnp.broadcast_to(strip_row[k : k + 1], (ROWS, 128)) == row_iota
        onehot[:, pl.ds(128 * k, 128)] = hit.astype(F32).astype(BF16)

    NAMES = ("h", "hu", "hv", "uu", "uv", "sx")

    def phase2(i):
        return pltpu.make_async_remote_copy(
            src_ref=mid_t.at[lax.rem(gy + i, NGY)],
            dst_ref=got.at[gy],
            send_sem=p2_send,
            recv_sem=p2_recv,
            device_id=gy_peer(i),
            device_id_type=pl.DeviceIdType.MESH,
        )

    def forward():
        pltpu.make_async_copy(mid.at[pl.ds(0, NGX - 1)], mid.at[pl.ds(0, NGX - 1)], p1_recv).wait()
        mid_flat = mid.reshape(NGX * NGY, 128)
        for b in range(NGY):
            mid_t[b] = mid_flat[pl.ds(b, NGX, stride=NGY), :]
        for i in FAR_GY:
            phase2(i).start()
        got[gy] = mid_t[gy]

    def sweep(src, off, outs, drained, pause, between):
        def ahead(r, i):
            h = src[0][r + off]
            if drained:
                less = slot_coef[r] * (level[r] - slot_pipe[r])
                h = h - less
                ring[3, i] = less
                ring[4, i] = h
            ring[0, i] = from_right(h)
            ring[1, i] = from_right(src[1][r + off])
            ring[2, i] = from_right(src[2][r + off])

        def one(r, i, carry):
            prev, part = carry
            h = ring[4, i] if drained else src[0][r + off]
            q = prim(h, src[1][r + off], src[2][r + off], om_s[r])
            right = prim(ring[0, i], ring[1, i], ring[2, i], omr_s[r])
            fx = face_x(wx_s[r], prev, q)
            outs[0][r] = part[0] - fx[0]
            outs[1][r] = part[1] - fx[1] - prev["h"] * sx_s[r]
            outs[2][r] = part[2] - fx[2]
            dy = [f - from_left(f) for f in face_y(wy_s[r], q, right)]
            part_h = q["h"] - dy[0] + fx[0]
            if drained:
                part_h = part_h - ring[3, i]
            part = (part_h, q["hu"] - dy[1] + fx[1], q["hv"] - dy[2] - q["h"] * sy_s[r] + fx[2])
            return {name: q[name] for name in NAMES}, part

        turns = ROWS // UNROLL
        for i in range(UNROLL):
            ahead(i, i)

        def some(t, carry):
            following = jnp.minimum(t + 1, turns - 1) * UNROLL
            for i in range(UNROLL):
                carry = one(t * UNROLL + i, i, carry)
                ahead(following + i, i)
            return carry

        start = ({name: zero_row for name in NAMES}, (zero_row,) * 3)
        carry = lax.fori_loop(0, pause, some, start) if pause else start
        between()
        prev, part = lax.fori_loop(pause, turns, some, carry)
        outs[0][ROWS] = part[0]
        outs[1][ROWS] = part[1] - prev["h"] * sx_s[ROWS]
        outs[2][ROWS] = part[2]

    sweep((h0, hu0, hv0), 0, (h1, hu1, hv1), False, 6, forward)

    for side in (0, 1):
        halo_rows(row_snd1, row_rcv1, side, 0).wait()
        halo_cols(col_snd1, col_rcv1, side, 0).wait()
    exists_x = (gx > 0, gx < NGX - 1)
    exists_y = (gy > 0, gy < NGY - 1)

    def keep(yes, x):
        return jnp.where(yes, x, 0.0)

    halo_x = [[keep(exists_x[side], row_rcv1[side, f]) for f in range(5)] for side in (0, 1)]
    mine_x = [[row_snd1[side, f] for f in range(5)] for side in (0, 1)]
    halo_y = [[keep(exists_y[side], col_rcv1[side, f : f + 1]) for f in range(5)] for side in (0, 1)]
    mine_y = [[col_snd1[side, f : f + 1] for f in range(5)] for side in (0, 1)]
    hmx = [halo_x[s][3] for s in (0, 1)]
    hzx = [halo_x[s][4] for s in (0, 1)]
    mmx = [mine_x[s][3] for s in (0, 1)]
    hmy = [halo_y[s][3] for s in (0, 1)]
    hzy = [halo_y[s][4] for s in (0, 1)]
    mmy = [mine_y[s][3] for s in (0, 1)]
    faces = faces_x([mine_x[s][:3] for s in (0, 1)], [halo_x[s][:3] for s in (0, 1)], hmx, hzx, mmx)
    for side, r in ((0, 1), (1, ROWS)):
        for f, ref in enumerate((h1, hu1, hv1)):
            ref[r] = ref[r] + faces[side][f]
    faces = faces_y([mine_y[s][:3] for s in (0, 1)], [halo_y[s][:3] for s in (0, 1)], hmy, hzy, mmy)
    cols2 = []
    for f, ref in enumerate((h1, hu1, hv1)):
        low, high = edge_slabs(ref, 1, edge_matrix(faces[0][f], faces[1][f]))
        flat, rows = slab_of(ref, 1, 0)
        flat[rows, :] = low
        flat, rows = slab_of(ref, 1, 7)
        flat[rows, :] = high
        cols2.append(edge_columns(low, high))

    pltpu.make_async_copy(got.at[pl.ds(0, NGY - 1)], got.at[pl.ds(0, NGY - 1)], p2_recv).wait()
    got_flat = got.reshape(NGX * NGY, 128)
    arrived = jnp.concatenate([got_flat[pl.ds(a, NGY, stride=NGX), :] for a in range(NGX)], axis=0).T
    level_sum = jnp.zeros((16, 128), F32)
    for k in range(16):
        row = jnp.broadcast_to(arrived[32 + k : 33 + k], (16, 128))
        level_sum = jnp.where(k_of == k, lanes_at(row, tile_of & 127), level_sum)
    rate = jnp.where(slot >= 0, coef * (level_sum - 128.0 * pipe), 0.0)
    block = lax.broadcasted_iota(I32, (8, 128), 0)
    for l in range(16):
        s_row = sec[l : l + 1]
        hit = (jnp.broadcast_to(s_row & 127, (128, 128)) == tile_iota).astype(F32).astype(BF16)
        value = jnp.where(
            jnp.broadcast_to(s_row >> 7, (8, 128)) == block, jnp.broadcast_to(rate[l : l + 1], (8, 128)), 0.0
        )
        got_l = lax.dot_general(jnp.concatenate(thirds(value), axis=0), hit, NT, preferred_element_type=F32)
        got_l = got_l[0:8] + got_l[8:16] + got_l[16:24]
        for b in range(4):
            inflow_out[l : l + 1, pl.ds(128 * b, 128)] = got_l[b : b + 1]

    load_small(5).wait()
    cv = conv[...]
    sec_lane = lax.broadcasted_iota(I32, (16, 512), 1)
    face_k = jnp.where(sec_lane == 511, cv, 0.5 * (cv + pltpu.roll(cv, 511, 1)))
    sewer_in[0] = heads[...]
    sewer_in[1] = face_k
    sewer_in[2] = jnp.where(sec_lane == 0, 0.0, pltpu.roll(face_k, 1, 1))
    right = []
    j_iota = lax.broadcasted_iota(I32, (8, 128), 0)
    for k in range(16):
        hit = jnp.broadcast_to(strip_j[k : k + 1], (8, 128)) == j_iota
        both = jnp.concatenate(
            [
                jnp.where(hit, jnp.broadcast_to(arrived[k : k + 1], (8, 128)), 0.0),
                jnp.where(hit, jnp.broadcast_to(arrived[16 + k : 17 + k], (8, 128)), 0.0),
            ],
            axis=0,
        )
        right.append(jnp.concatenate(thirds(both), axis=0))
    by_row = lax.dot_general(jnp.concatenate(right, axis=1), onehot[...], NT, preferred_element_type=F32)
    by_row = by_row[0:16] + by_row[16:32] + by_row[32:48]
    by_row = jnp.concatenate([DT * by_row[0:8], by_row[8:16]], axis=0)

    def drain_of(r):
        lanes = by_row[:, 0:128] if r < 128 else by_row[:, 128:256]
        at = r % 128
        c = jnp.broadcast_to(lanes[0:8, at : at + 1], (8, 128))
        p = jnp.broadcast_to(lanes[8:16, at : at + 1], (8, 128))
        return c * (level[r] - p)

    own_x = []
    for side, r in ((0, 0), (1, ROWS - 1)):
        own_x.append((h1[r + 1] - drain_of(r), hu1[r + 1], hv1[r + 1]))
        for f in range(3):
            row_snd2[side, f] = own_x[side][f]
    own_y = []
    for side, j in ((0, 0), (1, 7)):
        lev = mine_y[side][0] + mine_y[side][4]
        less = by_row[j : j + 1] * (lev - by_row[8 + j : 9 + j])
        own_y.append((cols2[0][side] - less, cols2[1][side], cols2[2][side]))
        col_snd2[side] = jnp.concatenate(list(own_y[side]) + [jnp.zeros((5, ROWS), F32)], axis=0)
    for side in (0, 1):
        halo_rows(row_snd2, row_rcv2, side, 4).start()
        halo_cols(col_snd2, col_rcv2, side, 4).start()

    for ref, first in ((slot_coef, 0), (slot_pipe, 8)):
        for half in range(2):
            for j in range(8):
                value = by_row[first + j : first + j + 1, 128 * half : 128 * half + 128]
                flat = ref.reshape(ROWS * 8, 128)
                flat[pl.ds(1024 * half + j, 128, stride=8), :] = jnp.broadcast_to(value, (128, 128)).T
    sweep((h1, hu1, hv1), 1, (h2, hu2, hv2), True, 0, lambda: None)

    for side in (0, 1):
        halo_rows(row_snd2, row_rcv2, side, 4).wait()
        halo_cols(col_snd2, col_rcv2, side, 4).wait()
    halo_x = [[keep(exists_x[side], row_rcv2[side, f]) for f in range(3)] for side in (0, 1)]
    halo_y = [[keep(exists_y[side], col_rcv2[side, f : f + 1]) for f in range(3)] for side in (0, 1)]
    faces = faces_x(own_x, halo_x, hmx, hzx, mmx)
    for side, r in ((0, 1), (1, ROWS)):
        for f, ref in enumerate((h2, hu2, hv2)):
            ref[r] = ref[r] + faces[side][f]

    for side in (0, 1):
        rows = list(own_y[side]) + [mmy[side], hzy[side], hmy[side]] + halo_y[side]
        edge_out[side] = jnp.concatenate(rows + [jnp.zeros((7, ROWS), F32)], axis=0)

    pltpu.make_async_copy(msg.at[pl.ds(0, NGX - 1)], msg.at[pl.ds(0, NGX - 1)], p1_send).wait()
    pltpu.make_async_copy(mid_t.at[pl.ds(0, NGY - 1)], mid_t.at[pl.ds(0, NGY - 1)], p2_send).wait()


def finish(
    h2, hu2, hv2, edge, inflow, sewer_in,
    out_h, out_hu, out_hv, out_sewer,
    slabs, sewer,
    out_sem, sewer_sem,
):
    outs = ((h2, out_h), (hu2, out_hu), (hv2, out_hv))

    def store(f, j):
        src, dst = outs[f]
        if j in (0, 7):
            part = slabs.at[f, j // 7]
        else:
            part = src.at[pl.ds(1, ROWS), j, :]
        return pltpu.make_async_copy(part, dst.at[:, pl.ds(128 * j, 128)], out_sem.at[f])

    for f in range(3):
        for j in range(1, 7):
            store(f, j).start()

    def row(side, i):
        return edge[side, i : i + 1]

    own = [[row(s, i) for i in range(3)] for s in (0, 1)]
    halo = [[row(s, 6 + i) for i in range(3)] for s in (0, 1)]
    faces = faces_y(
        own, halo, [row(s, 5) for s in (0, 1)], [row(s, 4) for s in (0, 1)], [row(s, 3) for s in (0, 1)]
    )
    for f, (ref, _) in enumerate(outs):
        both = edge_slabs(ref, 1, edge_matrix(faces[0][f], faces[1][f]))
        for side in (0, 1):
            slabs[f, side] = both[side]

    share = inflow[...] / AREA
    head, face_k, above_k = sewer_in[0], sewer_in[1], sewer_in[2]
    sec_lane = lax.broadcasted_iota(I32, (16, 512), 1)
    for turn in range(SUBSTEPS):
        below = jnp.where(sec_lane == 511, 0.0, pltpu.roll(head, 511, 1))
        leaving = face_k * (head - below)
        entering = above_k * (pltpu.roll(head, 1, 1) - head)
        head = head + SEWER_DT * (entering - leaving + share)
    sewer[...] = head
    for f in range(3):
        for side in (0, 1):
            store(f, 7 * side).start()
    sewer_copy = pltpu.make_async_copy(sewer, out_sewer, sewer_sem)
    sewer_copy.start()
    for f, (src, _) in enumerate(outs):
        whole = src.at[pl.ds(1, ROWS)]
        pltpu.make_async_copy(whole, whole, out_sem.at[f]).wait()
    sewer_copy.wait()

def body(*args):
    args = [jnp.swapaxes(a, 1, 2) if a.ndim == 3 else a for a in args]
    rows, cols = args[0].shape
    grid = jax.ShapeDtypeStruct((rows, cols), F32)
    sewer = jax.ShapeDtypeStruct(args[9].shape, F32)
    args = [pltpu.with_memory_space_constraint(a, pltpu.HBM) for a in args]
    depth, mom_x, mom_y, bed, cells, strips, slots, sections, coefs, heads, conv = args
    hbm = pl.BlockSpec(memory_space=pltpu.HBM)
    vmem = pl.BlockSpec(memory_space=pltpu.VMEM)
    dma = pltpu.SemaphoreType.DMA
    padded = pltpu.VMEM((ROWS + 1, 8, 128), F32)
    h2, hu2, hv2, edge, inflow, sewer_in = pl.pallas_call(
        kernel,
        out_shape=(padded,) * 3
        + (pltpu.VMEM((2, 16, ROWS), F32), pltpu.VMEM((16, 512), F32), pltpu.VMEM((3, 16, 512), F32)),
        in_specs=[hbm] * 11,
        out_specs=(vmem,) * 6,
        scratch_shapes=[pltpu.VMEM((ROWS, 8, 128), F32)] * 4
        + [pltpu.VMEM((ROWS, 8, 128), I32), pltpu.VMEM((ROWS, 8, 128), F32)]
        + [pltpu.VMEM((ROWS + 1, 8, 128), F32)] * 9
        + [
            pltpu.VMEM((1, 16, 128), I32),
            pltpu.VMEM((16, 128), I32),
            pltpu.VMEM((16, 128), I32),
            pltpu.VMEM((16, 128), F32),
            pltpu.VMEM((16, 512), F32),
            pltpu.VMEM((16, 512), F32),
            pltpu.VMEM((ROWS, 2048), BF16),
            pltpu.VMEM((NGX, NGY, 128), F32),
            pltpu.VMEM((NGX, NGY, 128), F32),
            pltpu.VMEM((NGY, NGX, 128), F32),
            pltpu.VMEM((NGY, NGX, 128), F32),
            pltpu.VMEM((ROWS, 8, 128), F32),
            pltpu.VMEM((ROWS, 8, 128), F32),
            pltpu.VMEM((5, UNROLL, 8, 128), F32),
            pltpu.VMEM((2, 5, 8, 128), F32),
            pltpu.VMEM((2, 5, 8, 128), F32),
            pltpu.VMEM((2, 3, 8, 128), F32),
            pltpu.VMEM((2, 3, 8, 128), F32),
            pltpu.VMEM((2, 8, ROWS), F32),
            pltpu.VMEM((2, 8, ROWS), F32),
            pltpu.VMEM((2, 8, ROWS), F32),
            pltpu.VMEM((2, 8, ROWS), F32),
            dma((5, 2)),
            dma((6,)),
            dma,
            dma,
            dma,
            dma,
            dma((8,)),
            dma((8,)),
        ],
        compiler_params=pltpu.CompilerParams(
            collective_id=0, has_side_effects=True, vmem_limit_bytes=40 * 1024 * 1024
        ),
        name="street_flood",
    )(depth, mom_x, mom_y, bed, cells, strips, slots, sections, coefs, heads, conv)
    return pl.pallas_call(
        finish,
        out_shape=(grid, grid, grid, sewer),
        in_specs=[vmem] * 6,
        out_specs=(hbm,) * 4,
        scratch_shapes=[
            pltpu.VMEM((3, 2, ROWS, 128), F32),
            pltpu.VMEM((16, 512), F32),
            dma((3,)),
            dma,
        ],
        compiler_params=pltpu.CompilerParams(vmem_limit_bytes=16 * 1024 * 1024),
        name="flood_finish",
    )(h2, hu2, hv2, edge, inflow, sewer_in)


def solution(mesh):
    tiles = P("gx", "gy")
    lines = P(("gx", "gy"), None)
    return jax.shard_map(
        body,
        mesh=mesh,
        in_specs=(tiles,) * 5 + (P(("gx", "gy"), None, None),) + (lines,) * 5,
        out_specs=(tiles, tiles, tiles, lines),
        check_vma=False,
    )
```

```python
import math

import jax
import jax.numpy as jnp
from jax import lax
from jax.experimental import pallas as pl
from jax.experimental.pallas import tpu as pltpu
from jax.sharding import PartitionSpec as P

SUBSTEPS = 8
GRAVITY = 9.81
DT = 0.02
SEWER_DT = 0.5
AREA = 256.0
HALF_DT = 0.5 * DT
ROOT_G = math.sqrt(GRAVITY)
HALF_G = 0.5 * GRAVITY
SLOPE = 0.5 * GRAVITY * DT
NGX = 8
FAR_GY = (10, 9, 11, 6, 14, 8, 2, 5, 7, 13, 15, 1, 3, 4, 12)
FAR_GX = (4, 3, 5, 2, 6, 1, 7)
NGY = 16
ROWS = 256
UNROLL = 16
F32 = jnp.float32
BF16 = jnp.bfloat16
I32 = jnp.int32
NT = (((1,), (1,)), ((), ()))


def thirds(x):
    a = x.astype(BF16)
    rest = x - a.astype(F32)
    b = rest.astype(BF16)
    c = (rest - b.astype(F32)).astype(BF16)
    return a, b, c


def lanes_at(row, idx):
    return jnp.take_along_axis(row, idx, axis=1, mode="promise_in_bounds")


def prim(h, hu, hv, om):
    hs = h + om
    y = lax.rsqrt(hs)
    inv = y * y
    u = hu * inv
    v = hv * inv
    c = (ROOT_G * hs) * y
    p = HALF_G * h * h
    return dict(
        h=h,
        hu=hu,
        hv=hv,
        uu=hu * u + p,
        uv=hu * v,
        vv=hv * v + p,
        sx=jnp.abs(u) + c,
        sy=jnp.abs(v) + c,
    )


def face_x(wall, l, r):
    a = jnp.maximum(l["sx"], r["sx"])
    return (
        wall * ((l["hu"] + r["hu"]) - a * (r["h"] - l["h"])),
        wall * ((l["uu"] + r["uu"]) - a * (r["hu"] - l["hu"])),
        wall * ((l["uv"] + r["uv"]) - a * (r["hv"] - l["hv"])),
    )


def face_y(wall, l, r):
    a = jnp.maximum(l["sy"], r["sy"])
    return (
        wall * ((l["hv"] + r["hv"]) - a * (r["h"] - l["h"])),
        wall * ((l["uv"] + r["uv"]) - a * (r["hu"] - l["hu"])),
        wall * ((l["vv"] + r["vv"]) - a * (r["hv"] - l["hv"])),
    )


def faces_x(rows, halo, halo_m, halo_z, mine_m):
    out = []
    for side in (0, 1):
        mine = prim(*rows[side], 1.0 - mine_m[side])
        other = prim(*halo[side], 1.0 - halo_m[side])
        wall = (HALF_DT * halo_m[side]) * mine_m[side]
        slope = (SLOPE * mine_m[side]) * (halo_z[side] * mine["h"])
        if side == 0:
            f = face_x(wall, other, mine)
            out.append((f[0], f[1] + slope, f[2]))
        else:
            f = face_x(wall, mine, other)
            out.append((-f[0], -f[1] - slope, -f[2]))
    return out


def faces_y(cols, halo, halo_m, halo_z, mine_m):
    out = []
    for side in (0, 1):
        mine = prim(*cols[side], 1.0 - mine_m[side])
        other = prim(*halo[side], 1.0 - halo_m[side])
        wall = (HALF_DT * halo_m[side]) * mine_m[side]
        slope = (SLOPE * mine_m[side]) * (halo_z[side] * mine["h"])
        if side == 0:
            f = face_y(wall, other, mine)
            out.append((f[0], f[1], f[2] + slope))
        else:
            f = face_y(wall, mine, other)
            out.append((-f[0], -f[1], -f[2] - slope))
    return out


def slab_of(ref, first, j):
    return ref.reshape(ref.shape[0] * 8, 128), pl.ds(first * 8 + j, ROWS, stride=8)


def edge_matrix(left, right):
    sub = lax.broadcasted_iota(I32, (8, ROWS), 0)
    top = jnp.where(sub == 0, jnp.broadcast_to(left, (8, ROWS)), 0.0)
    bottom = jnp.where(sub == 7, jnp.broadcast_to(right, (8, ROWS)), 0.0)
    return jnp.concatenate([top, jnp.zeros((112, ROWS), F32), bottom], axis=0).T


def edge_slabs(ref, first, terms):
    lane = lax.broadcasted_iota(I32, (ROWS, 128), 1)
    flat, low = slab_of(ref, first, 0)
    _, high = slab_of(ref, first, 7)
    return (
        flat[low, :] + jnp.where(lane == 0, terms, 0.0),
        flat[high, :] + jnp.where(lane == 127, terms, 0.0),
    )


def edge_columns(low, high):
    lane = lax.broadcasted_iota(I32, (ROWS, 128), 1)
    both = jnp.where(lane < 64, low, high).T
    return both[0:1], both[127:128]


def kernel(
    depth, mom_x, mom_y, bed, cells, strips_in, slots_in, sections_in, coefs_in, heads_in, conv_in,
    h2, hu2, hv2, edge_out, inflow_out, sewer_in,
    h0, hu0, hv0, z0, m0, level, h1, hu1, hv1,
    om_s, omr_s, wx_s, wy_s, sx_s, sy_s,
    strips, slots, sections, coefs, heads, conv,
    onehot, msg, mid, mid_t, got, slot_coef, slot_pipe, hur, hvr, in_section, ring,
    row_snd1, row_rcv1, row_snd2, row_rcv2, col_snd1, col_rcv1, col_snd2, col_rcv2,
    in_sem, small_sem, p1_send, p1_recv, p2_send, p2_recv, halo_send, halo_recv,
):
    gx = lax.axis_index("gx")
    gy = lax.axis_index("gy")

    def gx_peer(i):
        return {"gx": lax.rem(gx + i, NGX)}

    def gy_peer(i):
        return {"gy": lax.rem(gy + i, NGY)}

    barrier = pltpu.get_barrier_semaphore()
    for i in FAR_GX:
        pl.semaphore_signal(barrier, inc=1, device_id=gx_peer(i), device_id_type=pl.DeviceIdType.MESH)
    for i in FAR_GY:
        pl.semaphore_signal(barrier, inc=1, device_id=gy_peer(i), device_id_type=pl.DeviceIdType.MESH)

    pairs = ((depth, h0), (bed, z0), (cells, m0), (mom_x, hu0), (mom_y, hv0))

    def load(f, j, part=None):
        src, dst = pairs[f]
        rows = pl.ds(0, ROWS) if part is None else pl.ds(part * (ROWS // 2), ROWS // 2)
        return pltpu.make_async_copy(
            src.at[rows, pl.ds(128 * j, 128)], dst.at[rows, j, :], in_sem.at[f, part or 0]
        )

    def loaded(f, part=None):
        rows = pl.ds(0, ROWS) if part is None else pl.ds(part * (ROWS // 2), ROWS // 2)
        whole = pairs[f][1].at[rows]
        return pltpu.make_async_copy(whole, whole, in_sem.at[f, part or 0])

    small = ((slots_in, slots), (sections_in, sections), (coefs_in, coefs), (heads_in, heads), (strips_in, strips), (conv_in, conv))

    def load_small(i):
        return pltpu.make_async_copy(small[i][0], small[i][1], small_sem.at[i])

    for i in range(6):
        load_small(i).start()
    for part in (0, 1):
        for f in (0, 1):
            for j in range(8):
                load(f, j, part).start()
    for f in (2, 3, 4):
        for j in range(8):
            load(f, j).start()

    lane = lax.broadcasted_iota(I32, (8, 128), 1)
    sub = lax.broadcasted_iota(I32, (8, 128), 0)
    zero_row = jnp.zeros((8, 128), F32)

    for i in range(4):
        load_small(i).wait()
    slot = slots[...]
    sec = sections[...]
    coef = coefs[...]
    tile_of = slot >> 4
    k_of = slot & 15
    pipe = jnp.zeros((16, 128), F32)
    for b in range(4):
        part = lanes_at(heads[:, pl.ds(128 * b, 128)], sec & 127)
        pipe = jnp.where((sec >> 7) == b, part, pipe)
    tile_iota = lax.broadcasted_iota(I32, (128, 128), 0)
    k_iota = lax.broadcasted_iota(I32, (16, 128), 0)
    left = []
    right = []
    for l in range(16):
        left.append((jnp.broadcast_to(tile_of[l : l + 1], (128, 128)) == tile_iota).astype(F32).astype(BF16))
        hit = jnp.broadcast_to(k_of[l : l + 1], (16, 128)) == k_iota
        both = jnp.concatenate(
            [
                jnp.where(hit, jnp.broadcast_to(coef[l : l + 1], (16, 128)), 0.0),
                jnp.where(hit, jnp.broadcast_to(pipe[l : l + 1], (16, 128)), 0.0),
            ],
            axis=0,
        )
        right.append(jnp.concatenate(thirds(both), axis=0))
    by_slot = lax.dot_general(
        jnp.concatenate(right, axis=1), jnp.concatenate(left, axis=1), NT, preferred_element_type=F32
    )
    by_slot = by_slot[0:32] + by_slot[32:64] + by_slot[64:96]

    load_small(4).wait()
    strip = strips[0]
    strip_row = strip >> 3
    strip_j = strip & 7
    lane2 = lax.broadcasted_iota(I32, (8, 256), 1)

    def level_rows(t, sums):
        for i in range(32):
            r = t * 32 + i
            lev = h0[r] + z0[r]
            level[r] = lev
            sums = jnp.where(lane2 == r, jnp.sum(lev, axis=1, keepdims=True), sums)
        return sums

    sums = jnp.zeros((8, 256), F32)
    for part in (0, 1):
        for f in (0, 1):
            loaded(f, part).wait()
        sums = lax.fori_loop(4 * part, 4 * part + 4, level_rows, sums)
    by_strip = jnp.zeros((16, 128), F32)
    for half in range(2):
        for j in range(8):
            row = jnp.broadcast_to(sums[j : j + 1, 128 * half : 128 * half + 128], (16, 128))
            part = lanes_at(row, strip_row & 127)
            by_strip = jnp.where((strip_j == j) & ((strip_row >> 7) == half), part, by_strip)
    packed = jnp.concatenate([by_slot, by_strip, jnp.zeros((80, 128), F32)], axis=0).T
    msg[...] = packed.reshape(NGX, NGY, 128)

    pl.semaphore_wait(barrier, NGX + NGY - 2)

    def phase1(i):
        return pltpu.make_async_remote_copy(
            src_ref=msg.at[lax.rem(gx + i, NGX)],
            dst_ref=mid.at[gx],
            send_sem=p1_send,
            recv_sem=p1_recv,
            device_id=gx_peer(i),
            device_id_type=pl.DeviceIdType.MESH,
        )

    for i in FAR_GX:
        phase1(i).start()
    mid[gx] = msg[gx]

    loaded(2).wait()
    last_lane = lane == 127
    first_lane = lane == 0
    corner_r = (lane == 127) & (sub == 7)
    corner_l = (lane == 0) & (sub == 0)

    def from_right(x):
        a = pltpu.roll(x, 127, 1)
        return jnp.where(last_lane, pltpu.roll(a, 7, 0), a)

    def from_left(x):
        a = pltpu.roll(x, 1, 1)
        return jnp.where(first_lane, pltpu.roll(a, 1, 0), a)

    def static_rows(t, carry):
        for i in range(32):
            r = t * 32 + i
            m_prev, z_prev, z_prev2 = carry
            m = m0[r].astype(F32)
            z = z0[r]
            mr = from_right(m)
            om_s[r] = 1.0 - m
            omr_s[r] = 1.0 - mr
            wx_s[r] = (HALF_DT * m_prev) * m
            wy_s[r] = jnp.where(corner_r, 0.0, (HALF_DT * m) * mr)
            sx_s[r] = (SLOPE * m_prev) * (z - z_prev2)
            zr = jnp.where(corner_r, 0.0, from_right(z))
            zl = jnp.where(corner_l, 0.0, from_left(z))
            sy_s[r] = (SLOPE * m) * (zr - zl)
            carry = (m, z, z_prev)
        return carry

    m_end, _, z_end = lax.fori_loop(0, ROWS // 32, static_rows, (zero_row,) * 3)
    sx_s[ROWS] = (SLOPE * m_end) * (-z_end)

    for f in (3, 4):
        loaded(f).wait()

    def rows_of(r):
        return (h0[r], hu0[r], hv0[r], m0[r].astype(F32), z0[r])

    for side, r in ((0, 0), (1, ROWS - 1)):
        for f, value in enumerate(rows_of(r)):
            row_snd1[side, f] = value

    def halo_rows(snd, rcv, side, base):
        return pltpu.make_async_remote_copy(
            src_ref=snd.at[side],
            dst_ref=rcv.at[1 - side],
            send_sem=halo_send.at[base + side],
            recv_sem=halo_recv.at[base + side],
            device_id=gx_peer(NGX - 1 if side == 0 else 1),
            device_id_type=pl.DeviceIdType.MESH,
        )

    def halo_cols(snd, rcv, side, base):
        return pltpu.make_async_remote_copy(
            src_ref=snd.at[side],
            dst_ref=rcv.at[1 - side],
            send_sem=halo_send.at[base + 2 + side],
            recv_sem=halo_recv.at[base + 2 + side],
            device_id=gy_peer(NGY - 1 if side == 0 else 1),
            device_id_type=pl.DeviceIdType.MESH,
        )

    for side in (0, 1):
        halo_rows(row_snd1, row_rcv1, side, 0).start()

    cols1 = ([], [])
    for ref in (h0, hu0, hv0, m0, z0):
        flat, low = slab_of(ref, 0, 0)
        _, high = slab_of(ref, 0, 7)
        ends = edge_columns(flat[low, :].astype(F32), flat[high, :].astype(F32))
        for side in (0, 1):
            cols1[side].append(ends[side])
    for side in (0, 1):
        col_snd1[side] = jnp.concatenate(cols1[side] + [jnp.zeros((3, ROWS), F32)], axis=0)
        halo_cols(col_snd1, col_rcv1, side, 0).start()

    row_iota = lax.broadcasted_iota(I32, (ROWS, 128), 0)
    for k in range(16):
        hit = jnp.broadcast_to(strip_row[k : k + 1], (ROWS, 128)) == row_iota
        onehot[:, pl.ds(128 * k, 128)] = hit.astype(F32).astype(BF16)

    NAMES = ("h", "hu", "hv", "uu", "uv", "sx")

    def phase2(i):
        return pltpu.make_async_remote_copy(
            src_ref=mid_t.at[lax.rem(gy + i, NGY)],
            dst_ref=got.at[gy],
            send_sem=p2_send,
            recv_sem=p2_recv,
            device_id=gy_peer(i),
            device_id_type=pl.DeviceIdType.MESH,
        )

    def forward():
        pltpu.make_async_copy(mid.at[pl.ds(0, NGX - 1)], mid.at[pl.ds(0, NGX - 1)], p1_recv).wait()
        mid_flat = mid.reshape(NGX * NGY, 128)
        for b in range(NGY):
            mid_t[b] = mid_flat[pl.ds(b, NGX, stride=NGY), :]
        for i in FAR_GY:
            phase2(i).start()
        got[gy] = mid_t[gy]

    def sweep(src, off, outs, rolled, pause, between):
        drained = rolled is not None
        def ahead(r, i):
            h = src[0][r + off]
            if drained:
                less = slot_coef[r] * (level[r] - slot_pipe[r])
                h = h - less
                ring[3, i] = less
                ring[4, i] = h
            ring[0, i] = from_right(h)
            if not drained:
                ring[1, i] = from_right(src[1][r + off])
                ring[2, i] = from_right(src[2][r + off])

        def one(r, i, carry):
            prev, part = carry
            h = ring[4, i] if drained else src[0][r + off]
            q = prim(h, src[1][r + off], src[2][r + off], om_s[r])
            if drained:
                right = prim(ring[0, i], rolled[0][r], rolled[1][r], omr_s[r])
            else:
                right = prim(ring[0, i], ring[1, i], ring[2, i], omr_s[r])
            fx = face_x(wx_s[r], prev, q)
            outs[0][r] = part[0] - fx[0]
            outs[1][r] = part[1] - fx[1] - prev["h"] * sx_s[r]
            outs[2][r] = part[2] - fx[2]
            dy = [f - from_left(f) for f in face_y(wy_s[r], q, right)]
            part_h = q["h"] - dy[0] + fx[0]
            if drained:
                part_h = part_h - ring[3, i]
            part = (part_h, q["hu"] - dy[1] + fx[1], q["hv"] - dy[2] - q["h"] * sy_s[r] + fx[2])
            return {name: q[name] for name in NAMES}, part

        turns = ROWS // UNROLL
        for i in range(UNROLL):
            ahead(i, i)

        def some(t, carry):
            following = jnp.minimum(t + 1, turns - 1) * UNROLL
            for i in range(UNROLL):
                carry = one(t * UNROLL + i, i, carry)
                ahead(following + i, i)
            return carry

        start = ({name: zero_row for name in NAMES}, (zero_row,) * 3)
        carry = lax.fori_loop(0, pause, some, start) if pause else start
        between()
        prev, part = lax.fori_loop(pause, turns, some, carry)
        outs[0][ROWS] = part[0]
        outs[1][ROWS] = part[1] - prev["h"] * sx_s[ROWS]
        outs[2][ROWS] = part[2]

    sweep((h0, hu0, hv0), 0, (h1, hu1, hv1), None, 6, forward)

    for side in (0, 1):
        halo_rows(row_snd1, row_rcv1, side, 0).wait()
        halo_cols(col_snd1, col_rcv1, side, 0).wait()
    exists_x = (gx > 0, gx < NGX - 1)
    exists_y = (gy > 0, gy < NGY - 1)

    def keep(yes, x):
        return jnp.where(yes, x, 0.0)

    halo_x = [[keep(exists_x[side], row_rcv1[side, f]) for f in range(5)] for side in (0, 1)]
    mine_x = [[row_snd1[side, f] for f in range(5)] for side in (0, 1)]
    halo_y = [[keep(exists_y[side], col_rcv1[side, f : f + 1]) for f in range(5)] for side in (0, 1)]
    mine_y = [[col_snd1[side, f : f + 1] for f in range(5)] for side in (0, 1)]
    hmx = [halo_x[s][3] for s in (0, 1)]
    hzx = [halo_x[s][4] for s in (0, 1)]
    mmx = [mine_x[s][3] for s in (0, 1)]
    hmy = [halo_y[s][3] for s in (0, 1)]
    hzy = [halo_y[s][4] for s in (0, 1)]
    mmy = [mine_y[s][3] for s in (0, 1)]
    faces = faces_x([mine_x[s][:3] for s in (0, 1)], [halo_x[s][:3] for s in (0, 1)], hmx, hzx, mmx)
    for side, r in ((0, 1), (1, ROWS)):
        for f, ref in enumerate((h1, hu1, hv1)):
            ref[r] = ref[r] + faces[side][f]
    faces = faces_y([mine_y[s][:3] for s in (0, 1)], [halo_y[s][:3] for s in (0, 1)], hmy, hzy, mmy)
    cols2 = []
    for f, ref in enumerate((h1, hu1, hv1)):
        low, high = edge_slabs(ref, 1, edge_matrix(faces[0][f], faces[1][f]))
        flat, rows = slab_of(ref, 1, 0)
        flat[rows, :] = low
        flat, rows = slab_of(ref, 1, 7)
        flat[rows, :] = high
        cols2.append(edge_columns(low, high))

    def rolled_rows(t, carry):
        for i in range(32):
            r = t * 32 + i
            hur[r] = from_right(hu1[r + 1])
            hvr[r] = from_right(hv1[r + 1])
        return carry

    lax.fori_loop(0, ROWS // 32, rolled_rows, 0)

    load_small(5).wait()
    cv = conv[...]
    sec_lane = lax.broadcasted_iota(I32, (16, 512), 1)
    face_k = jnp.where(sec_lane == 511, cv, 0.5 * (cv + pltpu.roll(cv, 511, 1)))
    sewer_in[0] = heads[...]
    sewer_in[1] = face_k
    sewer_in[2] = jnp.where(sec_lane == 0, 0.0, pltpu.roll(face_k, 1, 1))
    for l in range(16):
        hit = jnp.broadcast_to(sec[l : l + 1] & 127, (128, 128)) == tile_iota
        in_section[l] = hit.astype(F32).astype(BF16)

    pltpu.make_async_copy(got.at[pl.ds(0, NGY - 1)], got.at[pl.ds(0, NGY - 1)], p2_recv).wait()
    got_flat = got.reshape(NGX * NGY, 128)
    arrived = jnp.concatenate([got_flat[pl.ds(a, NGY, stride=NGX), :] for a in range(NGX)], axis=0).T
    right = []
    j_iota = lax.broadcasted_iota(I32, (8, 128), 0)
    for k in range(16):
        hit = jnp.broadcast_to(strip_j[k : k + 1], (8, 128)) == j_iota
        both = jnp.concatenate(
            [
                jnp.where(hit, jnp.broadcast_to(arrived[k : k + 1], (8, 128)), 0.0),
                jnp.where(hit, jnp.broadcast_to(arrived[16 + k : 17 + k], (8, 128)), 0.0),
            ],
            axis=0,
        )
        right.append(jnp.concatenate(thirds(both), axis=0))
    by_row = lax.dot_general(jnp.concatenate(right, axis=1), onehot[...], NT, preferred_element_type=F32)
    by_row = by_row[0:16] + by_row[16:32] + by_row[32:48]
    by_row = jnp.concatenate([DT * by_row[0:8], by_row[8:16]], axis=0)

    def drain_of(r):
        lanes = by_row[:, 0:128] if r < 128 else by_row[:, 128:256]
        at = r % 128
        c = jnp.broadcast_to(lanes[0:8, at : at + 1], (8, 128))
        p = jnp.broadcast_to(lanes[8:16, at : at + 1], (8, 128))
        return c * (level[r] - p)

    own_x = []
    for side, r in ((0, 0), (1, ROWS - 1)):
        own_x.append((h1[r + 1] - drain_of(r), hu1[r + 1], hv1[r + 1]))
        for f in range(3):
            row_snd2[side, f] = own_x[side][f]
    own_y = []
    for side, j in ((0, 0), (1, 7)):
        lev = mine_y[side][0] + mine_y[side][4]
        less = by_row[j : j + 1] * (lev - by_row[8 + j : 9 + j])
        own_y.append((cols2[0][side] - less, cols2[1][side], cols2[2][side]))
        col_snd2[side] = jnp.concatenate(list(own_y[side]) + [jnp.zeros((5, ROWS), F32)], axis=0)
    for side in (0, 1):
        halo_rows(row_snd2, row_rcv2, side, 4).start()
        halo_cols(col_snd2, col_rcv2, side, 4).start()

    level_sum = jnp.zeros((16, 128), F32)
    for k in range(16):
        row = jnp.broadcast_to(arrived[32 + k : 33 + k], (16, 128))
        level_sum = jnp.where(k_of == k, lanes_at(row, tile_of & 127), level_sum)
    rate = jnp.where(slot >= 0, coef * (level_sum - 128.0 * pipe), 0.0)
    block = lax.broadcasted_iota(I32, (8, 128), 0)
    for l in range(16):
        s_row = sec[l : l + 1]
        value = jnp.where(
            jnp.broadcast_to(s_row >> 7, (8, 128)) == block, jnp.broadcast_to(rate[l : l + 1], (8, 128)), 0.0
        )
        got_l = lax.dot_general(jnp.concatenate(thirds(value), axis=0), in_section[l], NT, preferred_element_type=F32)
        got_l = got_l[0:8] + got_l[8:16] + got_l[16:24]
        for b in range(4):
            inflow_out[l : l + 1, pl.ds(128 * b, 128)] = got_l[b : b + 1]

    for ref, first in ((slot_coef, 0), (slot_pipe, 8)):
        for half in range(2):
            for j in range(8):
                value = by_row[first + j : first + j + 1, 128 * half : 128 * half + 128]
                flat = ref.reshape(ROWS * 8, 128)
                flat[pl.ds(1024 * half + j, 128, stride=8), :] = jnp.broadcast_to(value, (128, 128)).T
    sweep((h1, hu1, hv1), 1, (h2, hu2, hv2), (hur, hvr), 0, lambda: None)

    for side in (0, 1):
        halo_rows(row_snd2, row_rcv2, side, 4).wait()
        halo_cols(col_snd2, col_rcv2, side, 4).wait()
    halo_x = [[keep(exists_x[side], row_rcv2[side, f]) for f in range(3)] for side in (0, 1)]
    halo_y = [[keep(exists_y[side], col_rcv2[side, f : f + 1]) for f in range(3)] for side in (0, 1)]
    faces = faces_x(own_x, halo_x, hmx, hzx, mmx)
    for side, r in ((0, 1), (1, ROWS)):
        for f, ref in enumerate((h2, hu2, hv2)):
            ref[r] = ref[r] + faces[side][f]

    for side in (0, 1):
        rows = list(own_y[side]) + [mmy[side], hzy[side], hmy[side]] + halo_y[side]
        edge_out[side] = jnp.concatenate(rows + [jnp.zeros((7, ROWS), F32)], axis=0)

    pltpu.make_async_copy(msg.at[pl.ds(0, NGX - 1)], msg.at[pl.ds(0, NGX - 1)], p1_send).wait()
    pltpu.make_async_copy(mid_t.at[pl.ds(0, NGY - 1)], mid_t.at[pl.ds(0, NGY - 1)], p2_send).wait()


def finish(
    h2, hu2, hv2, edge, inflow, sewer_in,
    out_h, out_hu, out_hv, out_sewer,
    slabs, sewer,
    out_sem, sewer_sem,
):
    outs = ((h2, out_h), (hu2, out_hu), (hv2, out_hv))

    def store(f, j):
        src, dst = outs[f]
        if j in (0, 7):
            part = slabs.at[f, j // 7]
        else:
            part = src.at[pl.ds(1, ROWS), j, :]
        return pltpu.make_async_copy(part, dst.at[:, pl.ds(128 * j, 128)], out_sem.at[f])

    for f in range(3):
        for j in range(1, 7):
            store(f, j).start()

    def row(side, i):
        return edge[side, i : i + 1]

    own = [[row(s, i) for i in range(3)] for s in (0, 1)]
    halo = [[row(s, 6 + i) for i in range(3)] for s in (0, 1)]
    faces = faces_y(
        own, halo, [row(s, 5) for s in (0, 1)], [row(s, 4) for s in (0, 1)], [row(s, 3) for s in (0, 1)]
    )
    for f, (ref, _) in enumerate(outs):
        both = edge_slabs(ref, 1, edge_matrix(faces[0][f], faces[1][f]))
        for side in (0, 1):
            slabs[f, side] = both[side]

    share = inflow[...] / AREA
    head, face_k, above_k = sewer_in[0], sewer_in[1], sewer_in[2]
    sec_lane = lax.broadcasted_iota(I32, (16, 512), 1)
    for turn in range(SUBSTEPS):
        below = jnp.where(sec_lane == 511, 0.0, pltpu.roll(head, 511, 1))
        leaving = face_k * (head - below)
        entering = above_k * (pltpu.roll(head, 1, 1) - head)
        head = head + SEWER_DT * (entering - leaving + share)
    sewer[...] = head
    for f in range(3):
        for side in (0, 1):
            store(f, 7 * side).start()
    sewer_copy = pltpu.make_async_copy(sewer, out_sewer, sewer_sem)
    sewer_copy.start()
    for f, (src, _) in enumerate(outs):
        whole = src.at[pl.ds(1, ROWS)]
        pltpu.make_async_copy(whole, whole, out_sem.at[f]).wait()
    sewer_copy.wait()

def body(*args):
    args = [jnp.swapaxes(a, 1, 2) if a.ndim == 3 else a for a in args]
    rows, cols = args[0].shape
    grid = jax.ShapeDtypeStruct((rows, cols), F32)
    sewer = jax.ShapeDtypeStruct(args[9].shape, F32)
    args = [pltpu.with_memory_space_constraint(a, pltpu.HBM) for a in args]
    depth, mom_x, mom_y, bed, cells, strips, slots, sections, coefs, heads, conv = args
    hbm = pl.BlockSpec(memory_space=pltpu.HBM)
    vmem = pl.BlockSpec(memory_space=pltpu.VMEM)
    dma = pltpu.SemaphoreType.DMA
    padded = pltpu.VMEM((ROWS + 1, 8, 128), F32)
    h2, hu2, hv2, edge, inflow, sewer_in = pl.pallas_call(
        kernel,
        out_shape=(padded,) * 3
        + (pltpu.VMEM((2, 16, ROWS), F32), pltpu.VMEM((16, 512), F32), pltpu.VMEM((3, 16, 512), F32)),
        in_specs=[hbm] * 11,
        out_specs=(vmem,) * 6,
        scratch_shapes=[pltpu.VMEM((ROWS, 8, 128), F32)] * 4
        + [pltpu.VMEM((ROWS, 8, 128), I32), pltpu.VMEM((ROWS, 8, 128), F32)]
        + [pltpu.VMEM((ROWS + 1, 8, 128), F32)] * 9
        + [
            pltpu.VMEM((1, 16, 128), I32),
            pltpu.VMEM((16, 128), I32),
            pltpu.VMEM((16, 128), I32),
            pltpu.VMEM((16, 128), F32),
            pltpu.VMEM((16, 512), F32),
            pltpu.VMEM((16, 512), F32),
            pltpu.VMEM((ROWS, 2048), BF16),
            pltpu.VMEM((NGX, NGY, 128), F32),
            pltpu.VMEM((NGX, NGY, 128), F32),
            pltpu.VMEM((NGY, NGX, 128), F32),
            pltpu.VMEM((NGY, NGX, 128), F32),
            pltpu.VMEM((ROWS, 8, 128), F32),
            pltpu.VMEM((ROWS, 8, 128), F32),
            pltpu.VMEM((ROWS, 8, 128), F32),
            pltpu.VMEM((ROWS, 8, 128), F32),
            pltpu.VMEM((16, 128, 128), BF16),
            pltpu.VMEM((5, UNROLL, 8, 128), F32),
            pltpu.VMEM((2, 5, 8, 128), F32),
            pltpu.VMEM((2, 5, 8, 128), F32),
            pltpu.VMEM((2, 3, 8, 128), F32),
            pltpu.VMEM((2, 3, 8, 128), F32),
            pltpu.VMEM((2, 8, ROWS), F32),
            pltpu.VMEM((2, 8, ROWS), F32),
            pltpu.VMEM((2, 8, ROWS), F32),
            pltpu.VMEM((2, 8, ROWS), F32),
            dma((5, 2)),
            dma((6,)),
            dma,
            dma,
            dma,
            dma,
            dma((8,)),
            dma((8,)),
        ],
        compiler_params=pltpu.CompilerParams(
            collective_id=0, has_side_effects=True, vmem_limit_bytes=40 * 1024 * 1024
        ),
        name="street_flood",
    )(depth, mom_x, mom_y, bed, cells, strips, slots, sections, coefs, heads, conv)
    return pl.pallas_call(
        finish,
        out_shape=(grid, grid, grid, sewer),
        in_specs=[vmem] * 6,
        out_specs=(hbm,) * 4,
        scratch_shapes=[
            pltpu.VMEM((3, 2, ROWS, 128), F32),
            pltpu.VMEM((16, 512), F32),
            dma((3,)),
            dma,
        ],
        compiler_params=pltpu.CompilerParams(vmem_limit_bytes=16 * 1024 * 1024),
        name="flood_finish",
    )(h2, hu2, hv2, edge, inflow, sewer_in)


def solution(mesh):
    tiles = P("gx", "gy")
    lines = P(("gx", "gy"), None)
    return jax.shard_map(
        body,
        mesh=mesh,
        in_specs=(tiles,) * 5 + (P(("gx", "gy"), None, None),) + (lines,) * 5,
        out_specs=(tiles, tiles, tiles, lines),
        check_vma=False,
    )
```

```python
import math

import jax
import jax.numpy as jnp
from jax import lax
from jax.experimental import pallas as pl
from jax.experimental.pallas import tpu as pltpu
from jax.sharding import PartitionSpec as P

SUBSTEPS = 8
GRAVITY = 9.81
DT = 0.02
SEWER_DT = 0.5
AREA = 256.0
HALF_DT = 0.5 * DT
ROOT_G = math.sqrt(GRAVITY)
HALF_G = 0.5 * GRAVITY
SLOPE = 0.5 * GRAVITY * DT
NGX = 8
FAR_GY = (10, 9, 11, 6, 14, 8, 2, 5, 7, 13, 15, 1, 3, 4, 12)
FAR_GX = (4, 3, 5, 2, 6, 1, 7)
NGY = 16
ROWS = 256
UNROLL = 16
F32 = jnp.float32
BF16 = jnp.bfloat16
I32 = jnp.int32
NT = (((1,), (1,)), ((), ()))


def thirds(x):
    a = x.astype(BF16)
    rest = x - a.astype(F32)
    b = rest.astype(BF16)
    c = (rest - b.astype(F32)).astype(BF16)
    return a, b, c


def lanes_at(row, idx):
    return jnp.take_along_axis(row, idx, axis=1, mode="promise_in_bounds")


def prim(h, hu, hv, om):
    hs = h + om
    y = lax.rsqrt(hs)
    inv = y * y
    u = hu * inv
    v = hv * inv
    c = (ROOT_G * hs) * y
    p = HALF_G * h * h
    return dict(
        h=h,
        hu=hu,
        hv=hv,
        uu=hu * u + p,
        uv=hu * v,
        vv=hv * v + p,
        sx=jnp.abs(u) + c,
        sy=jnp.abs(v) + c,
    )


def face_x(wall, l, r):
    a = jnp.maximum(l["sx"], r["sx"])
    return (
        wall * ((l["hu"] + r["hu"]) - a * (r["h"] - l["h"])),
        wall * ((l["uu"] + r["uu"]) - a * (r["hu"] - l["hu"])),
        wall * ((l["uv"] + r["uv"]) - a * (r["hv"] - l["hv"])),
    )


def face_y(wall, l, r):
    a = jnp.maximum(l["sy"], r["sy"])
    return (
        wall * ((l["hv"] + r["hv"]) - a * (r["h"] - l["h"])),
        wall * ((l["uv"] + r["uv"]) - a * (r["hu"] - l["hu"])),
        wall * ((l["vv"] + r["vv"]) - a * (r["hv"] - l["hv"])),
    )


def faces_x(rows, halo, halo_m, halo_z, mine_m):
    out = []
    for side in (0, 1):
        mine = prim(*rows[side], 1.0 - mine_m[side])
        other = prim(*halo[side], 1.0 - halo_m[side])
        wall = (HALF_DT * halo_m[side]) * mine_m[side]
        slope = (SLOPE * mine_m[side]) * (halo_z[side] * mine["h"])
        if side == 0:
            f = face_x(wall, other, mine)
            out.append((f[0], f[1] + slope, f[2]))
        else:
            f = face_x(wall, mine, other)
            out.append((-f[0], -f[1] - slope, -f[2]))
    return out


def faces_y(cols, halo, halo_m, halo_z, mine_m):
    out = []
    for side in (0, 1):
        mine = prim(*cols[side], 1.0 - mine_m[side])
        other = prim(*halo[side], 1.0 - halo_m[side])
        wall = (HALF_DT * halo_m[side]) * mine_m[side]
        slope = (SLOPE * mine_m[side]) * (halo_z[side] * mine["h"])
        if side == 0:
            f = face_y(wall, other, mine)
            out.append((f[0], f[1], f[2] + slope))
        else:
            f = face_y(wall, mine, other)
            out.append((-f[0], -f[1], -f[2] - slope))
    return out


def slab_of(ref, first, j):
    return ref.reshape(ref.shape[0] * 8, 128), pl.ds(first * 8 + j, ROWS, stride=8)


def edge_matrix(left, right):
    sub = lax.broadcasted_iota(I32, (8, ROWS), 0)
    top = jnp.where(sub == 0, jnp.broadcast_to(left, (8, ROWS)), 0.0)
    bottom = jnp.where(sub == 7, jnp.broadcast_to(right, (8, ROWS)), 0.0)
    return jnp.concatenate([top, jnp.zeros((112, ROWS), F32), bottom], axis=0).T


def edge_slabs(ref, first, terms):
    lane = lax.broadcasted_iota(I32, (ROWS, 128), 1)
    flat, low = slab_of(ref, first, 0)
    _, high = slab_of(ref, first, 7)
    return (
        flat[low, :] + jnp.where(lane == 0, terms, 0.0),
        flat[high, :] + jnp.where(lane == 127, terms, 0.0),
    )


def edge_columns(low, high):
    lane = lax.broadcasted_iota(I32, (ROWS, 128), 1)
    both = jnp.where(lane < 64, low, high).T
    return both[0:1], both[127:128]


def kernel(
    depth, mom_x, mom_y, bed, cells, strips_in, slots_in, sections_in, coefs_in, heads_in, conv_in,
    h2, hu2, hv2, edge_out, inflow_out, sewer_in,
    h0, hu0, hv0, z0, m0, level, h1, hu1, hv1,
    om_s, omr_s, wx_s, wy_s, sx_s, sy_s,
    strips, slots, sections, coefs, heads, conv,
    onehot, msg, mid, mid_t, got, slot_coef, slot_pipe, hur, hvr, in_section, ring,
    row_snd1, row_rcv1, row_snd2, row_rcv2, col_snd1, col_rcv1, col_snd2, col_rcv2,
    in_sem, small_sem, p1_send, p1_recv, p2_send, p2_recv, halo_send, halo_recv,
):
    gx = lax.axis_index("gx")
    gy = lax.axis_index("gy")

    def gx_peer(i):
        return {"gx": lax.rem(gx + i, NGX)}

    def gy_peer(i):
        return {"gy": lax.rem(gy + i, NGY)}

    barrier = pltpu.get_barrier_semaphore()
    for i in FAR_GX:
        pl.semaphore_signal(barrier, inc=1, device_id=gx_peer(i), device_id_type=pl.DeviceIdType.MESH)
    for i in FAR_GY:
        pl.semaphore_signal(barrier, inc=1, device_id=gy_peer(i), device_id_type=pl.DeviceIdType.MESH)

    def start_halo(copy, side, at, last):
        @pl.when(at > 0 if side == 0 else at < last)
        def _():
            copy.start()

    def wait_halo(copy, side, at, last):
        @pl.when(at > 0 if side == 0 else at < last)
        def _():
            copy.wait_send()

        @pl.when(at < last if side == 0 else at > 0)
        def _():
            copy.wait_recv()

    pairs = ((depth, h0), (bed, z0), (cells, m0), (mom_x, hu0), (mom_y, hv0))

    def load(f, j, part=None):
        src, dst = pairs[f]
        rows = pl.ds(0, ROWS) if part is None else pl.ds(part * (ROWS // 2), ROWS // 2)
        return pltpu.make_async_copy(
            src.at[rows, pl.ds(128 * j, 128)], dst.at[rows, j, :], in_sem.at[f, part or 0]
        )

    def loaded(f, part=None):
        rows = pl.ds(0, ROWS) if part is None else pl.ds(part * (ROWS // 2), ROWS // 2)
        whole = pairs[f][1].at[rows]
        return pltpu.make_async_copy(whole, whole, in_sem.at[f, part or 0])

    small = ((slots_in, slots), (sections_in, sections), (coefs_in, coefs), (heads_in, heads), (strips_in, strips), (conv_in, conv))

    def load_small(i):
        return pltpu.make_async_copy(small[i][0], small[i][1], small_sem.at[i])

    for i in range(6):
        load_small(i).start()
    for part in (0, 1):
        for f in (0, 1):
            for j in range(8):
                load(f, j, part).start()
    for f in (2, 3, 4):
        for j in range(8):
            load(f, j).start()

    lane = lax.broadcasted_iota(I32, (8, 128), 1)
    sub = lax.broadcasted_iota(I32, (8, 128), 0)
    zero_row = jnp.zeros((8, 128), F32)

    for i in range(4):
        load_small(i).wait()
    slot = slots[...]
    sec = sections[...]
    coef = coefs[...]
    tile_of = slot >> 4
    k_of = slot & 15
    pipe = jnp.zeros((16, 128), F32)
    for b in range(4):
        part = lanes_at(heads[:, pl.ds(128 * b, 128)], sec & 127)
        pipe = jnp.where((sec >> 7) == b, part, pipe)
    tile_iota = lax.broadcasted_iota(I32, (128, 128), 0)
    k_iota = lax.broadcasted_iota(I32, (16, 128), 0)
    left = []
    right = []
    for l in range(16):
        left.append((jnp.broadcast_to(tile_of[l : l + 1], (128, 128)) == tile_iota).astype(F32).astype(BF16))
        hit = jnp.broadcast_to(k_of[l : l + 1], (16, 128)) == k_iota
        both = jnp.concatenate(
            [
                jnp.where(hit, jnp.broadcast_to(coef[l : l + 1], (16, 128)), 0.0),
                jnp.where(hit, jnp.broadcast_to(pipe[l : l + 1], (16, 128)), 0.0),
            ],
            axis=0,
        )
        right.append(jnp.concatenate(thirds(both), axis=0))
    by_slot = lax.dot_general(
        jnp.concatenate(right, axis=1), jnp.concatenate(left, axis=1), NT, preferred_element_type=F32
    )
    by_slot = by_slot[0:32] + by_slot[32:64] + by_slot[64:96]

    load_small(4).wait()
    strip = strips[0]
    strip_row = strip >> 3
    strip_j = strip & 7
    lane2 = lax.broadcasted_iota(I32, (8, 256), 1)

    def level_rows(t, sums):
        for i in range(32):
            r = t * 32 + i
            lev = h0[r] + z0[r]
            level[r] = lev
            sums = jnp.where(lane2 == r, jnp.sum(lev, axis=1, keepdims=True), sums)
        return sums

    sums = jnp.zeros((8, 256), F32)
    for part in (0, 1):
        for f in (0, 1):
            loaded(f, part).wait()
        sums = lax.fori_loop(4 * part, 4 * part + 4, level_rows, sums)
    by_strip = jnp.zeros((16, 128), F32)
    for half in range(2):
        for j in range(8):
            row = jnp.broadcast_to(sums[j : j + 1, 128 * half : 128 * half + 128], (16, 128))
            part = lanes_at(row, strip_row & 127)
            by_strip = jnp.where((strip_j == j) & ((strip_row >> 7) == half), part, by_strip)
    packed = jnp.concatenate([by_slot, by_strip, jnp.zeros((80, 128), F32)], axis=0).T
    msg[...] = packed.reshape(NGX, NGY, 128)

    pl.semaphore_wait(barrier, NGX + NGY - 2)

    def phase1(i):
        return pltpu.make_async_remote_copy(
            src_ref=msg.at[lax.rem(gx + i, NGX)],
            dst_ref=mid.at[gx],
            send_sem=p1_send,
            recv_sem=p1_recv,
            device_id=gx_peer(i),
            device_id_type=pl.DeviceIdType.MESH,
        )

    for i in FAR_GX:
        phase1(i).start()
    mid[gx] = msg[gx]

    loaded(2).wait()
    last_lane = lane == 127
    first_lane = lane == 0
    corner_r = (lane == 127) & (sub == 7)
    corner_l = (lane == 0) & (sub == 0)

    def from_right(x):
        a = pltpu.roll(x, 127, 1)
        return jnp.where(last_lane, pltpu.roll(a, 7, 0), a)

    def from_left(x):
        a = pltpu.roll(x, 1, 1)
        return jnp.where(first_lane, pltpu.roll(a, 1, 0), a)

    def static_rows(t, carry):
        for i in range(32):
            r = t * 32 + i
            m_prev, z_prev, z_prev2 = carry
            m = m0[r].astype(F32)
            z = z0[r]
            mr = from_right(m)
            om_s[r] = 1.0 - m
            omr_s[r] = 1.0 - mr
            wx_s[r] = (HALF_DT * m_prev) * m
            wy_s[r] = jnp.where(corner_r, 0.0, (HALF_DT * m) * mr)
            sx_s[r] = (SLOPE * m_prev) * (z - z_prev2)
            zr = jnp.where(corner_r, 0.0, from_right(z))
            zl = jnp.where(corner_l, 0.0, from_left(z))
            sy_s[r] = (SLOPE * m) * (zr - zl)
            carry = (m, z, z_prev)
        return carry

    m_end, _, z_end = lax.fori_loop(0, ROWS // 32, static_rows, (zero_row,) * 3)
    sx_s[ROWS] = (SLOPE * m_end) * (-z_end)

    for f in (3, 4):
        loaded(f).wait()

    def rows_of(r):
        return (h0[r], hu0[r], hv0[r], m0[r].astype(F32), z0[r])

    for side, r in ((0, 0), (1, ROWS - 1)):
        for f, value in enumerate(rows_of(r)):
            row_snd1[side, f] = value

    def halo_rows(snd, rcv, side, base):
        return pltpu.make_async_remote_copy(
            src_ref=snd.at[side],
            dst_ref=rcv.at[1 - side],
            send_sem=halo_send.at[base + side],
            recv_sem=halo_recv.at[base + side],
            device_id=gx_peer(NGX - 1 if side == 0 else 1),
            device_id_type=pl.DeviceIdType.MESH,
        )

    def halo_cols(snd, rcv, side, base):
        return pltpu.make_async_remote_copy(
            src_ref=snd.at[side],
            dst_ref=rcv.at[1 - side],
            send_sem=halo_send.at[base + 2 + side],
            recv_sem=halo_recv.at[base + 2 + side],
            device_id=gy_peer(NGY - 1 if side == 0 else 1),
            device_id_type=pl.DeviceIdType.MESH,
        )

    for side in (0, 1):
        start_halo(halo_rows(row_snd1, row_rcv1, side, 0), side, gx, NGX - 1)

    cols1 = ([], [])
    for ref in (h0, hu0, hv0, m0, z0):
        flat, low = slab_of(ref, 0, 0)
        _, high = slab_of(ref, 0, 7)
        ends = edge_columns(flat[low, :].astype(F32), flat[high, :].astype(F32))
        for side in (0, 1):
            cols1[side].append(ends[side])
    for side in (0, 1):
        col_snd1[side] = jnp.concatenate(cols1[side] + [jnp.zeros((3, ROWS), F32)], axis=0)
        start_halo(halo_cols(col_snd1, col_rcv1, side, 0), side, gy, NGY - 1)

    load_small(5).wait()
    cv = conv[...]
    sec_lane = lax.broadcasted_iota(I32, (16, 512), 1)
    face_k = jnp.where(sec_lane == 511, cv, 0.5 * (cv + pltpu.roll(cv, 511, 1)))
    sewer_in[0] = heads[...]
    sewer_in[1] = face_k
    sewer_in[2] = jnp.where(sec_lane == 0, 0.0, pltpu.roll(face_k, 1, 1))
    for l in range(16):
        hit = jnp.broadcast_to(sec[l : l + 1] & 127, (128, 128)) == tile_iota
        in_section[l] = hit.astype(F32).astype(BF16)

    row_iota = lax.broadcasted_iota(I32, (ROWS, 128), 0)
    for k in range(16):
        hit = jnp.broadcast_to(strip_row[k : k + 1], (ROWS, 128)) == row_iota
        onehot[:, pl.ds(128 * k, 128)] = hit.astype(F32).astype(BF16)

    NAMES = ("h", "hu", "hv", "uu", "uv", "sx")

    def phase2(i):
        return pltpu.make_async_remote_copy(
            src_ref=mid_t.at[lax.rem(gy + i, NGY)],
            dst_ref=got.at[gy],
            send_sem=p2_send,
            recv_sem=p2_recv,
            device_id=gy_peer(i),
            device_id_type=pl.DeviceIdType.MESH,
        )

    def forward():
        pltpu.make_async_copy(mid.at[pl.ds(0, NGX - 1)], mid.at[pl.ds(0, NGX - 1)], p1_recv).wait()
        mid_flat = mid.reshape(NGX * NGY, 128)
        for b in range(NGY):
            mid_t[b] = mid_flat[pl.ds(b, NGX, stride=NGY), :]
        for i in FAR_GY:
            phase2(i).start()
        got[gy] = mid_t[gy]

    def sweep(src, off, outs, rolled, pause, between):
        drained = rolled is not None
        def ahead(r, i):
            h = src[0][r + off]
            if drained:
                less = slot_coef[r] * (level[r] - slot_pipe[r])
                h = h - less
                ring[3, i] = less
                ring[4, i] = h
            ring[0, i] = from_right(h)
            if not drained:
                ring[1, i] = from_right(src[1][r + off])
                ring[2, i] = from_right(src[2][r + off])

        def one(r, i, carry):
            prev, part = carry
            h = ring[4, i] if drained else src[0][r + off]
            q = prim(h, src[1][r + off], src[2][r + off], om_s[r])
            if drained:
                right = prim(ring[0, i], rolled[0][r], rolled[1][r], omr_s[r])
            else:
                right = prim(ring[0, i], ring[1, i], ring[2, i], omr_s[r])
            fx = face_x(wx_s[r], prev, q)
            outs[0][r] = part[0] - fx[0]
            outs[1][r] = part[1] - fx[1] - prev["h"] * sx_s[r]
            outs[2][r] = part[2] - fx[2]
            dy = [f - from_left(f) for f in face_y(wy_s[r], q, right)]
            part_h = q["h"] - dy[0] + fx[0]
            if drained:
                part_h = part_h - ring[3, i]
            part = (part_h, q["hu"] - dy[1] + fx[1], q["hv"] - dy[2] - q["h"] * sy_s[r] + fx[2])
            return {name: q[name] for name in NAMES}, part

        turns = ROWS // UNROLL
        for i in range(UNROLL):
            ahead(i, i)

        def some(t, carry):
            following = jnp.minimum(t + 1, turns - 1) * UNROLL
            for i in range(UNROLL):
                carry = one(t * UNROLL + i, i, carry)
                ahead(following + i, i)
            return carry

        start = ({name: zero_row for name in NAMES}, (zero_row,) * 3)
        carry = lax.fori_loop(0, pause, some, start) if pause else start
        between()
        prev, part = lax.fori_loop(pause, turns, some, carry)
        outs[0][ROWS] = part[0]
        outs[1][ROWS] = part[1] - prev["h"] * sx_s[ROWS]
        outs[2][ROWS] = part[2]

    sweep((h0, hu0, hv0), 0, (h1, hu1, hv1), None, 8, forward)

    for side in (0, 1):
        wait_halo(halo_rows(row_snd1, row_rcv1, side, 0), side, gx, NGX - 1)
        wait_halo(halo_cols(col_snd1, col_rcv1, side, 0), side, gy, NGY - 1)
    exists_x = (gx > 0, gx < NGX - 1)
    exists_y = (gy > 0, gy < NGY - 1)

    def keep(yes, x):
        return jnp.where(yes, x, 0.0)

    halo_x = [[keep(exists_x[side], row_rcv1[side, f]) for f in range(5)] for side in (0, 1)]
    mine_x = [[row_snd1[side, f] for f in range(5)] for side in (0, 1)]
    halo_y = [[keep(exists_y[side], col_rcv1[side, f : f + 1]) for f in range(5)] for side in (0, 1)]
    mine_y = [[col_snd1[side, f : f + 1] for f in range(5)] for side in (0, 1)]
    hmx = [halo_x[s][3] for s in (0, 1)]
    hzx = [halo_x[s][4] for s in (0, 1)]
    mmx = [mine_x[s][3] for s in (0, 1)]
    hmy = [halo_y[s][3] for s in (0, 1)]
    hzy = [halo_y[s][4] for s in (0, 1)]
    mmy = [mine_y[s][3] for s in (0, 1)]
    faces = faces_x([mine_x[s][:3] for s in (0, 1)], [halo_x[s][:3] for s in (0, 1)], hmx, hzx, mmx)
    for side, r in ((0, 1), (1, ROWS)):
        for f, ref in enumerate((h1, hu1, hv1)):
            ref[r] = ref[r] + faces[side][f]
    faces = faces_y([mine_y[s][:3] for s in (0, 1)], [halo_y[s][:3] for s in (0, 1)], hmy, hzy, mmy)
    cols2 = []
    for f, ref in enumerate((h1, hu1, hv1)):
        low, high = edge_slabs(ref, 1, edge_matrix(faces[0][f], faces[1][f]))
        flat, rows = slab_of(ref, 1, 0)
        flat[rows, :] = low
        flat, rows = slab_of(ref, 1, 7)
        flat[rows, :] = high
        cols2.append(edge_columns(low, high))

    def rolled_rows(t, carry):
        for i in range(32):
            r = t * 32 + i
            hur[r] = from_right(hu1[r + 1])
            hvr[r] = from_right(hv1[r + 1])
        return carry

    lax.fori_loop(0, ROWS // 32, rolled_rows, 0)

    pltpu.make_async_copy(got.at[pl.ds(0, NGY - 1)], got.at[pl.ds(0, NGY - 1)], p2_recv).wait()
    got_flat = got.reshape(NGX * NGY, 128)
    arrived = jnp.concatenate([got_flat[pl.ds(a, NGY, stride=NGX), :] for a in range(NGX)], axis=0).T
    right = []
    j_iota = lax.broadcasted_iota(I32, (8, 128), 0)
    for k in range(16):
        hit = jnp.broadcast_to(strip_j[k : k + 1], (8, 128)) == j_iota
        both = jnp.concatenate(
            [
                jnp.where(hit, jnp.broadcast_to(arrived[k : k + 1], (8, 128)), 0.0),
                jnp.where(hit, jnp.broadcast_to(arrived[16 + k : 17 + k], (8, 128)), 0.0),
            ],
            axis=0,
        )
        right.append(jnp.concatenate(thirds(both), axis=0))
    by_row = lax.dot_general(jnp.concatenate(right, axis=1), onehot[...], NT, preferred_element_type=F32)
    by_row = by_row[0:16] + by_row[16:32] + by_row[32:48]
    by_row = jnp.concatenate([DT * by_row[0:8], by_row[8:16]], axis=0)

    def drain_of(r):
        lanes = by_row[:, 0:128] if r < 128 else by_row[:, 128:256]
        at = r % 128
        c = jnp.broadcast_to(lanes[0:8, at : at + 1], (8, 128))
        p = jnp.broadcast_to(lanes[8:16, at : at + 1], (8, 128))
        return c * (level[r] - p)

    own_x = []
    for side, r in ((0, 0), (1, ROWS - 1)):
        own_x.append((h1[r + 1] - drain_of(r), hu1[r + 1], hv1[r + 1]))
        for f in range(3):
            row_snd2[side, f] = own_x[side][f]
    own_y = []
    for side, j in ((0, 0), (1, 7)):
        lev = mine_y[side][0] + mine_y[side][4]
        less = by_row[j : j + 1] * (lev - by_row[8 + j : 9 + j])
        own_y.append((cols2[0][side] - less, cols2[1][side], cols2[2][side]))
        col_snd2[side] = jnp.concatenate(list(own_y[side]) + [jnp.zeros((5, ROWS), F32)], axis=0)
    for side in (0, 1):
        start_halo(halo_rows(row_snd2, row_rcv2, side, 4), side, gx, NGX - 1)
        start_halo(halo_cols(col_snd2, col_rcv2, side, 4), side, gy, NGY - 1)

    level_sum = jnp.zeros((16, 128), F32)
    for k in range(16):
        row = jnp.broadcast_to(arrived[32 + k : 33 + k], (16, 128))
        level_sum = jnp.where(k_of == k, lanes_at(row, tile_of & 127), level_sum)
    rate = jnp.where(slot >= 0, coef * (level_sum - 128.0 * pipe), 0.0)
    block = lax.broadcasted_iota(I32, (8, 128), 0)
    for l in range(16):
        s_row = sec[l : l + 1]
        value = jnp.where(
            jnp.broadcast_to(s_row >> 7, (8, 128)) == block, jnp.broadcast_to(rate[l : l + 1], (8, 128)), 0.0
        )
        got_l = lax.dot_general(jnp.concatenate(thirds(value), axis=0), in_section[l], NT, preferred_element_type=F32)
        got_l = got_l[0:8] + got_l[8:16] + got_l[16:24]
        for b in range(4):
            inflow_out[l : l + 1, pl.ds(128 * b, 128)] = got_l[b : b + 1]

    for ref, first in ((slot_coef, 0), (slot_pipe, 8)):
        for half in range(2):
            for j in range(8):
                value = by_row[first + j : first + j + 1, 128 * half : 128 * half + 128]
                flat = ref.reshape(ROWS * 8, 128)
                flat[pl.ds(1024 * half + j, 128, stride=8), :] = jnp.broadcast_to(value, (128, 128)).T
    sweep((h1, hu1, hv1), 1, (h2, hu2, hv2), (hur, hvr), 0, lambda: None)

    for side in (0, 1):
        wait_halo(halo_rows(row_snd2, row_rcv2, side, 4), side, gx, NGX - 1)
        wait_halo(halo_cols(col_snd2, col_rcv2, side, 4), side, gy, NGY - 1)
    halo_x = [[keep(exists_x[side], row_rcv2[side, f]) for f in range(3)] for side in (0, 1)]
    halo_y = [[keep(exists_y[side], col_rcv2[side, f : f + 1]) for f in range(3)] for side in (0, 1)]
    faces = faces_x(own_x, halo_x, hmx, hzx, mmx)
    for side, r in ((0, 1), (1, ROWS)):
        for f, ref in enumerate((h2, hu2, hv2)):
            ref[r] = ref[r] + faces[side][f]

    for side in (0, 1):
        rows = list(own_y[side]) + [mmy[side], hzy[side], hmy[side]] + halo_y[side]
        edge_out[side] = jnp.concatenate(rows + [jnp.zeros((7, ROWS), F32)], axis=0)

    pltpu.make_async_copy(msg.at[pl.ds(0, NGX - 1)], msg.at[pl.ds(0, NGX - 1)], p1_send).wait()
    pltpu.make_async_copy(mid_t.at[pl.ds(0, NGY - 1)], mid_t.at[pl.ds(0, NGY - 1)], p2_send).wait()


def finish(
    h2, hu2, hv2, edge, inflow, sewer_in,
    out_h, out_hu, out_hv, out_sewer,
    slabs, sewer,
    out_sem, sewer_sem,
):
    outs = ((h2, out_h), (hu2, out_hu), (hv2, out_hv))

    def store(f, j):
        src, dst = outs[f]
        if j in (0, 7):
            part = slabs.at[f, j // 7]
        else:
            part = src.at[pl.ds(1, ROWS), j, :]
        return pltpu.make_async_copy(part, dst.at[:, pl.ds(128 * j, 128)], out_sem.at[f])

    for f in range(3):
        for j in range(1, 7):
            store(f, j).start()

    def row(side, i):
        return edge[side, i : i + 1]

    own = [[row(s, i) for i in range(3)] for s in (0, 1)]
    halo = [[row(s, 6 + i) for i in range(3)] for s in (0, 1)]
    faces = faces_y(
        own, halo, [row(s, 5) for s in (0, 1)], [row(s, 4) for s in (0, 1)], [row(s, 3) for s in (0, 1)]
    )
    for f, (ref, _) in enumerate(outs):
        both = edge_slabs(ref, 1, edge_matrix(faces[0][f], faces[1][f]))
        for side in (0, 1):
            slabs[f, side] = both[side]

    share = inflow[...] / AREA
    head, face_k, above_k = sewer_in[0], sewer_in[1], sewer_in[2]
    sec_lane = lax.broadcasted_iota(I32, (16, 512), 1)
    for turn in range(SUBSTEPS):
        below = jnp.where(sec_lane == 511, 0.0, pltpu.roll(head, 511, 1))
        leaving = face_k * (head - below)
        entering = above_k * (pltpu.roll(head, 1, 1) - head)
        head = head + SEWER_DT * (entering - leaving + share)
    sewer[...] = head
    for f in range(3):
        for side in (0, 1):
            store(f, 7 * side).start()
    sewer_copy = pltpu.make_async_copy(sewer, out_sewer, sewer_sem)
    sewer_copy.start()
    for f, (src, _) in enumerate(outs):
        whole = src.at[pl.ds(1, ROWS)]
        pltpu.make_async_copy(whole, whole, out_sem.at[f]).wait()
    sewer_copy.wait()

def body(*args):
    args = [jnp.swapaxes(a, 1, 2) if a.ndim == 3 else a for a in args]
    rows, cols = args[0].shape
    grid = jax.ShapeDtypeStruct((rows, cols), F32)
    sewer = jax.ShapeDtypeStruct(args[9].shape, F32)
    args = [pltpu.with_memory_space_constraint(a, pltpu.HBM) for a in args]
    depth, mom_x, mom_y, bed, cells, strips, slots, sections, coefs, heads, conv = args
    hbm = pl.BlockSpec(memory_space=pltpu.HBM)
    vmem = pl.BlockSpec(memory_space=pltpu.VMEM)
    dma = pltpu.SemaphoreType.DMA
    padded = pltpu.VMEM((ROWS + 1, 8, 128), F32)
    h2, hu2, hv2, edge, inflow, sewer_in = pl.pallas_call(
        kernel,
        out_shape=(padded,) * 3
        + (pltpu.VMEM((2, 16, ROWS), F32), pltpu.VMEM((16, 512), F32), pltpu.VMEM((3, 16, 512), F32)),
        in_specs=[hbm] * 11,
        out_specs=(vmem,) * 6,
        scratch_shapes=[pltpu.VMEM((ROWS, 8, 128), F32)] * 4
        + [pltpu.VMEM((ROWS, 8, 128), I32), pltpu.VMEM((ROWS, 8, 128), F32)]
        + [pltpu.VMEM((ROWS + 1, 8, 128), F32)] * 9
        + [
            pltpu.VMEM((1, 16, 128), I32),
            pltpu.VMEM((16, 128), I32),
            pltpu.VMEM((16, 128), I32),
            pltpu.VMEM((16, 128), F32),
            pltpu.VMEM((16, 512), F32),
            pltpu.VMEM((16, 512), F32),
            pltpu.VMEM((ROWS, 2048), BF16),
            pltpu.VMEM((NGX, NGY, 128), F32),
            pltpu.VMEM((NGX, NGY, 128), F32),
            pltpu.VMEM((NGY, NGX, 128), F32),
            pltpu.VMEM((NGY, NGX, 128), F32),
            pltpu.VMEM((ROWS, 8, 128), F32),
            pltpu.VMEM((ROWS, 8, 128), F32),
            pltpu.VMEM((ROWS, 8, 128), F32),
            pltpu.VMEM((ROWS, 8, 128), F32),
            pltpu.VMEM((16, 128, 128), BF16),
            pltpu.VMEM((5, UNROLL, 8, 128), F32),
            pltpu.VMEM((2, 5, 8, 128), F32),
            pltpu.VMEM((2, 5, 8, 128), F32),
            pltpu.VMEM((2, 3, 8, 128), F32),
            pltpu.VMEM((2, 3, 8, 128), F32),
            pltpu.VMEM((2, 8, ROWS), F32),
            pltpu.VMEM((2, 8, ROWS), F32),
            pltpu.VMEM((2, 8, ROWS), F32),
            pltpu.VMEM((2, 8, ROWS), F32),
            dma((5, 2)),
            dma((6,)),
            dma,
            dma,
            dma,
            dma,
            dma((8,)),
            dma((8,)),
        ],
        compiler_params=pltpu.CompilerParams(
            collective_id=0, has_side_effects=True, vmem_limit_bytes=40 * 1024 * 1024
        ),
        name="street_flood",
    )(depth, mom_x, mom_y, bed, cells, strips, slots, sections, coefs, heads, conv)
    return pl.pallas_call(
        finish,
        out_shape=(grid, grid, grid, sewer),
        in_specs=[vmem] * 6,
        out_specs=(hbm,) * 4,
        scratch_shapes=[
            pltpu.VMEM((3, 2, ROWS, 128), F32),
            pltpu.VMEM((16, 512), F32),
            dma((3,)),
            dma,
        ],
        compiler_params=pltpu.CompilerParams(vmem_limit_bytes=16 * 1024 * 1024),
        name="flood_finish",
    )(h2, hu2, hv2, edge, inflow, sewer_in)


def solution(mesh):
    tiles = P("gx", "gy")
    lines = P(("gx", "gy"), None)
    return jax.shard_map(
        body,
        mesh=mesh,
        in_specs=(tiles,) * 5 + (P(("gx", "gy"), None, None),) + (lines,) * 5,
        out_specs=(tiles, tiles, tiles, lines),
        check_vma=False,
    )
```

```python
import math

import jax
import jax.numpy as jnp
from jax import lax
from jax.experimental import pallas as pl
from jax.experimental.pallas import tpu as pltpu
from jax.sharding import PartitionSpec as P

SUBSTEPS = 8
GRAVITY = 9.81
DT = 0.02
SEWER_DT = 0.5
AREA = 256.0
HALF_DT = 0.5 * DT
ROOT_G = math.sqrt(GRAVITY)
HALF_G = 0.5 * GRAVITY
SLOPE = 0.5 * GRAVITY * DT
NGX = 8
FAR_GY = (10, 9, 11, 6, 14, 8, 2, 5, 7, 13, 15, 1, 3, 4, 12)
FAR_GX = (4, 3, 5, 2, 6, 1, 7)
NGY = 16
ROWS = 256
UNROLL = 16
F32 = jnp.float32
BF16 = jnp.bfloat16
I32 = jnp.int32
NT = (((1,), (1,)), ((), ()))


def thirds(x):
    a = x.astype(BF16)
    rest = x - a.astype(F32)
    b = rest.astype(BF16)
    c = (rest - b.astype(F32)).astype(BF16)
    return a, b, c


def lanes_at(row, idx):
    return jnp.take_along_axis(row, idx, axis=1, mode="promise_in_bounds")


def prim(h, hu, hv, om):
    hs = h + om
    y = lax.rsqrt(hs)
    inv = y * y
    u = hu * inv
    v = hv * inv
    c = (ROOT_G * hs) * y
    p = HALF_G * h * h
    return dict(
        h=h,
        hu=hu,
        hv=hv,
        uu=hu * u + p,
        uv=hu * v,
        vv=hv * v + p,
        sx=jnp.abs(u) + c,
        sy=jnp.abs(v) + c,
    )


def face_x(wall, l, r):
    a = jnp.maximum(l["sx"], r["sx"])
    return (
        wall * ((l["hu"] + r["hu"]) - a * (r["h"] - l["h"])),
        wall * ((l["uu"] + r["uu"]) - a * (r["hu"] - l["hu"])),
        wall * ((l["uv"] + r["uv"]) - a * (r["hv"] - l["hv"])),
    )


def face_y(wall, l, r):
    a = jnp.maximum(l["sy"], r["sy"])
    return (
        wall * ((l["hv"] + r["hv"]) - a * (r["h"] - l["h"])),
        wall * ((l["uv"] + r["uv"]) - a * (r["hu"] - l["hu"])),
        wall * ((l["vv"] + r["vv"]) - a * (r["hv"] - l["hv"])),
    )


def faces_x(rows, halo, halo_m, halo_z, mine_m):
    out = []
    for side in (0, 1):
        mine = prim(*rows[side], 1.0 - mine_m[side])
        other = prim(*halo[side], 1.0 - halo_m[side])
        wall = (HALF_DT * halo_m[side]) * mine_m[side]
        slope = (SLOPE * mine_m[side]) * (halo_z[side] * mine["h"])
        if side == 0:
            f = face_x(wall, other, mine)
            out.append((f[0], f[1] + slope, f[2]))
        else:
            f = face_x(wall, mine, other)
            out.append((-f[0], -f[1] - slope, -f[2]))
    return out


def faces_y(cols, halo, halo_m, halo_z, mine_m):
    out = []
    for side in (0, 1):
        mine = prim(*cols[side], 1.0 - mine_m[side])
        other = prim(*halo[side], 1.0 - halo_m[side])
        wall = (HALF_DT * halo_m[side]) * mine_m[side]
        slope = (SLOPE * mine_m[side]) * (halo_z[side] * mine["h"])
        if side == 0:
            f = face_y(wall, other, mine)
            out.append((f[0], f[1], f[2] + slope))
        else:
            f = face_y(wall, mine, other)
            out.append((-f[0], -f[1], -f[2] - slope))
    return out


def slab_of(ref, first, j):
    return ref.reshape(ref.shape[0] * 8, 128), pl.ds(first * 8 + j, ROWS, stride=8)


def edge_matrix(left, right):
    sub = lax.broadcasted_iota(I32, (8, ROWS), 0)
    top = jnp.where(sub == 0, jnp.broadcast_to(left, (8, ROWS)), 0.0)
    bottom = jnp.where(sub == 7, jnp.broadcast_to(right, (8, ROWS)), 0.0)
    return jnp.concatenate([top, jnp.zeros((112, ROWS), F32), bottom], axis=0).T


def edge_slabs(ref, first, terms):
    lane = lax.broadcasted_iota(I32, (ROWS, 128), 1)
    flat, low = slab_of(ref, first, 0)
    _, high = slab_of(ref, first, 7)
    return (
        flat[low, :] + jnp.where(lane == 0, terms, 0.0),
        flat[high, :] + jnp.where(lane == 127, terms, 0.0),
    )


def edge_columns(low, high):
    lane = lax.broadcasted_iota(I32, (ROWS, 128), 1)
    both = jnp.where(lane < 64, low, high).T
    return both[0:1], both[127:128]


def kernel(
    depth, mom_x, mom_y, bed, cells, strips_in, slots_in, sections_in, coefs_in, heads_in, conv_in,
    h2, hu2, hv2, edge_out, inflow_out, sewer_in,
    h0, hu0, hv0, z0, m0, level, h1, hu1, hv1,
    om_s, omr_s, wx_s, wy_s, sx_s, sy_s,
    strips, slots, sections, coefs, heads, conv,
    onehot, msg, mid, mid_t, got, slot_coef, slot_pipe, hur, hvr, in_section, ring,
    row_snd1, row_rcv1, row_snd2, row_rcv2, col_snd1, col_rcv1, col_snd2, col_rcv2,
    in_sem, small_sem, p1_send, p1_recv, p2_send, p2_recv, halo_send, halo_recv,
):
    gx = lax.axis_index("gx")
    gy = lax.axis_index("gy")

    def gx_peer(i):
        return {"gx": lax.rem(gx + i, NGX)}

    def gy_peer(i):
        return {"gy": lax.rem(gy + i, NGY)}

    barrier = pltpu.get_barrier_semaphore()
    for i in FAR_GX:
        pl.semaphore_signal(barrier, inc=1, device_id=gx_peer(i), device_id_type=pl.DeviceIdType.MESH)
    for i in FAR_GY:
        pl.semaphore_signal(barrier, inc=1, device_id=gy_peer(i), device_id_type=pl.DeviceIdType.MESH)

    def start_halo(copy, side, at, last):
        @pl.when(at > 0 if side == 0 else at < last)
        def _():
            copy.start()

    def wait_halo(copy, side, at, last):
        @pl.when(at > 0 if side == 0 else at < last)
        def _():
            copy.wait_send()

        @pl.when(at < last if side == 0 else at > 0)
        def _():
            copy.wait_recv()

    pairs = ((depth, h0), (bed, z0), (cells, m0), (mom_x, hu0), (mom_y, hv0))

    def load(f, j, part=None):
        src, dst = pairs[f]
        rows = pl.ds(0, ROWS) if part is None else pl.ds(part * (ROWS // 2), ROWS // 2)
        return pltpu.make_async_copy(
            src.at[rows, pl.ds(128 * j, 128)], dst.at[rows, j, :], in_sem.at[f, part or 0]
        )

    def loaded(f, part=None):
        rows = pl.ds(0, ROWS) if part is None else pl.ds(part * (ROWS // 2), ROWS // 2)
        whole = pairs[f][1].at[rows]
        return pltpu.make_async_copy(whole, whole, in_sem.at[f, part or 0])

    small = ((slots_in, slots), (sections_in, sections), (coefs_in, coefs), (heads_in, heads), (strips_in, strips), (conv_in, conv))

    def load_small(i):
        return pltpu.make_async_copy(small[i][0], small[i][1], small_sem.at[i])

    for i in range(6):
        load_small(i).start()
    for part in (0, 1):
        for f in (0, 1):
            for j in range(8):
                load(f, j, part).start()
    for f in (2, 3, 4):
        for j in range(8):
            load(f, j).start()

    lane = lax.broadcasted_iota(I32, (8, 128), 1)
    sub = lax.broadcasted_iota(I32, (8, 128), 0)
    zero_row = jnp.zeros((8, 128), F32)

    for i in range(4):
        load_small(i).wait()
    slot = slots[...]
    sec = sections[...]
    coef = coefs[...]
    tile_of = slot >> 4
    k_of = slot & 15
    pipe = jnp.zeros((16, 128), F32)
    for b in range(4):
        part = lanes_at(heads[:, pl.ds(128 * b, 128)], sec & 127)
        pipe = jnp.where((sec >> 7) == b, part, pipe)
    tile_iota = lax.broadcasted_iota(I32, (128, 128), 0)
    k_iota = lax.broadcasted_iota(I32, (16, 128), 0)
    left = []
    right = []
    for l in range(16):
        left.append((jnp.broadcast_to(tile_of[l : l + 1], (128, 128)) == tile_iota).astype(F32).astype(BF16))
        hit = jnp.broadcast_to(k_of[l : l + 1], (16, 128)) == k_iota
        both = jnp.concatenate(
            [
                jnp.where(hit, jnp.broadcast_to(coef[l : l + 1], (16, 128)), 0.0),
                jnp.where(hit, jnp.broadcast_to(pipe[l : l + 1], (16, 128)), 0.0),
            ],
            axis=0,
        )
        right.append(jnp.concatenate(thirds(both), axis=0))
    by_slot = lax.dot_general(
        jnp.concatenate(right, axis=1), jnp.concatenate(left, axis=1), NT, preferred_element_type=F32
    )
    by_slot = by_slot[0:32] + by_slot[32:64] + by_slot[64:96]

    load_small(4).wait()
    strip = strips[0]
    strip_row = strip >> 3
    strip_j = strip & 7
    lane2 = lax.broadcasted_iota(I32, (8, 256), 1)

    def level_rows(t, sums):
        for i in range(32):
            r = t * 32 + i
            lev = h0[r] + z0[r]
            level[r] = lev
            sums = jnp.where(lane2 == r, jnp.sum(lev, axis=1, keepdims=True), sums)
        return sums

    sums = jnp.zeros((8, 256), F32)
    for part in (0, 1):
        for f in (0, 1):
            loaded(f, part).wait()
        sums = lax.fori_loop(4 * part, 4 * part + 4, level_rows, sums)
    by_strip = jnp.zeros((16, 128), F32)
    for half in range(2):
        for j in range(8):
            row = jnp.broadcast_to(sums[j : j + 1, 128 * half : 128 * half + 128], (16, 128))
            part = lanes_at(row, strip_row & 127)
            by_strip = jnp.where((strip_j == j) & ((strip_row >> 7) == half), part, by_strip)
    packed = jnp.concatenate([by_slot, by_strip, jnp.zeros((80, 128), F32)], axis=0).T
    msg[...] = packed.reshape(NGX, NGY, 128)

    pl.semaphore_wait(barrier, NGX + NGY - 2)

    def phase1(i):
        return pltpu.make_async_remote_copy(
            src_ref=msg.at[lax.rem(gx + i, NGX)],
            dst_ref=mid.at[gx],
            send_sem=p1_send,
            recv_sem=p1_recv,
            device_id=gx_peer(i),
            device_id_type=pl.DeviceIdType.MESH,
        )

    for i in FAR_GX:
        phase1(i).start()
    mid[gx] = msg[gx]

    loaded(2).wait()
    last_lane = lane == 127
    first_lane = lane == 0
    corner_r = (lane == 127) & (sub == 7)
    corner_l = (lane == 0) & (sub == 0)

    def from_right(x):
        a = pltpu.roll(x, 127, 1)
        return jnp.where(last_lane, pltpu.roll(a, 7, 0), a)

    def from_left(x):
        a = pltpu.roll(x, 1, 1)
        return jnp.where(first_lane, pltpu.roll(a, 1, 0), a)

    def static_rows(t, carry):
        for i in range(32):
            r = t * 32 + i
            m_prev, z_prev, z_prev2 = carry
            m = m0[r].astype(F32)
            z = z0[r]
            mr = from_right(m)
            om_s[r] = 1.0 - m
            omr_s[r] = 1.0 - mr
            wx_s[r] = (HALF_DT * m_prev) * m
            wy_s[r] = jnp.where(corner_r, 0.0, (HALF_DT * m) * mr)
            sx_s[r] = (SLOPE * m_prev) * (z - z_prev2)
            zr = jnp.where(corner_r, 0.0, from_right(z))
            zl = jnp.where(corner_l, 0.0, from_left(z))
            sy_s[r] = (SLOPE * m) * (zr - zl)
            carry = (m, z, z_prev)
        return carry

    m_end, _, z_end = lax.fori_loop(0, ROWS // 32, static_rows, (zero_row,) * 3)
    sx_s[ROWS] = (SLOPE * m_end) * (-z_end)

    for f in (3, 4):
        loaded(f).wait()

    def rows_of(r):
        return (h0[r], hu0[r], hv0[r], m0[r].astype(F32), z0[r])

    for side, r in ((0, 0), (1, ROWS - 1)):
        for f, value in enumerate(rows_of(r)):
            row_snd1[side, f] = value

    def halo_rows(snd, rcv, side, base):
        return pltpu.make_async_remote_copy(
            src_ref=snd.at[side],
            dst_ref=rcv.at[1 - side],
            send_sem=halo_send.at[base + side],
            recv_sem=halo_recv.at[base + side],
            device_id=gx_peer(NGX - 1 if side == 0 else 1),
            device_id_type=pl.DeviceIdType.MESH,
        )

    def halo_cols(snd, rcv, side, base):
        return pltpu.make_async_remote_copy(
            src_ref=snd.at[side],
            dst_ref=rcv.at[1 - side],
            send_sem=halo_send.at[base + 2 + side],
            recv_sem=halo_recv.at[base + 2 + side],
            device_id=gy_peer(NGY - 1 if side == 0 else 1),
            device_id_type=pl.DeviceIdType.MESH,
        )

    for side in (0, 1):
        start_halo(halo_rows(row_snd1, row_rcv1, side, 0), side, gx, NGX - 1)

    cols1 = ([], [])
    for ref in (h0, hu0, hv0, m0, z0):
        flat, low = slab_of(ref, 0, 0)
        _, high = slab_of(ref, 0, 7)
        ends = edge_columns(flat[low, :].astype(F32), flat[high, :].astype(F32))
        for side in (0, 1):
            cols1[side].append(ends[side])
    for side in (0, 1):
        col_snd1[side] = jnp.concatenate(cols1[side] + [jnp.zeros((3, ROWS), F32)], axis=0)
        start_halo(halo_cols(col_snd1, col_rcv1, side, 0), side, gy, NGY - 1)

    load_small(5).wait()
    cv = conv[...]
    sec_lane = lax.broadcasted_iota(I32, (16, 512), 1)
    face_k = jnp.where(sec_lane == 511, cv, 0.5 * (cv + pltpu.roll(cv, 511, 1)))
    sewer_in[0] = heads[...]
    sewer_in[1] = face_k
    sewer_in[2] = jnp.where(sec_lane == 0, 0.0, pltpu.roll(face_k, 1, 1))
    for l in range(16):
        hit = jnp.broadcast_to(sec[l : l + 1] & 127, (128, 128)) == tile_iota
        in_section[l] = hit.astype(F32).astype(BF16)

    row_iota = lax.broadcasted_iota(I32, (ROWS, 128), 0)
    for k in range(16):
        hit = jnp.broadcast_to(strip_row[k : k + 1], (ROWS, 128)) == row_iota
        onehot[:, pl.ds(128 * k, 128)] = hit.astype(F32).astype(BF16)

    NAMES = ("h", "hu", "hv", "uu", "uv", "sx")

    def phase2(i):
        return pltpu.make_async_remote_copy(
            src_ref=mid_t.at[lax.rem(gy + i, NGY)],
            dst_ref=got.at[gy],
            send_sem=p2_send,
            recv_sem=p2_recv,
            device_id=gy_peer(i),
            device_id_type=pl.DeviceIdType.MESH,
        )

    def forward():
        pltpu.make_async_copy(mid.at[pl.ds(0, NGX - 1)], mid.at[pl.ds(0, NGX - 1)], p1_recv).wait()
        mid_flat = mid.reshape(NGX * NGY, 128)
        for b in range(NGY):
            mid_t[b] = mid_flat[pl.ds(b, NGX, stride=NGY), :]
        for i in FAR_GY:
            phase2(i).start()
        got[gy] = mid_t[gy]

    def sweep(src, off, outs, rolled, pause, between):
        drained = rolled is not None
        def ahead(r, i):
            h = src[0][r + off]
            if drained:
                less = slot_coef[r] * (level[r] - slot_pipe[r])
                h = h - less
                ring[3, i] = less
                ring[4, i] = h
            ring[0, i] = from_right(h)
            if not drained:
                ring[1, i] = from_right(src[1][r + off])
                ring[2, i] = from_right(src[2][r + off])

        def one(r, i, carry):
            prev, part = carry
            h = ring[4, i] if drained else src[0][r + off]
            q = prim(h, src[1][r + off], src[2][r + off], om_s[r])
            if drained:
                right = prim(ring[0, i], rolled[0][r], rolled[1][r], omr_s[r])
            else:
                right = prim(ring[0, i], ring[1, i], ring[2, i], omr_s[r])
            fx = face_x(wx_s[r], prev, q)
            outs[0][r] = part[0] - fx[0]
            outs[1][r] = part[1] - fx[1] - prev["h"] * sx_s[r]
            outs[2][r] = part[2] - fx[2]
            dy = [f - from_left(f) for f in face_y(wy_s[r], q, right)]
            part_h = q["h"] - dy[0] + fx[0]
            if drained:
                part_h = part_h - ring[3, i]
            part = (part_h, q["hu"] - dy[1] + fx[1], q["hv"] - dy[2] - q["h"] * sy_s[r] + fx[2])
            return {name: q[name] for name in NAMES}, part

        turns = ROWS // UNROLL
        for i in range(UNROLL):
            ahead(i, i)

        def some(t, carry):
            following = jnp.minimum(t + 1, turns - 1) * UNROLL
            for i in range(UNROLL):
                carry = one(t * UNROLL + i, i, carry)
                ahead(following + i, i)
            return carry

        start = ({name: zero_row for name in NAMES}, (zero_row,) * 3)
        carry = lax.fori_loop(0, pause, some, start) if pause else start
        between()
        prev, part = lax.fori_loop(pause, turns, some, carry)
        outs[0][ROWS] = part[0]
        outs[1][ROWS] = part[1] - prev["h"] * sx_s[ROWS]
        outs[2][ROWS] = part[2]

    sweep((h0, hu0, hv0), 0, (h1, hu1, hv1), None, 10, forward)

    for side in (0, 1):
        wait_halo(halo_rows(row_snd1, row_rcv1, side, 0), side, gx, NGX - 1)
        wait_halo(halo_cols(col_snd1, col_rcv1, side, 0), side, gy, NGY - 1)
    exists_x = (gx > 0, gx < NGX - 1)
    exists_y = (gy > 0, gy < NGY - 1)

    def keep(yes, x):
        return jnp.where(yes, x, 0.0)

    halo_x = [[keep(exists_x[side], row_rcv1[side, f]) for f in range(5)] for side in (0, 1)]
    mine_x = [[row_snd1[side, f] for f in range(5)] for side in (0, 1)]
    halo_y = [[keep(exists_y[side], col_rcv1[side, f : f + 1]) for f in range(5)] for side in (0, 1)]
    mine_y = [[col_snd1[side, f : f + 1] for f in range(5)] for side in (0, 1)]
    hmx = [halo_x[s][3] for s in (0, 1)]
    hzx = [halo_x[s][4] for s in (0, 1)]
    mmx = [mine_x[s][3] for s in (0, 1)]
    hmy = [halo_y[s][3] for s in (0, 1)]
    hzy = [halo_y[s][4] for s in (0, 1)]
    mmy = [mine_y[s][3] for s in (0, 1)]
    faces = faces_x([mine_x[s][:3] for s in (0, 1)], [halo_x[s][:3] for s in (0, 1)], hmx, hzx, mmx)
    for side, r in ((0, 1), (1, ROWS)):
        for f, ref in enumerate((h1, hu1, hv1)):
            ref[r] = ref[r] + faces[side][f]
    faces = faces_y([mine_y[s][:3] for s in (0, 1)], [halo_y[s][:3] for s in (0, 1)], hmy, hzy, mmy)
    cols2 = []
    for f, ref in enumerate((h1, hu1, hv1)):
        low, high = edge_slabs(ref, 1, edge_matrix(faces[0][f], faces[1][f]))
        flat, rows = slab_of(ref, 1, 0)
        flat[rows, :] = low
        flat, rows = slab_of(ref, 1, 7)
        flat[rows, :] = high
        cols2.append(edge_columns(low, high))

    def rolled_rows(t, carry):
        for i in range(32):
            r = t * 32 + i
            hur[r] = from_right(hu1[r + 1])
            hvr[r] = from_right(hv1[r + 1])
        return carry

    lax.fori_loop(0, ROWS // 32, rolled_rows, 0)

    pltpu.make_async_copy(got.at[pl.ds(0, NGY - 1)], got.at[pl.ds(0, NGY - 1)], p2_recv).wait()
    got_flat = got.reshape(NGX * NGY, 128)
    arrived = jnp.concatenate([got_flat[pl.ds(a, NGY, stride=NGX), :] for a in range(NGX)], axis=0).T
    right = []
    j_iota = lax.broadcasted_iota(I32, (8, 128), 0)
    for k in range(16):
        hit = jnp.broadcast_to(strip_j[k : k + 1], (8, 128)) == j_iota
        both = jnp.concatenate(
            [
                jnp.where(hit, jnp.broadcast_to(arrived[k : k + 1], (8, 128)), 0.0),
                jnp.where(hit, jnp.broadcast_to(arrived[16 + k : 17 + k], (8, 128)), 0.0),
            ],
            axis=0,
        )
        right.append(jnp.concatenate(thirds(both), axis=0))
    by_row = lax.dot_general(jnp.concatenate(right, axis=1), onehot[...], NT, preferred_element_type=F32)
    by_row = by_row[0:16] + by_row[16:32] + by_row[32:48]
    by_row = jnp.concatenate([DT * by_row[0:8], by_row[8:16]], axis=0)

    def drain_of(r):
        lanes = by_row[:, 0:128] if r < 128 else by_row[:, 128:256]
        at = r % 128
        c = jnp.broadcast_to(lanes[0:8, at : at + 1], (8, 128))
        p = jnp.broadcast_to(lanes[8:16, at : at + 1], (8, 128))
        return c * (level[r] - p)

    own_x = []
    for side, r in ((0, 0), (1, ROWS - 1)):
        own_x.append((h1[r + 1] - drain_of(r), hu1[r + 1], hv1[r + 1]))
        for f in range(3):
            row_snd2[side, f] = own_x[side][f]
    own_y = []
    for side, j in ((0, 0), (1, 7)):
        lev = mine_y[side][0] + mine_y[side][4]
        less = by_row[j : j + 1] * (lev - by_row[8 + j : 9 + j])
        own_y.append((cols2[0][side] - less, cols2[1][side], cols2[2][side]))
        col_snd2[side] = jnp.concatenate(list(own_y[side]) + [jnp.zeros((5, ROWS), F32)], axis=0)
    for side in (0, 1):
        start_halo(halo_rows(row_snd2, row_rcv2, side, 4), side, gx, NGX - 1)
        start_halo(halo_cols(col_snd2, col_rcv2, side, 4), side, gy, NGY - 1)

    level_sum = jnp.zeros((16, 128), F32)
    for k in range(16):
        row = jnp.broadcast_to(arrived[32 + k : 33 + k], (16, 128))
        level_sum = jnp.where(k_of == k, lanes_at(row, tile_of & 127), level_sum)
    rate = jnp.where(slot >= 0, coef * (level_sum - 128.0 * pipe), 0.0)
    block = lax.broadcasted_iota(I32, (8, 128), 0)
    for l in range(16):
        s_row = sec[l : l + 1]
        value = jnp.where(
            jnp.broadcast_to(s_row >> 7, (8, 128)) == block, jnp.broadcast_to(rate[l : l + 1], (8, 128)), 0.0
        )
        got_l = lax.dot_general(jnp.concatenate(thirds(value), axis=0), in_section[l], NT, preferred_element_type=F32)
        got_l = got_l[0:8] + got_l[8:16] + got_l[16:24]
        for b in range(4):
            inflow_out[l : l + 1, pl.ds(128 * b, 128)] = got_l[b : b + 1]

    for ref, first in ((slot_coef, 0), (slot_pipe, 8)):
        for half in range(2):
            for j in range(8):
                value = by_row[first + j : first + j + 1, 128 * half : 128 * half + 128]
                flat = ref.reshape(ROWS * 8, 128)
                flat[pl.ds(1024 * half + j, 128, stride=8), :] = jnp.broadcast_to(value, (128, 128)).T
    sweep((h1, hu1, hv1), 1, (h2, hu2, hv2), (hur, hvr), 0, lambda: None)

    for side in (0, 1):
        wait_halo(halo_rows(row_snd2, row_rcv2, side, 4), side, gx, NGX - 1)
        wait_halo(halo_cols(col_snd2, col_rcv2, side, 4), side, gy, NGY - 1)
    halo_x = [[keep(exists_x[side], row_rcv2[side, f]) for f in range(3)] for side in (0, 1)]
    halo_y = [[keep(exists_y[side], col_rcv2[side, f : f + 1]) for f in range(3)] for side in (0, 1)]
    faces = faces_x(own_x, halo_x, hmx, hzx, mmx)
    for side, r in ((0, 1), (1, ROWS)):
        for f, ref in enumerate((h2, hu2, hv2)):
            ref[r] = ref[r] + faces[side][f]

    for side in (0, 1):
        rows = list(own_y[side]) + [mmy[side], hzy[side], hmy[side]] + halo_y[side]
        edge_out[side] = jnp.concatenate(rows + [jnp.zeros((7, ROWS), F32)], axis=0)

    pltpu.make_async_copy(msg.at[pl.ds(0, NGX - 1)], msg.at[pl.ds(0, NGX - 1)], p1_send).wait()
    pltpu.make_async_copy(mid_t.at[pl.ds(0, NGY - 1)], mid_t.at[pl.ds(0, NGY - 1)], p2_send).wait()


def finish(
    h2, hu2, hv2, edge, inflow, sewer_in,
    out_h, out_hu, out_hv, out_sewer,
    slabs, sewer,
    out_sem, sewer_sem,
):
    outs = ((h2, out_h), (hu2, out_hu), (hv2, out_hv))

    def store(f, j):
        src, dst = outs[f]
        if j in (0, 7):
            part = slabs.at[f, j // 7]
        else:
            part = src.at[pl.ds(1, ROWS), j, :]
        return pltpu.make_async_copy(part, dst.at[:, pl.ds(128 * j, 128)], out_sem.at[f])

    for f in range(3):
        for j in range(1, 7):
            store(f, j).start()

    def row(side, i):
        return edge[side, i : i + 1]

    own = [[row(s, i) for i in range(3)] for s in (0, 1)]
    halo = [[row(s, 6 + i) for i in range(3)] for s in (0, 1)]
    faces = faces_y(
        own, halo, [row(s, 5) for s in (0, 1)], [row(s, 4) for s in (0, 1)], [row(s, 3) for s in (0, 1)]
    )
    for f, (ref, _) in enumerate(outs):
        both = edge_slabs(ref, 1, edge_matrix(faces[0][f], faces[1][f]))
        for side in (0, 1):
            slabs[f, side] = both[side]

    share = inflow[...] / AREA
    head, face_k, above_k = sewer_in[0], sewer_in[1], sewer_in[2]
    sec_lane = lax.broadcasted_iota(I32, (16, 512), 1)
    for turn in range(SUBSTEPS):
        below = jnp.where(sec_lane == 511, 0.0, pltpu.roll(head, 511, 1))
        leaving = face_k * (head - below)
        entering = above_k * (pltpu.roll(head, 1, 1) - head)
        head = head + SEWER_DT * (entering - leaving + share)
    sewer[...] = head
    for f in range(3):
        for side in (0, 1):
            store(f, 7 * side).start()
    sewer_copy = pltpu.make_async_copy(sewer, out_sewer, sewer_sem)
    sewer_copy.start()
    for f, (src, _) in enumerate(outs):
        whole = src.at[pl.ds(1, ROWS)]
        pltpu.make_async_copy(whole, whole, out_sem.at[f]).wait()
    sewer_copy.wait()

def body(*args):
    args = [jnp.swapaxes(a, 1, 2) if a.ndim == 3 else a for a in args]
    rows, cols = args[0].shape
    grid = jax.ShapeDtypeStruct((rows, cols), F32)
    sewer = jax.ShapeDtypeStruct(args[9].shape, F32)
    args = [pltpu.with_memory_space_constraint(a, pltpu.HBM) for a in args]
    depth, mom_x, mom_y, bed, cells, strips, slots, sections, coefs, heads, conv = args
    hbm = pl.BlockSpec(memory_space=pltpu.HBM)
    vmem = pl.BlockSpec(memory_space=pltpu.VMEM)
    dma = pltpu.SemaphoreType.DMA
    padded = pltpu.VMEM((ROWS + 1, 8, 128), F32)
    h2, hu2, hv2, edge, inflow, sewer_in = pl.pallas_call(
        kernel,
        out_shape=(padded,) * 3
        + (pltpu.VMEM((2, 16, ROWS), F32), pltpu.VMEM((16, 512), F32), pltpu.VMEM((3, 16, 512), F32)),
        in_specs=[hbm] * 11,
        out_specs=(vmem,) * 6,
        scratch_shapes=[pltpu.VMEM((ROWS, 8, 128), F32)] * 4
        + [pltpu.VMEM((ROWS, 8, 128), I32), pltpu.VMEM((ROWS, 8, 128), F32)]
        + [pltpu.VMEM((ROWS + 1, 8, 128), F32)] * 9
        + [
            pltpu.VMEM((1, 16, 128), I32),
            pltpu.VMEM((16, 128), I32),
            pltpu.VMEM((16, 128), I32),
            pltpu.VMEM((16, 128), F32),
            pltpu.VMEM((16, 512), F32),
            pltpu.VMEM((16, 512), F32),
            pltpu.VMEM((ROWS, 2048), BF16),
            pltpu.VMEM((NGX, NGY, 128), F32),
            pltpu.VMEM((NGX, NGY, 128), F32),
            pltpu.VMEM((NGY, NGX, 128), F32),
            pltpu.VMEM((NGY, NGX, 128), F32),
            pltpu.VMEM((ROWS, 8, 128), F32),
            pltpu.VMEM((ROWS, 8, 128), F32),
            pltpu.VMEM((ROWS, 8, 128), F32),
            pltpu.VMEM((ROWS, 8, 128), F32),
            pltpu.VMEM((16, 128, 128), BF16),
            pltpu.VMEM((5, UNROLL, 8, 128), F32),
            pltpu.VMEM((2, 5, 8, 128), F32),
            pltpu.VMEM((2, 5, 8, 128), F32),
            pltpu.VMEM((2, 3, 8, 128), F32),
            pltpu.VMEM((2, 3, 8, 128), F32),
            pltpu.VMEM((2, 8, ROWS), F32),
            pltpu.VMEM((2, 8, ROWS), F32),
            pltpu.VMEM((2, 8, ROWS), F32),
            pltpu.VMEM((2, 8, ROWS), F32),
            dma((5, 2)),
            dma((6,)),
            dma,
            dma,
            dma,
            dma,
            dma((8,)),
            dma((8,)),
        ],
        compiler_params=pltpu.CompilerParams(
            collective_id=0, has_side_effects=True, vmem_limit_bytes=40 * 1024 * 1024
        ),
        name="street_flood",
    )(depth, mom_x, mom_y, bed, cells, strips, slots, sections, coefs, heads, conv)
    return pl.pallas_call(
        finish,
        out_shape=(grid, grid, grid, sewer),
        in_specs=[vmem] * 6,
        out_specs=(hbm,) * 4,
        scratch_shapes=[
            pltpu.VMEM((3, 2, ROWS, 128), F32),
            pltpu.VMEM((16, 512), F32),
            dma((3,)),
            dma,
        ],
        compiler_params=pltpu.CompilerParams(vmem_limit_bytes=16 * 1024 * 1024),
        name="flood_finish",
    )(h2, hu2, hv2, edge, inflow, sewer_in)


def solution(mesh):
    tiles = P("gx", "gy")
    lines = P(("gx", "gy"), None)
    return jax.shard_map(
        body,
        mesh=mesh,
        in_specs=(tiles,) * 5 + (P(("gx", "gy"), None, None),) + (lines,) * 5,
        out_specs=(tiles, tiles, tiles, lines),
        check_vma=False,
    )
```
